128 devices in a mesh: tm: 4 (over x_hi, core), tile: 32 (over z, y, x_lo).
Axes of the slice: x: 4 (x_hi: 2, x_lo: 2; x = x_hi * 2 + x_lo), y: 4, z: 4, core: 2. Of those that a mesh axis runs over, the one named last changes fastest.
Arguments:
- tokens: bfloat16 [32768, 5120], P(('tm', 'tile')), may hold values from -6 to 6
- head_shift: float32 [5120], replicated, may hold values from -3 to 3
- head_scale: float32 [5120], replicated, may hold values from -3 to 3
- head_weight: bfloat16 [5120, 64], replicated, may hold values from -0.078125 to 0.078125
- head_bias: float32 [64], replicated, may hold values from -3 to 3
- in_weight: bfloat16 [3, 3, 3, 16, 384], replicated, may hold values from -0.3125 to 0.3125
- in_bias: float32 [384], replicated, may hold values from -3 to 3
- gain_one: float32 [384], replicated, may hold values from 0.1 to 1.9
- weight_one: bfloat16 [3, 3, 3, 384, 384], replicated, may hold values from -0.0625 to 0.0625
- bias_one: float32 [384], replicated, may hold values from -3 to 3
- gain_two: float32 [384], replicated, may hold values from 0.1 to 1.9
- weight_two: bfloat16 [3, 3, 3, 384, 384], replicated, may hold values from -0.0625 to 0.0625
- bias_two: float32 [384], replicated, may hold values from -3 to 3
Outputs:
- result: bfloat16 [16, 32, 64, 4, 384], P('tm', 'tile')
The draws below stay inside these ranges and needn't reach their ends.
All inputs are finite; a program needn't handle non-finite values.
Results may differ from the reference program's by a relative error of at most 0.013.
Values may be sent and summed in bfloat16 or wider, within the bound.
A program may use at most 256 MiB of HBM per device.

```python
import jax
import jax.numpy as jnp
from jax import lax

D = 5120
LAT_C = 16
CHANNELS = 384
PATCH_OUT = 64
TH = 4
TW = 64
GY = 32
GX = 1
FRAMES = 16
WIDTH = 64
HEIGHT = 128
TOKENS = 32768


def steps_of(rng, shape, split, smallest, largest):
    factor_of = 1.0
    for position, blocks in split:
        steps = jax.random.uniform(jax.random.fold_in(jax.random.fold_in(rng, 6), position), (blocks,), jnp.float32, smallest / len(split), largest / len(split))
        factor_of = factor_of * jnp.repeat(jnp.exp(steps), shape[position] // blocks).reshape((-1,) + (1,) * (len(shape) - 1 - position))
    return factor_of


def gaussian(stream_key, dims, spread, reach, split=(), held_as=jnp.bfloat16):
    loudness = steps_of(stream_key, dims, split, -0.22, 0.18) if split else 1.0
    entries = jax.random.normal(stream_key, dims, jnp.float32) * spread * loudness
    return jnp.minimum(jnp.maximum(entries, -reach), reach).astype(held_as)


def setup_inputs(seed: int = 0) -> dict:
    splits = jax.random.split(jax.random.key(seed), 14)
    tokens = gaussian(splits[0], (TOKENS, D), 1.0, 6.0, ((0, 128),))
    head_shift = gaussian(splits[1], (D,), 0.5, 3.0, (), jnp.float32)
    head_scale = gaussian(splits[2], (D,), 0.5, 3.0, (), jnp.float32)
    head_weight = gaussian(splits[3], (D, PATCH_OUT), D ** -0.5, 0.078125)
    head_bias = gaussian(splits[4], (PATCH_OUT,), 0.5, 3.0, (), jnp.float32)
    in_weight = gaussian(splits[5], (3, 3, 3, LAT_C, CHANNELS), (27 * LAT_C) ** -0.5, 0.3125)
    in_bias = gaussian(splits[6], (CHANNELS,), 0.5, 3.0, (), jnp.float32)
    gain_one = jnp.clip(1.0 + 0.18 * jax.random.normal(splits[7], (CHANNELS,), jnp.float32), 0.1, 1.9)
    weight_one = gaussian(splits[8], (3, 3, 3, CHANNELS, CHANNELS), (27 * CHANNELS) ** -0.5, 0.0625)
    bias_one = gaussian(splits[9], (CHANNELS,), 0.5, 3.0, (), jnp.float32)
    gain_two = jnp.clip(1.0 + 0.18 * jax.random.normal(splits[10], (CHANNELS,), jnp.float32), 0.1, 1.9)
    weight_two = gaussian(splits[11], (3, 3, 3, CHANNELS, CHANNELS), (27 * CHANNELS) ** -0.5, 0.0625)
    bias_two = gaussian(splits[12], (CHANNELS,), 0.5, 3.0, (), jnp.float32)
    return dict(tokens=tokens, head_shift=head_shift, head_scale=head_scale, head_weight=head_weight, head_bias=head_bias, in_weight=in_weight, in_bias=in_bias, gain_one=gain_one, weight_one=weight_one, bias_one=bias_one, gain_two=gain_two, weight_two=weight_two, bias_two=bias_two)


def causal_conv(field_data, weight, shift_vec):
    frame_count, column_count, height, channel_count = field_data.shape
    padded = jnp.pad(field_data, ((2, 0), (1, 1), (1, 1), (0, 0)))

    def one_frame(frame_index):
        window_slab = lax.dynamic_slice_in_dim(padded, frame_index, 3, 0)
        running_sum = jnp.zeros((column_count * height, weight.shape[-1]), jnp.float32)
        for offset_t in range(3):
            for offset_w in range(3):
                sheet = window_slab[offset_t, offset_w:offset_w + column_count]
                stacked_taps = jnp.concatenate([sheet[:, offset_h:offset_h + height] for offset_h in range(3)], axis=-1)
                stacked_taps = stacked_taps.reshape(column_count * height, 3 * channel_count)
                running_sum = running_sum + jnp.dot(stacked_taps, weight[offset_t, offset_w].reshape(3 * channel_count, -1), preferred_element_type=jnp.float32)
        return running_sum.reshape(column_count, height, -1) + shift_vec
    return lax.map(one_frame, jnp.arange(frame_count, dtype=jnp.int32))

def normed_silu(field_data, gain_vec):
    values = field_data.astype(jnp.float32)
    scaled = values * lax.rsqrt(lax.optimization_barrier(jnp.mean(values * values, axis=-1, keepdims=True)) + 1e-06) * gain_vec
    return jax.nn.silu(scaled).astype(jnp.bfloat16)

def reference(tokens, head_shift, head_scale, head_weight, head_bias, in_weight, in_bias, gain_one, weight_one, bias_one, gain_two, weight_two, bias_two):
    per_frame = tokens.reshape(FRAMES, TOKENS // FRAMES, D)

    def frame_head(frame_tokens):
        token_values = frame_tokens.astype(jnp.float32)
        average = lax.optimization_barrier(jnp.mean(token_values, axis=-1, keepdims=True))
        centred = token_values - average
        variance = lax.optimization_barrier(jnp.mean(centred * centred, axis=-1, keepdims=True))
        modulated = (centred * lax.rsqrt(variance + 1e-06) * (1.0 + head_scale) + head_shift).astype(jnp.bfloat16)
        return (jnp.dot(modulated, head_weight, preferred_element_type=jnp.float32) + head_bias).astype(jnp.bfloat16)
    patches = lax.map(frame_head, per_frame)
    patches = patches.reshape(FRAMES, HEIGHT // 2, WIDTH // 2, 2, 2, LAT_C)
    latent = patches.transpose(0, 2, 4, 1, 3, 5).reshape(FRAMES, WIDTH, HEIGHT, LAT_C)
    stream = causal_conv(latent, in_weight, in_bias).astype(jnp.bfloat16)
    act_one = normed_silu(stream, gain_one)
    conv_one = causal_conv(act_one, weight_one, bias_one)
    act_two = normed_silu(conv_one, gain_two)
    conv_two = causal_conv(act_two, weight_two, bias_two)
    whole = (conv_two + stream.astype(jnp.float32)).astype(jnp.bfloat16)
    tiled = whole.reshape(FRAMES, GX, TW, GY, TH, CHANNELS).transpose(0, 3, 1, 2, 4, 5)
    return tiled.reshape(FRAMES, GY * GX, TW, TH, CHANNELS)
```

```python
import functools

import jax
import jax.numpy as jnp
from jax import lax
from jax.experimental import pallas as pl
from jax.experimental.pallas import tpu as pltpu
from jax.sharding import PartitionSpec as P

MESH = pl.DeviceIdType.MESH
TF = 4
TH = 4
KC = 32
EXT_F = TF + 2
EXT_R = TH + 2
ODD_BACK, EVEN, ODD, EVEN_ON = range(4)
ALL_ROWS = (0, 1, 2, 3)
ALL_TAPS = (0, 1, 2)

PIECES = {-1: (0, 1, 3), 0: (0, 3, 1), 1: (1, 4, 0), 2: (3, 4, 0), 3: (5, 3, 0), 4: (7, 1, 0)}


def body_kernel(
    tiles,
    blocks,
    tokens,
    shift_ref,
    scale_ref,
    head_w_ref,
    head_b_ref,
    in_w,
    in_b_ref,
    gain_one_ref,
    w_one,
    bias_one_ref,
    gain_two_ref,
    w_two,
    bias_two_ref,
    out_ref,
    tok,
    modulated,
    own,
    got,
    corner,
    w_in,
    w_corner,
    w1,
    w2,
    act_one,
    act_two,
    stream,
    acc,
    tok_sem,
    w_sem,
    in_sem,
    own_send,
    main_recv,
    side_recv,
    row_send,
    row_recv,
    tm_send,
    tm_recv,
    edge_send,
    edge_recv,
):
    me_m = lax.axis_index("tm")
    me_g = lax.axis_index("tile")
    chan = w1.shape[-1]
    depth = tok.shape[1]
    i32 = jnp.int32

    def at(m, g):
        return {"tm": m, "tile": g}

    def row_of(ref):
        return ref[...].reshape(1, ref.shape[0])

    tok_rows = tok.shape[0] // 4
    tok_copies = [
        pltpu.make_async_copy(
            tokens.at[pl.ds(i * tok_rows, tok_rows)],
            tok.at[pl.ds(i * tok_rows, tok_rows)],
            tok_sem.at[i],
        )
        for i in range(4)
    ]
    in_copy = pltpu.make_async_copy(in_w, w_in, in_sem)
    w_copies = [
        [
            pltpu.make_async_copy(src.at[pl.ds(9 * a, 9)], dst.at[pl.ds(9 * a, 9)], w_sem.at[n, a])
            for a in range(3)
        ]
        for n, (src, dst) in enumerate(((w_one, w1), (w_two, w2)))
    ]
    for copy in tok_copies:
        copy.start()
    in_copy.start()

    frame = lax.div(me_g, tiles // TF)
    part = lax.rem(me_g, tiles // TF)
    home = lax.div(me_g, 4)
    place = lax.rem(me_g, 4)

    def target(dm, d):
        g = 4 * part + d
        m = me_m + dm
        inside = (g >= 0) & (g < tiles) & (m < blocks)
        remote = inside if dm else inside & (g != me_g)
        return m, g, remote

    def source(slot, side):
        m = me_m if slot >= TF else me_m - 1
        other = home + jnp.where(place == 0, -1, 1) if side else home
        g = (slot % TF) * (tiles // TF) + other
        inside = m >= 0
        if side:
            inside = (
                inside
                & ((place == 0) | (place == 3))
                & (other >= 0)
                & (other < tiles // TF)
            )
        remote = inside & (g != me_g) if slot >= TF else inside
        return m, g, remote

    has_up = me_g > 0
    has_down = me_g < tiles - 1
    has_prev = me_m > 0
    has_next = me_m < blocks - 1
    sends_edges = has_next & (lax.rem(me_m, 2) == 1)
    passes_edges = has_next & (lax.rem(me_m, 2) == 0)
    gets_edges = has_prev & (lax.rem(me_m, 2) == 0)

    barrier = pltpu.get_barrier_semaphore()

    def greet(m, g, here):
        @pl.when(here)
        def _():
            pl.semaphore_signal(barrier, inc=1, device_id=at(m, g), device_id_type=MESH)

    for slot in range(2 * TF):
        for side in range(2):
            greet(*source(slot, side))
    greet(me_m, me_g - 1, has_up)
    greet(me_m, me_g + 1, has_down)
    greet(me_m - 1, me_g, has_prev)
    greet(me_m - 1, me_g - 1, gets_edges & has_up)
    greet(me_m - 1, me_g + 1, gets_edges & has_down)

    zero_patch = jnp.zeros((KC, got.shape[-1]), jnp.bfloat16)

    @pl.when(jnp.logical_not(has_prev))
    def _():
        for slot in range(TF):
            for pair in range(4):
                got[slot, pair] = zero_patch
        for version in range(4):
            for row in range(EXT_R):
                for f in range(2):
                    act_two[version, f, row] = jnp.zeros((KC, chan), jnp.bfloat16)

    @pl.when(jnp.logical_not(has_up))
    def _():
        for slot in range(2 * TF):
            got[slot, 0] = zero_patch
        for version in range(4):
            for f in range(EXT_F):
                act_two[version, f, 0] = jnp.zeros((KC, chan), jnp.bfloat16)

    @pl.when(jnp.logical_not(has_down))
    def _():
        for slot in range(2 * TF):
            got[slot, 3] = zero_patch
        for version in range(4):
            for f in range(EXT_F):
                act_two[version, f, EXT_R - 1] = jnp.zeros((KC, chan), jnp.bfloat16)

    lanes = 128

    def head_rows(i, carry):
        rows = pl.ds(pl.multiple_of(i * 16, 16), 16)

        def piece(j):
            return tok[rows, j * lanes : (j + 1) * lanes].astype(jnp.float32)

        def over_lanes(term):
            parts = [jnp.zeros((16, lanes), jnp.float32)] * 2
            for j in range(depth // lanes):
                parts[j % 2] = parts[j % 2] + term(j)
            return jnp.sum(parts[0] + parts[1], axis=-1, keepdims=True) * (1.0 / depth)

        average = over_lanes(piece)

        def squared(j):
            centred = piece(j) - average
            return centred * centred

        factor = lax.rsqrt(over_lanes(squared) + 1e-06)
        for j in range(depth // lanes):
            part = pl.ds(j * lanes, lanes)
            normed = (piece(j) - average) * factor * (1.0 + scale_ref[:, part]) + shift_ref[:, part]
            modulated[rows, part] = normed.astype(jnp.bfloat16)
        return carry

    for i in range(4):
        tok_copies[i].wait()
        if i == 3:
            for copy in w_copies[0]:
                copy.start()
        blocks_of = tok_rows // 16
        lax.fori_loop(i * blocks_of, (i + 1) * blocks_of, head_rows, 0, unroll=min(4, blocks_of))
    head_w = head_w_ref[...]
    patches = lax.dot_general(
        modulated[...],
        jnp.concatenate([head_w, head_w], axis=0),
        (((1,), (1,)), ((), ())),
        preferred_element_type=jnp.float32,
    )
    head_b = jnp.concatenate([row_of(head_b_ref)] * 2, axis=1)
    own[...] = (patches + head_b).astype(jnp.bfloat16).reshape(own.shape)

    def patch_copy(n, dm, d):
        m, g, remote = target(dm, d)
        first, count, slot = PIECES[d]
        return remote, pltpu.make_async_remote_copy(
            src_ref=own.at[pl.ds(first, count)],
            dst_ref=got.at[(0 if dm else TF) + frame, pl.ds(slot, count)],
            send_sem=own_send.at[n],
            recv_sem=(side_recv if d in (-1, 4) else main_recv).at[(0 if dm else TF) + frame],
            device_id=at(m, g),
            device_id_type=MESH,
        )

    sends = [(dm, d) for dm in (1, 0) for d in PIECES]
    count = i32(0)
    for dm, d in sends:
        count = count + target(dm, d)[2].astype(i32)
    for here in (has_up, has_down, has_next, sends_edges & has_up, sends_edges & has_down):
        count = count + here.astype(i32)
    pl.semaphore_wait(barrier, count)

    for n, (dm, d) in enumerate(sends):
        remote, copy = patch_copy(n, dm, d)

        @pl.when(remote)
        def _(copy=copy):
            copy.start()

    for d, (first, size, slot) in PIECES.items():

        @pl.when(4 * part + d == me_g)
        def _(first=first, size=size, slot=slot):
            got[TF + frame, pl.ds(slot, size)] = own[pl.ds(first, size)]

    in_copy.wait()
    w_corner[...] = jnp.zeros(w_corner.shape, jnp.bfloat16)
    for a in range(3):
        for parity, middle in ((0, 2), (1, 1)):
            for cell in range(2):
                for s in range(3):
                    for u in range(3):
                        row = s + cell
                        col = u + middle - 1
                        at_k = (row // 2) * 128 + (col // 2) * 64 + (row % 2) * 32 + (col % 2) * 16
                        at_n = (2 * parity + cell) * chan
                        w_corner[a, pl.ds(at_k, 16), pl.ds(at_n, chan)] = w_in[
                            pl.ds(((a * 3 + u) * 3 + s) * 16, 16), :
                        ]

    for slot in range(2 * TF):
        for side in range(2):
            m, g, remote = source(slot, side)
            for d, (first, size, first_slot) in PIECES.items():
                if (d in (-1, 4)) != bool(side):
                    continue
                which = place == d % 4

                @pl.when(remote & which)
                def _(slot=slot, m=m, g=g, first=first, size=size, first_slot=first_slot, side=side):
                    pltpu.make_async_remote_copy(
                        src_ref=own.at[pl.ds(first, size)],
                        dst_ref=got.at[slot, pl.ds(first_slot, size)],
                        send_sem=own_send.at[0],
                        recv_sem=(side_recv if side else main_recv).at[slot],
                        device_id=at(m, g),
                        device_id_type=MESH,
                    ).wait_recv()

    width = got.shape[-1]
    flat = got[...].astype(jnp.float32).reshape(2 * TF * 4 * KC, width)
    lane = lax.broadcasted_iota(i32, flat.shape, 1)
    pair_col = lax.rem(lax.broadcasted_iota(i32, flat.shape, 0), KC)
    back = jnp.where(pair_col == 0, 0.0, pltpu.roll(flat, 1, 0))
    on = jnp.where(pair_col == KC - 1, 0.0, pltpu.roll(flat, flat.shape[0] - 1, 0))
    left = lane < width // 2
    corner[0] = jnp.where(left, back, flat).astype(jnp.bfloat16).reshape(corner.shape[1:])
    corner[1] = jnp.where(left, flat, on).astype(jnp.bfloat16).reshape(corner.shape[1:])

    col_index = lax.broadcasted_iota(i32, (KC, 1), 0)

    def normed_silu(values, gain, keep=None):
        mean = jnp.sum(values * values, axis=-1, keepdims=True) * (1.0 / chan)
        half = values * lax.rsqrt(mean + 1e-06) * gain
        act = half + half * jnp.tanh(half)
        return act if keep is None else act * keep

    def store_act(ref, f, row, parity, act):
        if parity == 0:
            ref[EVEN, f, row] = act.astype(jnp.bfloat16)
            moved = jnp.where(col_index == KC - 1, 0.0, pltpu.roll(act, KC - 1, 0))
            ref[EVEN_ON, f, row] = moved.astype(jnp.bfloat16)
        else:
            ref[ODD, f, row] = act.astype(jnp.bfloat16)
            moved = jnp.where(col_index == 0, 0.0, pltpu.roll(act, 1, 0))
            ref[ODD_BACK, f, row] = moved.astype(jnp.bfloat16)

    gain_one = row_of(gain_one_ref) * 0.5
    in_bias = jnp.concatenate([row_of(in_b_ref)] * 2, axis=1)
    top_keep = has_up.astype(jnp.float32)
    bottom_keep = has_down.astype(jnp.float32)

    def input_frames(pair, carry):
        first = 2 * pair
        frame_keep = ((pair > 0) | has_prev).astype(jnp.float32)
        for parity in range(2):
            taps = []
            for a in range(3):
                for di in range(2):
                    taps.append(
                        corner[parity, pl.ds(first + a, 2), di : di + 3].reshape(2 * 3 * KC, width)
                    )
            raw = jnp.dot(
                jnp.concatenate(taps, axis=1),
                w_corner[:, :, 2 * chan * parity : 2 * chan * (parity + 1)].reshape(
                    6 * width, 2 * chan
                ),
                preferred_element_type=jnp.float32,
            )
            raw = (raw + in_bias).reshape(2, 3, KC, 2 * chan)
            for f in range(2):
                for ci in range(3):
                    for cell in range(2):
                        row = 2 * ci + cell
                        cells = raw[f, ci, :, cell * chan : (cell + 1) * chan].astype(jnp.bfloat16)
                        stream[parity, first + f, row] = cells
                        keep = frame_keep
                        if row == 0:
                            keep = keep * top_keep
                        if row == EXT_R - 1:
                            keep = keep * bottom_keep
                        act = normed_silu(cells.astype(jnp.float32), gain_one, keep)
                        store_act(act_one, first + f, row, parity, act)
        return carry

    lax.fori_loop(0, 3, input_frames, 0)

    def tap(weight, a, u, s):
        return weight[a * 9 + u * 3 + s]

    def cells(field, version, frames, rows, s):
        if rows == ALL_ROWS:
            view = [field[version, f, s : s + TH] for f in frames]
        else:
            view = [field[version, f, v + s][None] for f in frames for v in rows]
        return jnp.concatenate(view, axis=0).reshape(len(frames) * len(rows) * KC, chan)

    def add_pairs(field, weight, a, first, count, rows, taps):
        total = jnp.dot(
            jnp.concatenate(
                [
                    cells(field, v, [first + a + n for n in range(count)], rows, s)
                    for s in taps
                    for v in (EVEN, ODD)
                ],
                axis=1,
            ),
            jnp.concatenate(
                [
                    jnp.concatenate([tap(weight, a, u + 1, s), tap(weight, a, u, s)], axis=1)
                    for s in taps
                    for u in (0, 1)
                ],
                axis=0,
            ),
            preferred_element_type=jnp.float32,
        ).reshape(count, len(rows), KC, 2 * chan)
        for n in range(count):
            if rows == ALL_ROWS:
                acc[first + n] += total[n]
            else:
                for i, v in enumerate(rows):
                    acc[first + n, v] += total[n, i]

    def add_sides(field, weight, rows, taps, groups, outs):
        for version, u, parity in ((ODD_BACK, 0, 0), (EVEN_ON, 2, 1)):
            total = jnp.dot(
                jnp.concatenate(
                    [cells(field, version, frames, rows, s) for frames, _ in groups for s in taps],
                    axis=1,
                ),
                jnp.concatenate(
                    [
                        jnp.concatenate([tap(weight, a, u, s) for a in times], axis=1)
                        for _, times in groups
                        for s in taps
                    ],
                    axis=0,
                ),
                preferred_element_type=jnp.float32,
            ).reshape(len(outs[0]), len(rows), KC, len(outs) * chan)
            part = pl.ds(parity * chan, chan)
            for k, frames in enumerate(outs):
                for n, f in enumerate(frames):
                    added = total[n, :, :, k * chan : (k + 1) * chan]
                    if rows == ALL_ROWS:
                        acc[f, :, :, part] += added
                    else:
                        for i, v in enumerate(rows):
                            acc[f, v, :, part] += added[i]

    def start_acc(bias_ref):
        bias = jnp.concatenate([row_of(bias_ref)] * 2, axis=1)
        acc[...] = jnp.broadcast_to(bias.reshape(1, 1, 1, 2 * chan), acc.shape)

    gain_two = row_of(gain_two_ref) * 0.5

    def conv_one_rows(rows):
        def one_time(a, carry):
            add_pairs(act_one, w1, a, 0, TF, rows, ALL_TAPS)
            return carry

        lax.fori_loop(0, 3, one_time, 0)
        add_sides(
            act_one, w1, rows, ALL_TAPS, [((1, 3), (1, 0)), ((2, 4), (2, 1))], [(0, 2), (1, 3)]
        )
        add_sides(act_one, w1, rows, ALL_TAPS, [((0, 2), (0,))], [(0, 2)])
        add_sides(act_one, w1, rows, ALL_TAPS, [((3, 5), (2,))], [(1, 3)])

        def finish(f, carry):
            for v in rows:
                for parity in range(2):
                    values = acc[f, v, :, parity * chan : (parity + 1) * chan]
                    store_act(act_two, f + 2, v + 1, parity, normed_silu(values, gain_two))
            return carry

        lax.fori_loop(0, TF, finish, 0, unroll=2)

    def row_copy(way):
        frames = pl.ds(2, TF)
        return pltpu.make_async_remote_copy(
            src_ref=act_two.at[pl.ds(EVEN, 2), frames, 1 if way else TH],
            dst_ref=act_two.at[pl.ds(EVEN, 2), frames, EXT_R - 1 if way else 0],
            send_sem=row_send.at[way],
            recv_sem=row_recv.at[way],
            device_id=at(me_m, me_g - 1 if way else me_g + 1),
            device_id_type=MESH,
        )

    def edge_copy(way):
        return pltpu.make_async_remote_copy(
            src_ref=act_two.at[pl.ds(EVEN, 2), pl.ds(TF, 2), 1 if way else TH],
            dst_ref=act_two.at[pl.ds(EVEN, 2), pl.ds(0, 2), EXT_R - 1 if way else 0],
            send_sem=edge_send.at[way],
            recv_sem=edge_recv.at[way],
            device_id=at(me_m + 1, me_g - 1 if way else me_g + 1),
            device_id_type=MESH,
        )

    def pass_copy(way):
        row = EXT_R - 1 if way else 0
        return pltpu.make_async_remote_copy(
            src_ref=act_two.at[pl.ds(EVEN, 2), pl.ds(TF, 2), row],
            dst_ref=act_two.at[pl.ds(EVEN, 2), pl.ds(0, 2), row],
            send_sem=edge_send.at[way],
            recv_sem=edge_recv.at[way],
            device_id=at(me_m + 1, me_g),
            device_id_type=MESH,
        )

    tm_copy = pltpu.make_async_remote_copy(
        src_ref=act_two.at[pl.ds(EVEN, 2), pl.ds(TF, 2), pl.ds(1, TH)],
        dst_ref=act_two.at[pl.ds(EVEN, 2), pl.ds(0, 2), pl.ds(1, TH)],
        send_sem=tm_send.at[0],
        recv_sem=tm_recv.at[0],
        device_id=at(me_m + 1, me_g),
        device_id_type=MESH,
    )
    way_out = (has_down, has_up)
    way_in = (has_up, has_down)

    def widen(f, row):
        even = act_two[EVEN, f, row].astype(jnp.float32)
        moved = jnp.where(col_index == KC - 1, 0.0, pltpu.roll(even, KC - 1, 0))
        act_two[EVEN_ON, f, row] = moved.astype(jnp.bfloat16)
        odd = act_two[ODD, f, row].astype(jnp.float32)
        moved = jnp.where(col_index == 0, 0.0, pltpu.roll(odd, 1, 0))
        act_two[ODD_BACK, f, row] = moved.astype(jnp.bfloat16)

    start_acc(bias_one_ref)
    for copy in w_copies[0]:
        copy.wait()
    for copy in w_copies[1]:
        copy.start()

    conv_one_rows((0, TH - 1))
    for way in range(2):

        @pl.when(way_out[way])
        def _(way=way):
            row_copy(way).start()

        @pl.when(way_out[way] & sends_edges)
        def _(way=way):
            edge_copy(way).start()

    conv_one_rows((1, 2))

    @pl.when(has_next)
    def _():
        tm_copy.start()

    start_acc(bias_two_ref)
    for copy in w_copies[1]:
        copy.wait()

    def conv_two_own(taps):
        for a in range(3):
            add_pairs(act_two, w2, a, 2 - a, TF - 2 + a, ALL_ROWS, taps)
        add_sides(act_two, w2, ALL_ROWS, taps, [((3,), (1, 0)), ((4,), (2, 1))], [(2,), (3,)])
        add_sides(act_two, w2, ALL_ROWS, taps, [((2,), (2, 1))], [(0,), (1,)])
        add_sides(act_two, w2, ALL_ROWS, taps, [((2,), (0,))], [(2,)])
        add_sides(act_two, w2, ALL_ROWS, taps, [((3, 5), (2,))], [(1, 3)])

    conv_two_own((1,))

    for way in range(2):

        @pl.when(way_in[way])
        def _(way=way):
            row_copy(way).wait_recv()

        @pl.when(way_in[way] & passes_edges)
        def _(way=way):
            pass_copy(way).start()

        @pl.when(way_in[way])
        def _(way=way):
            for f in range(TF):
                widen(2 + f, EXT_R - 1 if way else 0)

    conv_two_own((0, 2))

    @pl.when(has_prev)
    def _():
        tm_copy.wait_recv()

    for way in range(2):

        @pl.when(way_in[way] & has_prev)
        def _(way=way):
            edge_copy(way).wait_recv()

    @pl.when(has_prev)
    def _():
        for f in range(2):

            def widen_row(row, carry, f=f):
                widen(f, row)
                return carry

            lax.fori_loop(0, EXT_R, widen_row, 0, unroll=True)

    add_pairs(act_two, w2, 0, 0, 2, ALL_ROWS, ALL_TAPS)
    add_pairs(act_two, w2, 1, 0, 1, ALL_ROWS, ALL_TAPS)
    add_sides(act_two, w2, ALL_ROWS, ALL_TAPS, [((1,), (1, 0))], [(0,), (1,)])
    add_sides(act_two, w2, ALL_ROWS, ALL_TAPS, [((0,), (0,))], [(0,)])

    area = 2 * TH * KC
    to = lax.broadcasted_iota(i32, (area, area), 0)
    of = lax.broadcasted_iota(i32, (area, area), 1)
    order = jnp.where(
        (lax.div(to, 8) == lax.rem(of, KC)) & (lax.rem(to, 8) == lax.div(of, KC)), 1.0, 0.0
    ).astype(jnp.bfloat16)

    def finish_two(f, carry):
        halves = []
        for parity in range(2):
            whole = acc[f, :, :, parity * chan : (parity + 1) * chan] + stream[
                parity, f + 2, 1 : TH + 1
            ].astype(jnp.float32)
            halves.append(whole.astype(jnp.bfloat16).reshape(TH * KC, chan))
        placed = jnp.dot(
            order, jnp.concatenate(halves, axis=0), preferred_element_type=jnp.float32
        )
        out_ref[f, 0] = placed.reshape(2 * KC, TH, chan).astype(jnp.bfloat16)
        return carry

    lax.fori_loop(0, TF, finish_two, 0)

    for n, (dm, d) in enumerate(sends):
        remote, copy = patch_copy(n, dm, d)

        @pl.when(remote)
        def _(copy=copy):
            copy.wait_send()

    @pl.when(has_next)
    def _():
        tm_copy.wait_send()

    for way in range(2):

        @pl.when(way_out[way])
        def _(way=way):
            row_copy(way).wait_send()

        @pl.when(way_out[way] & sends_edges)
        def _(way=way):
            edge_copy(way).wait_send()

        @pl.when(way_in[way] & passes_edges)
        def _(way=way):
            pass_copy(way).wait_send()


def solution(mesh):
    tiles = mesh.shape["tile"]
    blocks = mesh.shape["tm"]

    def body(
        tokens,
        head_shift,
        head_scale,
        head_weight,
        head_bias,
        in_weight,
        in_bias,
        gain_one,
        weight_one,
        bias_one,
        gain_two,
        weight_two,
        bias_two,
    ):
        count, depth = tokens.shape
        chan = weight_one.shape[-1]
        wide = 2 * head_weight.shape[1]
        in_rows = in_weight.shape[0] * in_weight.shape[1] * in_weight.shape[2] * in_weight.shape[3]
        bf16 = jnp.bfloat16
        hbm = pl.BlockSpec(memory_space=pl.ANY)
        vmem = pl.BlockSpec(memory_space=pltpu.VMEM)
        dma = pltpu.SemaphoreType.DMA
        result = pl.pallas_call(
            functools.partial(body_kernel, tiles, blocks),
            out_shape=jax.ShapeDtypeStruct((TF, 1, 2 * KC, TH, chan), bf16),
            in_specs=[
                hbm, vmem, vmem, vmem, vmem, hbm, vmem, vmem, hbm, vmem, vmem, hbm, vmem,
            ],
            out_specs=vmem,
            scratch_shapes=[
                pltpu.VMEM((count, depth), bf16),
                pltpu.VMEM((count, depth), bf16),
                pltpu.VMEM((count // KC, KC, wide), bf16),
                pltpu.VMEM((2 * TF, 4, KC, wide), bf16),
                pltpu.VMEM((2, 2 * TF, 4, KC, wide), bf16),
                pltpu.VMEM((in_rows, chan), bf16),
                pltpu.VMEM((3, 2 * wide, 4 * chan), bf16),
                pltpu.VMEM((27, chan, chan), bf16),
                pltpu.VMEM((27, chan, chan), bf16),
                pltpu.VMEM((4, EXT_F, EXT_R, KC, chan), bf16),
                pltpu.VMEM((4, EXT_F, EXT_R, KC, chan), bf16),
                pltpu.VMEM((2, EXT_F, EXT_R, KC, chan), bf16),
                pltpu.VMEM((TF, TH, KC, 2 * chan), jnp.float32),
                dma((4,)),
                dma((2, 3)),
                dma,
                dma((12,)),
                dma((2 * TF,)),
                dma((2 * TF,)),
                dma((2,)),
                dma((2,)),
                dma((1,)),
                dma((1,)),
                dma((2,)),
                dma((2,)),
            ],
            compiler_params=pltpu.CompilerParams(
                collective_id=0, has_side_effects=True, vmem_limit_bytes=60 * 1024 * 1024
            ),
            name="decode",
        )(
            tokens,
            head_shift[None],
            head_scale[None],
            head_weight.T,
            head_bias,
            in_weight.reshape(in_rows, chan),
            in_bias,
            gain_one,
            weight_one.reshape(27, chan, chan),
            bias_one,
            gain_two,
            weight_two.reshape(27, chan, chan),
            bias_two,
        )
        return result

    in_specs = (P(("tm", "tile"), None), P(), P(), P(), P(), P(), P(), P(), P(), P(), P(), P(), P())
    out_specs = P("tm", "tile", None, None, None)
    return jax.shard_map(body, mesh=mesh, in_specs=in_specs, out_specs=out_specs, check_vma=False)
```

```python
import functools

import jax
import jax.numpy as jnp
from jax import lax
from jax.experimental import pallas as pl
from jax.experimental.pallas import tpu as pltpu
from jax.sharding import PartitionSpec as P

MESH = pl.DeviceIdType.MESH
TF = 4
TH = 4
KC = 32
EXT_F = TF + 2
EXT_R = TH + 2
ODD_BACK, EVEN, ODD, EVEN_ON = range(4)
ALL_ROWS = (0, 1, 2, 3)
ALL_TAPS = (0, 1, 2)

PIECES = {-1: (0, 1, 3), 0: (0, 3, 1), 1: (1, 4, 0), 2: (3, 4, 0), 3: (5, 3, 0), 4: (7, 1, 0)}


def body_kernel(
    tiles,
    blocks,
    tokens,
    shift_ref,
    scale_ref,
    head_w_ref,
    head_b_ref,
    in_w,
    in_b_ref,
    gain_one_ref,
    w_one,
    bias_one_ref,
    gain_two_ref,
    w_two,
    bias_two_ref,
    out_ref,
    tok,
    modulated,
    own,
    got,
    corner,
    w_in,
    w_corner,
    w1,
    w2,
    act_one,
    act_two,
    stream,
    acc,
    tok_sem,
    w_sem,
    in_sem,
    own_send,
    main_recv,
    side_recv,
    row_send,
    row_recv,
    tm_send,
    tm_recv,
    edge_send,
    edge_recv,
):
    me_m = lax.axis_index("tm")
    me_g = lax.axis_index("tile")
    chan = w1.shape[-1]
    depth = tok.shape[1]
    i32 = jnp.int32

    def at(m, g):
        return {"tm": m, "tile": g}

    def row_of(ref):
        return ref[...].reshape(1, ref.shape[0])

    tok_rows = tok.shape[0] // 4
    tok_copies = [
        pltpu.make_async_copy(
            tokens.at[pl.ds(i * tok_rows, tok_rows)],
            tok.at[pl.ds(i * tok_rows, tok_rows)],
            tok_sem.at[i],
        )
        for i in range(4)
    ]
    in_copy = pltpu.make_async_copy(in_w, w_in, in_sem)
    w_copies = [
        [
            pltpu.make_async_copy(src.at[pl.ds(9 * a, 9)], dst.at[pl.ds(9 * a, 9)], w_sem.at[n, a])
            for a in range(3)
        ]
        for n, (src, dst) in enumerate(((w_one, w1), (w_two, w2)))
    ]
    for copy in tok_copies:
        copy.start()
    in_copy.start()

    frame = lax.div(me_g, tiles // TF)
    part = lax.rem(me_g, tiles // TF)
    home = lax.div(me_g, 4)
    place = lax.rem(me_g, 4)

    def target(dm, d):
        g = 4 * part + d
        m = me_m + dm
        inside = (g >= 0) & (g < tiles) & (m < blocks)
        remote = inside if dm else inside & (g != me_g)
        return m, g, remote

    def source(slot, side):
        m = me_m if slot >= TF else me_m - 1
        other = home + jnp.where(place == 0, -1, 1) if side else home
        g = (slot % TF) * (tiles // TF) + other
        inside = m >= 0
        if side:
            inside = (
                inside
                & ((place == 0) | (place == 3))
                & (other >= 0)
                & (other < tiles // TF)
            )
        remote = inside & (g != me_g) if slot >= TF else inside
        return m, g, remote

    has_up = me_g > 0
    has_down = me_g < tiles - 1
    has_prev = me_m > 0
    has_next = me_m < blocks - 1
    sends_edges = has_next & (lax.rem(me_m, 2) == 1)
    passes_edges = has_next & (lax.rem(me_m, 2) == 0)
    gets_edges = has_prev & (lax.rem(me_m, 2) == 0)

    barrier = pltpu.get_barrier_semaphore()

    def greet(m, g, here):
        @pl.when(here)
        def _():
            pl.semaphore_signal(barrier, inc=1, device_id=at(m, g), device_id_type=MESH)

    for slot in range(2 * TF):
        for side in range(2):
            greet(*source(slot, side))
    greet(me_m, me_g - 1, has_up)
    greet(me_m, me_g + 1, has_down)
    greet(me_m - 1, me_g, has_prev)
    greet(me_m - 1, me_g - 1, gets_edges & has_up)
    greet(me_m - 1, me_g + 1, gets_edges & has_down)

    zero_patch = jnp.zeros((KC, got.shape[-1]), jnp.bfloat16)

    @pl.when(jnp.logical_not(has_prev))
    def _():
        for slot in range(TF):
            for pair in range(4):
                got[slot, pair] = zero_patch
        for version in range(4):
            for row in range(EXT_R):
                for f in range(2):
                    act_two[version, f, row] = jnp.zeros((KC, chan), jnp.bfloat16)

    @pl.when(jnp.logical_not(has_up))
    def _():
        for slot in range(2 * TF):
            got[slot, 0] = zero_patch
        for version in range(4):
            for f in range(EXT_F):
                act_two[version, f, 0] = jnp.zeros((KC, chan), jnp.bfloat16)

    @pl.when(jnp.logical_not(has_down))
    def _():
        for slot in range(2 * TF):
            got[slot, 3] = zero_patch
        for version in range(4):
            for f in range(EXT_F):
                act_two[version, f, EXT_R - 1] = jnp.zeros((KC, chan), jnp.bfloat16)

    lanes = 128

    def head_rows(i, carry):
        rows = pl.ds(pl.multiple_of(i * 16, 16), 16)

        def piece(j):
            return tok[rows, j * lanes : (j + 1) * lanes].astype(jnp.float32)

        def over_lanes(term):
            parts = [jnp.zeros((16, lanes), jnp.float32)] * 2
            for j in range(depth // lanes):
                parts[j % 2] = parts[j % 2] + term(j)
            return jnp.sum(parts[0] + parts[1], axis=-1, keepdims=True) * (1.0 / depth)

        average = over_lanes(piece)

        def squared(j):
            centred = piece(j) - average
            return centred * centred

        factor = lax.rsqrt(over_lanes(squared) + 1e-06)
        for j in range(depth // lanes):
            part = pl.ds(j * lanes, lanes)
            normed = (piece(j) - average) * factor * (1.0 + scale_ref[:, part]) + shift_ref[:, part]
            modulated[rows, part] = normed.astype(jnp.bfloat16)
        return carry

    for i in range(4):
        tok_copies[i].wait()
        if i == 3:
            for copy in w_copies[0]:
                copy.start()
        blocks_of = tok_rows // 16
        lax.fori_loop(i * blocks_of, (i + 1) * blocks_of, head_rows, 0, unroll=min(4, blocks_of))
    head_w = head_w_ref[...]
    patches = lax.dot_general(
        modulated[...],
        jnp.concatenate([head_w, head_w], axis=0),
        (((1,), (1,)), ((), ())),
        preferred_element_type=jnp.float32,
    )
    head_b = jnp.concatenate([row_of(head_b_ref)] * 2, axis=1)
    own[...] = (patches + head_b).astype(jnp.bfloat16).reshape(own.shape)

    def patch_copy(n, dm, d):
        m, g, remote = target(dm, d)
        first, count, slot = PIECES[d]
        return remote, pltpu.make_async_remote_copy(
            src_ref=own.at[pl.ds(first, count)],
            dst_ref=got.at[(0 if dm else TF) + frame, pl.ds(slot, count)],
            send_sem=own_send.at[n],
            recv_sem=(side_recv if d in (-1, 4) else main_recv).at[(0 if dm else TF) + frame],
            device_id=at(m, g),
            device_id_type=MESH,
        )

    sends = [(dm, d) for dm in (1, 0) for d in PIECES]
    count = i32(0)
    for dm, d in sends:
        count = count + target(dm, d)[2].astype(i32)
    for here in (has_up, has_down, has_next, sends_edges & has_up, sends_edges & has_down):
        count = count + here.astype(i32)
    pl.semaphore_wait(barrier, count)

    for n, (dm, d) in enumerate(sends):
        remote, copy = patch_copy(n, dm, d)

        @pl.when(remote)
        def _(copy=copy):
            copy.start()

    for d, (first, size, slot) in PIECES.items():

        @pl.when(4 * part + d == me_g)
        def _(first=first, size=size, slot=slot):
            got[TF + frame, pl.ds(slot, size)] = own[pl.ds(first, size)]

    in_copy.wait()
    w_corner[...] = jnp.zeros(w_corner.shape, jnp.bfloat16)
    for a in range(3):
        for parity, middle in ((0, 2), (1, 1)):
            for cell in range(2):
                for s in range(3):
                    for u in range(3):
                        row = s + cell
                        col = u + middle - 1
                        at_k = (row // 2) * 128 + (col // 2) * 64 + (row % 2) * 32 + (col % 2) * 16
                        at_n = (2 * parity + cell) * chan
                        w_corner[a, pl.ds(at_k, 16), pl.ds(at_n, chan)] = w_in[
                            pl.ds(((a * 3 + u) * 3 + s) * 16, 16), :
                        ]

    for slot in range(2 * TF):
        for side in range(2):
            m, g, remote = source(slot, side)
            for d, (first, size, first_slot) in PIECES.items():
                if (d in (-1, 4)) != bool(side):
                    continue
                which = place == d % 4

                @pl.when(remote & which)
                def _(slot=slot, m=m, g=g, first=first, size=size, first_slot=first_slot, side=side):
                    pltpu.make_async_remote_copy(
                        src_ref=own.at[pl.ds(first, size)],
                        dst_ref=got.at[slot, pl.ds(first_slot, size)],
                        send_sem=own_send.at[0],
                        recv_sem=(side_recv if side else main_recv).at[slot],
                        device_id=at(m, g),
                        device_id_type=MESH,
                    ).wait_recv()

    width = got.shape[-1]
    flat = got[...].astype(jnp.float32).reshape(2 * TF * 4 * KC, width)
    lane = lax.broadcasted_iota(i32, flat.shape, 1)
    pair_col = lax.rem(lax.broadcasted_iota(i32, flat.shape, 0), KC)
    back = jnp.where(pair_col == 0, 0.0, pltpu.roll(flat, 1, 0))
    on = jnp.where(pair_col == KC - 1, 0.0, pltpu.roll(flat, flat.shape[0] - 1, 0))
    left = lane < width // 2
    corner[0] = jnp.where(left, back, flat).astype(jnp.bfloat16).reshape(corner.shape[1:])
    corner[1] = jnp.where(left, flat, on).astype(jnp.bfloat16).reshape(corner.shape[1:])

    col_index = lax.broadcasted_iota(i32, (KC, 1), 0)

    def normed_silu(values, gain, keep=None):
        mean = jnp.sum(values * values, axis=-1, keepdims=True) * (1.0 / chan)
        half = values * lax.rsqrt(mean + 1e-06) * gain
        act = half + half * jnp.tanh(half)
        return act if keep is None else act * keep

    def store_act(ref, f, row, parity, act):
        if parity == 0:
            ref[EVEN, f, row] = act.astype(jnp.bfloat16)
            moved = jnp.where(col_index == KC - 1, 0.0, pltpu.roll(act, KC - 1, 0))
            ref[EVEN_ON, f, row] = moved.astype(jnp.bfloat16)
        else:
            ref[ODD, f, row] = act.astype(jnp.bfloat16)
            moved = jnp.where(col_index == 0, 0.0, pltpu.roll(act, 1, 0))
            ref[ODD_BACK, f, row] = moved.astype(jnp.bfloat16)

    gain_one = row_of(gain_one_ref) * 0.5
    in_bias = jnp.concatenate([row_of(in_b_ref)] * 2, axis=1)
    top_keep = has_up.astype(jnp.float32)
    bottom_keep = has_down.astype(jnp.float32)

    def input_frames(pair, carry):
        first = 2 * pair
        frame_keep = ((pair > 0) | has_prev).astype(jnp.float32)
        for parity in range(2):
            taps = []
            for a in range(3):
                for di in range(2):
                    taps.append(
                        corner[parity, pl.ds(first + a, 2), di : di + 3].reshape(2 * 3 * KC, width)
                    )
            raw = jnp.dot(
                jnp.concatenate(taps, axis=1),
                w_corner[:, :, 2 * chan * parity : 2 * chan * (parity + 1)].reshape(
                    6 * width, 2 * chan
                ),
                preferred_element_type=jnp.float32,
            )
            raw = (raw + in_bias).reshape(2, 3, KC, 2 * chan)
            for f in range(2):
                for ci in range(3):
                    for cell in range(2):
                        row = 2 * ci + cell
                        cells = raw[f, ci, :, cell * chan : (cell + 1) * chan].astype(jnp.bfloat16)
                        stream[parity, first + f, row] = cells
                        keep = frame_keep
                        if row == 0:
                            keep = keep * top_keep
                        if row == EXT_R - 1:
                            keep = keep * bottom_keep
                        act = normed_silu(cells.astype(jnp.float32), gain_one, keep)
                        store_act(act_one, first + f, row, parity, act)
        return carry

    lax.fori_loop(0, 3, input_frames, 0)

    def tap(weight, a, u, s):
        return weight[a * 9 + u * 3 + s]

    def cells(field, version, frames, rows, s):
        if rows is ALL_ROWS:
            view = [field[version, f, s : s + TH] for f in frames]
        else:
            view = [field[version, f, v + s][None] for f in frames for v in rows]
        return jnp.concatenate(view, axis=0).reshape(len(frames) * len(rows) * KC, chan)

    def conv(field, weight, terms, rows, taps):
        def part(versions, outs):
            return jnp.dot(
                jnp.concatenate(
                    [
                        cells(field, v, frames, rows, s)
                        for _, frames in terms
                        for s in taps
                        for v in versions
                    ],
                    axis=1,
                ),
                jnp.concatenate(
                    [
                        jnp.concatenate([tap(weight, a, out[k], s) for out in outs], axis=1)
                        for a, _ in terms
                        for s in taps
                        for k in range(len(versions))
                    ],
                    axis=0,
                ),
                preferred_element_type=jnp.float32,
            )

        even = part((ODD_BACK,), ((0,),))
        odd = part((EVEN_ON,), ((2,),))
        both = part((EVEN, ODD), ((1, 2), (0, 1)))
        total = both + jnp.concatenate([even, odd], axis=1)
        return total.reshape(len(terms[0][1]), len(rows), KC, 2 * chan)

    def add_conv(field, weight, a, first, count, rows, taps):
        total = conv(field, weight, [(a, [first + a + n for n in range(count)])], rows, taps)
        for n in range(count):
            if rows is ALL_ROWS:
                acc[first + n] += total[n]
            else:
                for i, v in enumerate(rows):
                    acc[first + n, v] += total[n, i]

    def start_acc(bias_ref):
        bias = jnp.concatenate([row_of(bias_ref)] * 2, axis=1)
        acc[...] = jnp.broadcast_to(bias.reshape(1, 1, 1, 2 * chan), acc.shape)

    gain_two = row_of(gain_two_ref) * 0.5

    bias_one = jnp.concatenate([row_of(bias_one_ref)] * 2, axis=1)

    def conv_one_rows(rows):
        total = conv(
            act_one, w1, [(a, [a + f for f in range(TF)]) for a in range(3)], rows, ALL_TAPS
        )
        total = total + bias_one
        for parity in range(2):
            for f in range(TF):
                for i, v in enumerate(rows):
                    values = total[f, i, :, parity * chan : (parity + 1) * chan]
                    store_act(act_two, f + 2, v + 1, parity, normed_silu(values, gain_two))

    def row_copy(way):
        frames = pl.ds(2, TF)
        return pltpu.make_async_remote_copy(
            src_ref=act_two.at[pl.ds(EVEN, 2), frames, 1 if way else TH],
            dst_ref=act_two.at[pl.ds(EVEN, 2), frames, EXT_R - 1 if way else 0],
            send_sem=row_send.at[way],
            recv_sem=row_recv.at[way],
            device_id=at(me_m, me_g - 1 if way else me_g + 1),
            device_id_type=MESH,
        )

    def edge_copy(way):
        return pltpu.make_async_remote_copy(
            src_ref=act_two.at[pl.ds(EVEN, 2), pl.ds(TF, 2), 1 if way else TH],
            dst_ref=act_two.at[pl.ds(EVEN, 2), pl.ds(0, 2), EXT_R - 1 if way else 0],
            send_sem=edge_send.at[way],
            recv_sem=edge_recv.at[way],
            device_id=at(me_m + 1, me_g - 1 if way else me_g + 1),
            device_id_type=MESH,
        )

    def pass_copy(way):
        row = EXT_R - 1 if way else 0
        return pltpu.make_async_remote_copy(
            src_ref=act_two.at[pl.ds(EVEN, 2), pl.ds(TF, 2), row],
            dst_ref=act_two.at[pl.ds(EVEN, 2), pl.ds(0, 2), row],
            send_sem=edge_send.at[way],
            recv_sem=edge_recv.at[way],
            device_id=at(me_m + 1, me_g),
            device_id_type=MESH,
        )

    tm_copy = pltpu.make_async_remote_copy(
        src_ref=act_two.at[pl.ds(EVEN, 2), pl.ds(TF, 2), pl.ds(1, TH)],
        dst_ref=act_two.at[pl.ds(EVEN, 2), pl.ds(0, 2), pl.ds(1, TH)],
        send_sem=tm_send.at[0],
        recv_sem=tm_recv.at[0],
        device_id=at(me_m + 1, me_g),
        device_id_type=MESH,
    )
    way_out = (has_down, has_up)
    way_in = (has_up, has_down)

    def widen(f, row):
        even = act_two[EVEN, f, row].astype(jnp.float32)
        moved = jnp.where(col_index == KC - 1, 0.0, pltpu.roll(even, KC - 1, 0))
        act_two[EVEN_ON, f, row] = moved.astype(jnp.bfloat16)
        odd = act_two[ODD, f, row].astype(jnp.float32)
        moved = jnp.where(col_index == 0, 0.0, pltpu.roll(odd, 1, 0))
        act_two[ODD_BACK, f, row] = moved.astype(jnp.bfloat16)

    for copy in w_copies[0]:
        copy.wait()
    for copy in w_copies[1]:
        copy.start()

    def conv_one_part(i, carry):
        conv_one_rows((i, TH - 1 - i))
        for way in range(2):

            @pl.when((i == 0) & way_out[way])
            def _(way=way):
                row_copy(way).start()

            @pl.when((i == 0) & way_out[way] & sends_edges)
            def _(way=way):
                edge_copy(way).start()

        return carry

    lax.fori_loop(0, 2, conv_one_part, 0)

    @pl.when(has_next)
    def _():
        tm_copy.start()

    start_acc(bias_two_ref)
    for copy in w_copies[1]:
        copy.wait()

    def receive_rows():
        for way in range(2):

            @pl.when(way_in[way])
            def _(way=way):
                row_copy(way).wait_recv()

            @pl.when(way_in[way] & passes_edges)
            def _(way=way):
                pass_copy(way).start()

            @pl.when(way_in[way])
            def _(way=way):
                for f in range(TF):
                    widen(2 + f, EXT_R - 1 if way else 0)

    def conv_two_part(i, carry):

        @pl.when(i == 1)
        def _():
            receive_rows()

        for a in (2, 1, 0):
            add_conv(act_two, w2, a, 2 - a, TF - 2 + a, (1 - i, 2 + i), ALL_TAPS)
        return carry

    lax.fori_loop(0, 2, conv_two_part, 0)

    @pl.when(has_prev)
    def _():
        tm_copy.wait_recv()

    for way in range(2):

        @pl.when(way_in[way] & has_prev)
        def _(way=way):
            edge_copy(way).wait_recv()

    @pl.when(has_prev)
    def _():
        for f in range(2):

            def widen_row(row, carry, f=f):
                widen(f, row)
                return carry

            lax.fori_loop(0, EXT_R, widen_row, 0, unroll=True)

    add_conv(act_two, w2, 0, 0, 2, ALL_ROWS, ALL_TAPS)
    add_conv(act_two, w2, 1, 0, 1, ALL_ROWS, ALL_TAPS)

    area = 2 * TH * KC
    to = lax.broadcasted_iota(i32, (area, area), 0)
    of = lax.broadcasted_iota(i32, (area, area), 1)
    order = jnp.where(
        (lax.div(to, 8) == lax.rem(of, KC)) & (lax.rem(to, 8) == lax.div(of, KC)), 1.0, 0.0
    ).astype(jnp.bfloat16)

    def finish_two(f, carry):
        halves = []
        for parity in range(2):
            whole = acc[f, :, :, parity * chan : (parity + 1) * chan] + stream[
                parity, f + 2, 1 : TH + 1
            ].astype(jnp.float32)
            halves.append(whole.astype(jnp.bfloat16).reshape(TH * KC, chan))
        placed = jnp.dot(
            order, jnp.concatenate(halves, axis=0), preferred_element_type=jnp.float32
        )
        out_ref[f, 0] = placed.reshape(2 * KC, TH, chan).astype(jnp.bfloat16)
        return carry

    lax.fori_loop(0, TF, finish_two, 0)

    for n, (dm, d) in enumerate(sends):
        remote, copy = patch_copy(n, dm, d)

        @pl.when(remote)
        def _(copy=copy):
            copy.wait_send()

    @pl.when(has_next)
    def _():
        tm_copy.wait_send()

    for way in range(2):

        @pl.when(way_out[way])
        def _(way=way):
            row_copy(way).wait_send()

        @pl.when(way_out[way] & sends_edges)
        def _(way=way):
            edge_copy(way).wait_send()

        @pl.when(way_in[way] & passes_edges)
        def _(way=way):
            pass_copy(way).wait_send()


def solution(mesh):
    tiles = mesh.shape["tile"]
    blocks = mesh.shape["tm"]

    def body(
        tokens,
        head_shift,
        head_scale,
        head_weight,
        head_bias,
        in_weight,
        in_bias,
        gain_one,
        weight_one,
        bias_one,
        gain_two,
        weight_two,
        bias_two,
    ):
        count, depth = tokens.shape
        chan = weight_one.shape[-1]
        wide = 2 * head_weight.shape[1]
        in_rows = in_weight.shape[0] * in_weight.shape[1] * in_weight.shape[2] * in_weight.shape[3]
        bf16 = jnp.bfloat16
        hbm = pl.BlockSpec(memory_space=pl.ANY)
        vmem = pl.BlockSpec(memory_space=pltpu.VMEM)
        dma = pltpu.SemaphoreType.DMA
        result = pl.pallas_call(
            functools.partial(body_kernel, tiles, blocks),
            out_shape=jax.ShapeDtypeStruct((TF, 1, 2 * KC, TH, chan), bf16),
            in_specs=[
                hbm, vmem, vmem, vmem, vmem, hbm, vmem, vmem, hbm, vmem, vmem, hbm, vmem,
            ],
            out_specs=vmem,
            scratch_shapes=[
                pltpu.VMEM((count, depth), bf16),
                pltpu.VMEM((count, depth), bf16),
                pltpu.VMEM((count // KC, KC, wide), bf16),
                pltpu.VMEM((2 * TF, 4, KC, wide), bf16),
                pltpu.VMEM((2, 2 * TF, 4, KC, wide), bf16),
                pltpu.VMEM((in_rows, chan), bf16),
                pltpu.VMEM((3, 2 * wide, 4 * chan), bf16),
                pltpu.VMEM((27, chan, chan), bf16),
                pltpu.VMEM((27, chan, chan), bf16),
                pltpu.VMEM((4, EXT_F, EXT_R, KC, chan), bf16),
                pltpu.VMEM((4, EXT_F, EXT_R, KC, chan), bf16),
                pltpu.VMEM((2, EXT_F, EXT_R, KC, chan), bf16),
                pltpu.VMEM((TF, TH, KC, 2 * chan), jnp.float32),
                dma((4,)),
                dma((2, 3)),
                dma,
                dma((12,)),
                dma((2 * TF,)),
                dma((2 * TF,)),
                dma((2,)),
                dma((2,)),
                dma((1,)),
                dma((1,)),
                dma((2,)),
                dma((2,)),
            ],
            compiler_params=pltpu.CompilerParams(
                collective_id=0, has_side_effects=True, vmem_limit_bytes=60 * 1024 * 1024
            ),
            name="decode",
        )(
            tokens,
            head_shift[None],
            head_scale[None],
            head_weight.T,
            head_bias,
            in_weight.reshape(in_rows, chan),
            in_bias,
            gain_one,
            weight_one.reshape(27, chan, chan),
            bias_one,
            gain_two,
            weight_two.reshape(27, chan, chan),
            bias_two,
        )
        return result

    in_specs = (P(("tm", "tile"), None), P(), P(), P(), P(), P(), P(), P(), P(), P(), P(), P(), P())
    out_specs = P("tm", "tile", None, None, None)
    return jax.shard_map(body, mesh=mesh, in_specs=in_specs, out_specs=out_specs, check_vma=False)
```

```python
import functools

import jax
import jax.numpy as jnp
from jax import lax
from jax.experimental import pallas as pl
from jax.experimental.pallas import tpu as pltpu
from jax.sharding import PartitionSpec as P

MESH = pl.DeviceIdType.MESH
TF = 4
TH = 4
KC = 32
EXT_F = TF + 2
EXT_R = TH + 2
ODD_BACK, EVEN, ODD, EVEN_ON = range(4)
ALL_ROWS = (0, 1, 2, 3)
ALL_TAPS = (0, 1, 2)

PIECES = {-1: (0, 1, 3), 0: (0, 3, 1), 1: (1, 4, 0), 2: (3, 4, 0), 3: (5, 3, 0), 4: (7, 1, 0)}


def body_kernel(
    tiles,
    blocks,
    tokens,
    shift_ref,
    scale_ref,
    head_w_ref,
    head_b_ref,
    in_w,
    in_b_ref,
    gain_one_ref,
    w_one,
    bias_one_ref,
    gain_two_ref,
    w_two,
    bias_two_ref,
    out_ref,
    tok,
    modulated,
    own,
    got,
    corner,
    w_in,
    w_corner,
    w1,
    w2,
    act_one,
    act_two,
    stream,
    acc,
    tok_sem,
    w_sem,
    in_sem,
    own_send,
    main_recv,
    side_recv,
    row_send,
    row_recv,
    tm_send,
    tm_recv,
    edge_send,
    edge_recv,
):
    me_m = lax.axis_index("tm")
    me_g = lax.axis_index("tile")
    chan = w1.shape[-1]
    depth = tok.shape[1]
    i32 = jnp.int32

    def at(m, g):
        return {"tm": m, "tile": g}

    def row_of(ref):
        return ref[...].reshape(1, ref.shape[0])

    tok_rows = tok.shape[0] // 4
    tok_copies = [
        pltpu.make_async_copy(
            tokens.at[pl.ds(i * tok_rows, tok_rows)],
            tok.at[pl.ds(i * tok_rows, tok_rows)],
            tok_sem.at[i],
        )
        for i in range(4)
    ]
    in_copy = pltpu.make_async_copy(in_w, w_in, in_sem)
    w_copies = [
        [
            pltpu.make_async_copy(src.at[pl.ds(9 * a, 9)], dst.at[pl.ds(9 * a, 9)], w_sem.at[n, a])
            for a in range(3)
        ]
        for n, (src, dst) in enumerate(((w_one, w1), (w_two, w2)))
    ]
    for copy in tok_copies:
        copy.start()
    in_copy.start()

    frame = lax.div(me_g, tiles // TF)
    part = lax.rem(me_g, tiles // TF)
    home = lax.div(me_g, 4)
    place = lax.rem(me_g, 4)

    def target(dm, d):
        g = 4 * part + d
        m = me_m + dm
        inside = (g >= 0) & (g < tiles) & (m < blocks)
        remote = inside if dm else inside & (g != me_g)
        return m, g, remote

    def source(slot, side):
        m = me_m if slot >= TF else me_m - 1
        other = home + jnp.where(place == 0, -1, 1) if side else home
        g = (slot % TF) * (tiles // TF) + other
        inside = m >= 0
        if side:
            inside = (
                inside
                & ((place == 0) | (place == 3))
                & (other >= 0)
                & (other < tiles // TF)
            )
        remote = inside & (g != me_g) if slot >= TF else inside
        return m, g, remote

    has_up = me_g > 0
    has_down = me_g < tiles - 1
    has_prev = me_m > 0
    has_next = me_m < blocks - 1
    sends_edges = has_next & (lax.rem(me_m, 2) == 1)
    passes_edges = has_next & (lax.rem(me_m, 2) == 0)
    gets_edges = has_prev & (lax.rem(me_m, 2) == 0)

    barrier = pltpu.get_barrier_semaphore()

    def greet(m, g, here):
        @pl.when(here)
        def _():
            pl.semaphore_signal(barrier, inc=1, device_id=at(m, g), device_id_type=MESH)

    for slot in range(2 * TF):
        for side in range(2):
            greet(*source(slot, side))
    greet(me_m, me_g - 1, has_up)
    greet(me_m, me_g + 1, has_down)
    greet(me_m - 1, me_g, has_prev)
    greet(me_m - 1, me_g - 1, gets_edges & has_up)
    greet(me_m - 1, me_g + 1, gets_edges & has_down)

    zero_patch = jnp.zeros(got.shape[2:], jnp.bfloat16)

    @pl.when(jnp.logical_not(has_prev))
    def _():
        for slot in range(TF):
            for pair in range(4):
                got[slot, pair] = zero_patch
        for version in range(4):
            for row in range(EXT_R):
                for f in range(2):
                    act_two[version, f, row] = jnp.zeros((KC, chan), jnp.bfloat16)

    @pl.when(jnp.logical_not(has_up))
    def _():
        for slot in range(2 * TF):
            got[slot, 0] = zero_patch
        for version in range(4):
            for f in range(EXT_F):
                act_two[version, f, 0] = jnp.zeros((KC, chan), jnp.bfloat16)

    @pl.when(jnp.logical_not(has_down))
    def _():
        for slot in range(2 * TF):
            got[slot, 3] = zero_patch
        for version in range(4):
            for f in range(EXT_F):
                act_two[version, f, EXT_R - 1] = jnp.zeros((KC, chan), jnp.bfloat16)

    lanes = 128

    def head_rows(i, carry):
        rows = pl.ds(pl.multiple_of(i * 16, 16), 16)

        def piece(j):
            return tok[rows, j * lanes : (j + 1) * lanes].astype(jnp.float32)

        def over_lanes(term):
            parts = [jnp.zeros((16, lanes), jnp.float32)] * 2
            for j in range(depth // lanes):
                parts[j % 2] = parts[j % 2] + term(j)
            return jnp.sum(parts[0] + parts[1], axis=-1, keepdims=True) * (1.0 / depth)

        average = over_lanes(piece)

        def squared(j):
            centred = piece(j) - average
            return centred * centred

        factor = lax.rsqrt(over_lanes(squared) + 1e-06)
        for j in range(depth // lanes):
            part = pl.ds(j * lanes, lanes)
            normed = (piece(j) - average) * factor * (1.0 + scale_ref[:, part]) + shift_ref[:, part]
            modulated[rows, part] = normed.astype(jnp.bfloat16)
        return carry

    for i in range(4):
        tok_copies[i].wait()
        if i == 3:
            for copy in w_copies[0]:
                copy.start()
        blocks_of = tok_rows // 16
        lax.fori_loop(i * blocks_of, (i + 1) * blocks_of, head_rows, 0, unroll=min(4, blocks_of))
    head_w = head_w_ref[...]
    patches = lax.dot_general(
        modulated[...],
        jnp.concatenate([head_w, head_w], axis=0),
        (((1,), (1,)), ((), ())),
        preferred_element_type=jnp.float32,
    )
    head_b = jnp.concatenate([row_of(head_b_ref)] * 2, axis=1)
    spread = (patches + head_b).reshape(own.shape[0], KC, own.shape[2])
    wide_left = lax.broadcasted_iota(i32, own.shape, 2) < own.shape[2] // 2
    own[...] = jnp.where(wide_left, spread[:, : KC // 2], spread[:, KC // 2 :]).astype(jnp.bfloat16)

    def patch_copy(n, dm, d):
        m, g, remote = target(dm, d)
        first, count, slot = PIECES[d]
        return remote, pltpu.make_async_remote_copy(
            src_ref=own.at[pl.ds(first, count)],
            dst_ref=got.at[(0 if dm else TF) + frame, pl.ds(slot, count)],
            send_sem=own_send.at[n],
            recv_sem=(side_recv if d in (-1, 4) else main_recv).at[(0 if dm else TF) + frame],
            device_id=at(m, g),
            device_id_type=MESH,
        )

    sends = [(dm, d) for dm in (1, 0) for d in PIECES]
    count = i32(0)
    for dm, d in sends:
        count = count + target(dm, d)[2].astype(i32)
    for here in (has_up, has_down, has_next, sends_edges & has_up, sends_edges & has_down):
        count = count + here.astype(i32)
    pl.semaphore_wait(barrier, count)

    for n, (dm, d) in enumerate(sends):
        remote, copy = patch_copy(n, dm, d)

        @pl.when(remote)
        def _(copy=copy):
            copy.start()

    for d, (first, size, slot) in PIECES.items():

        @pl.when(4 * part + d == me_g)
        def _(first=first, size=size, slot=slot):
            got[TF + frame, pl.ds(slot, size)] = own[pl.ds(first, size)]

    in_copy.wait()
    w_corner[...] = jnp.zeros(w_corner.shape, jnp.bfloat16)
    for a in range(3):
        for parity, middle in ((0, 2), (1, 1)):
            for cell in range(2):
                for s in range(3):
                    for u in range(3):
                        row = s + cell
                        col = u + middle - 1
                        at_k = (row // 2) * 128 + (col // 2) * 64 + (row % 2) * 32 + (col % 2) * 16
                        at_n = (2 * parity + cell) * chan
                        w_corner[a, pl.ds(at_k, 16), pl.ds(at_n, chan)] = w_in[
                            pl.ds(((a * 3 + u) * 3 + s) * 16, 16), :
                        ]

    for slot in range(2 * TF):
        for side in range(2):
            m, g, remote = source(slot, side)
            for d, (first, size, first_slot) in PIECES.items():
                if (d in (-1, 4)) != bool(side):
                    continue
                which = place == d % 4

                @pl.when(remote & which)
                def _(slot=slot, m=m, g=g, first=first, size=size, first_slot=first_slot, side=side):
                    pltpu.make_async_remote_copy(
                        src_ref=own.at[pl.ds(first, size)],
                        dst_ref=got.at[slot, pl.ds(first_slot, size)],
                        send_sem=own_send.at[0],
                        recv_sem=(side_recv if side else main_recv).at[slot],
                        device_id=at(m, g),
                        device_id_type=MESH,
                    ).wait_recv()

    width = got.shape[-1]
    packed = got[...].astype(jnp.float32).reshape(2 * TF * 4, KC // 2, width)
    turned = pltpu.roll(packed.reshape(-1, width), width // 2, 1).reshape(packed.shape)
    low = lax.broadcasted_iota(i32, packed.shape, 2) < width // 2
    flat = jnp.concatenate(
        [jnp.where(low, packed, turned), jnp.where(low, turned, packed)], axis=1
    ).reshape(2 * TF * 4 * KC, width)
    lane = lax.broadcasted_iota(i32, flat.shape, 1)
    pair_col = lax.rem(lax.broadcasted_iota(i32, flat.shape, 0), KC)
    back = jnp.where(pair_col == 0, 0.0, pltpu.roll(flat, 1, 0))
    on = jnp.where(pair_col == KC - 1, 0.0, pltpu.roll(flat, flat.shape[0] - 1, 0))
    left = lane < width // 2
    corner[0] = jnp.where(left, back, flat).astype(jnp.bfloat16).reshape(corner.shape[1:])
    corner[1] = jnp.where(left, flat, on).astype(jnp.bfloat16).reshape(corner.shape[1:])

    col_index = lax.broadcasted_iota(i32, (KC, 1), 0)

    def normed_silu(values, gain, keep=None):
        mean = jnp.sum(values * values, axis=-1, keepdims=True) * (1.0 / chan)
        half = values * lax.rsqrt(mean + 1e-06) * gain
        act = half + half * jnp.tanh(half)
        return act if keep is None else act * keep

    def store_act(ref, f, row, parity, act):
        if parity == 0:
            ref[EVEN, f, row] = act.astype(jnp.bfloat16)
            moved = jnp.where(col_index == KC - 1, 0.0, pltpu.roll(act, KC - 1, 0))
            ref[EVEN_ON, f, row] = moved.astype(jnp.bfloat16)
        else:
            ref[ODD, f, row] = act.astype(jnp.bfloat16)
            moved = jnp.where(col_index == 0, 0.0, pltpu.roll(act, 1, 0))
            ref[ODD_BACK, f, row] = moved.astype(jnp.bfloat16)

    gain_one = row_of(gain_one_ref) * 0.5
    in_bias = jnp.concatenate([row_of(in_b_ref)] * 2, axis=1)
    top_keep = has_up.astype(jnp.float32)
    bottom_keep = has_down.astype(jnp.float32)

    def input_frames(pair, carry):
        first = 2 * pair
        frame_keep = ((pair > 0) | has_prev).astype(jnp.float32)
        for parity in range(2):
            taps = []
            for a in range(3):
                for di in range(2):
                    taps.append(
                        corner[parity, pl.ds(first + a, 2), di : di + 3].reshape(2 * 3 * KC, width)
                    )
            raw = jnp.dot(
                jnp.concatenate(taps, axis=1),
                w_corner[:, :, 2 * chan * parity : 2 * chan * (parity + 1)].reshape(
                    6 * width, 2 * chan
                ),
                preferred_element_type=jnp.float32,
            )
            raw = (raw + in_bias).reshape(2, 3, KC, 2 * chan)
            for f in range(2):
                for ci in range(3):
                    for cell in range(2):
                        row = 2 * ci + cell
                        cells = raw[f, ci, :, cell * chan : (cell + 1) * chan].astype(jnp.bfloat16)
                        stream[parity, first + f, row] = cells
                        keep = frame_keep
                        if row == 0:
                            keep = keep * top_keep
                        if row == EXT_R - 1:
                            keep = keep * bottom_keep
                        act = normed_silu(cells.astype(jnp.float32), gain_one, keep)
                        store_act(act_one, first + f, row, parity, act)
        return carry

    lax.fori_loop(0, 3, input_frames, 0)

    def tap(weight, a, u, s):
        return weight[a * 9 + u * 3 + s]

    def cells(field, version, frames, rows, s):
        if rows is ALL_ROWS:
            view = [field[version, f, s : s + TH] for f in frames]
        else:
            view = [field[version, f, v + s][None] for f in frames for v in rows]
        return jnp.concatenate(view, axis=0).reshape(len(frames) * len(rows) * KC, chan)

    def conv(field, weight, terms, rows, taps):
        def part(versions, outs):
            return jnp.dot(
                jnp.concatenate(
                    [
                        cells(field, v, frames, rows, s)
                        for _, frames in terms
                        for s in taps
                        for v in versions
                    ],
                    axis=1,
                ),
                jnp.concatenate(
                    [
                        jnp.concatenate([tap(weight, a, out[k], s) for out in outs], axis=1)
                        for a, _ in terms
                        for s in taps
                        for k in range(len(versions))
                    ],
                    axis=0,
                ),
                preferred_element_type=jnp.float32,
            )

        even = part((ODD_BACK,), ((0,),))
        odd = part((EVEN_ON,), ((2,),))
        both = part((EVEN, ODD), ((1, 2), (0, 1)))
        total = both + jnp.concatenate([even, odd], axis=1)
        return total.reshape(len(terms[0][1]), len(rows), KC, 2 * chan)

    def start_acc(bias_ref):
        bias = jnp.concatenate([row_of(bias_ref)] * 2, axis=1)
        acc[...] = jnp.broadcast_to(bias.reshape(1, 1, 1, 2 * chan), acc.shape)

    gain_two = row_of(gain_two_ref) * 0.5

    bias_one = row_of(bias_one_ref)

    def conv_one_row(row):
        total = jnp.dot(
            jnp.concatenate(
                [
                    act_one[u : u + 2, a : a + TF, row + s].reshape(2 * TF * KC, chan)
                    for a in range(3)
                    for u in range(3)
                    for s in range(3)
                ],
                axis=1,
            ),
            w1[...].reshape(27 * chan, chan),
            preferred_element_type=jnp.float32,
        )
        total = (total + bias_one).reshape(2, TF, KC, chan)
        for parity in range(2):
            for f in range(TF):
                act = normed_silu(total[parity, f], gain_two)
                store_act(act_two, f + 2, row + 1, parity, act)

    def conv_one_rows(rows):
        total = conv(
            act_one, w1, [(a, [a + f for f in range(TF)]) for a in range(3)], rows, ALL_TAPS
        )
        total = total + jnp.concatenate([bias_one, bias_one], axis=1)
        for parity in range(2):
            for f in range(TF):
                for i, v in enumerate(rows):
                    values = total[f, i, :, parity * chan : (parity + 1) * chan]
                    store_act(act_two, f + 2, v + 1, parity, normed_silu(values, gain_two))

    def row_copy(way):
        frames = pl.ds(2, TF)
        return pltpu.make_async_remote_copy(
            src_ref=act_two.at[pl.ds(EVEN, 2), frames, 1 if way else TH],
            dst_ref=act_two.at[pl.ds(EVEN, 2), frames, EXT_R - 1 if way else 0],
            send_sem=row_send.at[way],
            recv_sem=row_recv.at[way],
            device_id=at(me_m, me_g - 1 if way else me_g + 1),
            device_id_type=MESH,
        )

    def edge_copy(way):
        return pltpu.make_async_remote_copy(
            src_ref=act_two.at[pl.ds(EVEN, 2), pl.ds(TF, 2), 1 if way else TH],
            dst_ref=act_two.at[pl.ds(EVEN, 2), pl.ds(0, 2), EXT_R - 1 if way else 0],
            send_sem=edge_send.at[way],
            recv_sem=edge_recv.at[way],
            device_id=at(me_m + 1, me_g - 1 if way else me_g + 1),
            device_id_type=MESH,
        )

    def pass_copy(way):
        row = EXT_R - 1 if way else 0
        return pltpu.make_async_remote_copy(
            src_ref=act_two.at[pl.ds(EVEN, 2), pl.ds(TF, 2), row],
            dst_ref=act_two.at[pl.ds(EVEN, 2), pl.ds(0, 2), row],
            send_sem=edge_send.at[way],
            recv_sem=edge_recv.at[way],
            device_id=at(me_m + 1, me_g),
            device_id_type=MESH,
        )

    tm_copy = pltpu.make_async_remote_copy(
        src_ref=act_two.at[pl.ds(EVEN, 2), pl.ds(TF, 2), pl.ds(1, TH)],
        dst_ref=act_two.at[pl.ds(EVEN, 2), pl.ds(0, 2), pl.ds(1, TH)],
        send_sem=tm_send.at[0],
        recv_sem=tm_recv.at[0],
        device_id=at(me_m + 1, me_g),
        device_id_type=MESH,
    )
    way_out = (has_down, has_up)
    way_in = (has_up, has_down)

    def widen(f, row):
        even = act_two[EVEN, f, row].astype(jnp.float32)
        moved = jnp.where(col_index == KC - 1, 0.0, pltpu.roll(even, KC - 1, 0))
        act_two[EVEN_ON, f, row] = moved.astype(jnp.bfloat16)
        odd = act_two[ODD, f, row].astype(jnp.float32)
        moved = jnp.where(col_index == 0, 0.0, pltpu.roll(odd, 1, 0))
        act_two[ODD_BACK, f, row] = moved.astype(jnp.bfloat16)

    for copy in w_copies[0]:
        copy.wait()
    for copy in w_copies[1]:
        copy.start()

    def conv_one_edge(i, carry):
        conv_one_row((TH - 1) * i)
        for way in range(2):

            @pl.when((i == 1 - way) & way_out[way])
            def _(way=way):
                row_copy(way).start()

            @pl.when((i == 1 - way) & way_out[way] & sends_edges)
            def _(way=way):
                edge_copy(way).start()

        return carry

    lax.fori_loop(0, 2, conv_one_edge, 0)
    conv_one_rows((1, 2))

    @pl.when(has_next)
    def _():
        tm_copy.start()

    start_acc(bias_two_ref)
    for copy in w_copies[1]:
        copy.wait()

    late = [(a, [2 + a, 3 + a]) for a in range(3)]
    acc[2:4] += conv(act_two, w2, late, ALL_ROWS, (1,))

    for way in range(2):

        @pl.when(way_in[way])
        def _(way=way):
            row_copy(way).wait_recv()

        @pl.when(way_in[way] & passes_edges)
        def _(way=way):
            pass_copy(way).start()

        @pl.when(way_in[way])
        def _(way=way):
            for f in range(TF):
                widen(2 + f, EXT_R - 1 if way else 0)

    acc[2:4] += conv(act_two, w2, late, ALL_ROWS, (0, 2))

    @pl.when(has_prev)
    def _():
        tm_copy.wait_recv()

    for way in range(2):

        @pl.when(way_in[way] & has_prev)
        def _(way=way):
            edge_copy(way).wait_recv()

    @pl.when(has_prev)
    def _():
        for f in range(2):

            def widen_row(row, carry, f=f):
                widen(f, row)
                return carry

            lax.fori_loop(0, EXT_R, widen_row, 0, unroll=True)

    early = [(a, [a, 1 + a]) for a in range(3)]
    acc[0:2] += conv(act_two, w2, early, ALL_ROWS, ALL_TAPS)

    area = 2 * TH * KC
    to = lax.broadcasted_iota(i32, (area, area), 0)
    of = lax.broadcasted_iota(i32, (area, area), 1)
    order = jnp.where(
        (lax.div(to, 8) == lax.rem(of, KC)) & (lax.rem(to, 8) == lax.div(of, KC)), 1.0, 0.0
    ).astype(jnp.bfloat16)

    def finish_two(f, carry):
        halves = []
        for parity in range(2):
            whole = acc[f, :, :, parity * chan : (parity + 1) * chan] + stream[
                parity, f + 2, 1 : TH + 1
            ].astype(jnp.float32)
            halves.append(whole.astype(jnp.bfloat16).reshape(TH * KC, chan))
        placed = jnp.dot(
            order, jnp.concatenate(halves, axis=0), preferred_element_type=jnp.float32
        )
        out_ref[f, 0] = placed.reshape(2 * KC, TH, chan).astype(jnp.bfloat16)
        return carry

    lax.fori_loop(0, TF, finish_two, 0)

    for n, (dm, d) in enumerate(sends):
        remote, copy = patch_copy(n, dm, d)

        @pl.when(remote)
        def _(copy=copy):
            copy.wait_send()

    @pl.when(has_next)
    def _():
        tm_copy.wait_send()

    for way in range(2):

        @pl.when(way_out[way])
        def _(way=way):
            row_copy(way).wait_send()

        @pl.when(way_out[way] & sends_edges)
        def _(way=way):
            edge_copy(way).wait_send()

        @pl.when(way_in[way] & passes_edges)
        def _(way=way):
            pass_copy(way).wait_send()


def place_kernel(held, out, stage, sem):
    loads = [pltpu.make_async_copy(held.at[f], stage.at[f], sem.at[0, f]) for f in range(TF)]
    stores = [pltpu.make_async_copy(stage.at[f], out.at[f], sem.at[1, f]) for f in range(TF)]
    for copy in loads:
        copy.start()
    for load, store in zip(loads, stores):
        load.wait()
        store.start()
    for copy in stores:
        copy.wait()


def solution(mesh):
    tiles = mesh.shape["tile"]
    blocks = mesh.shape["tm"]

    def body(
        tokens,
        head_shift,
        head_scale,
        head_weight,
        head_bias,
        in_weight,
        in_bias,
        gain_one,
        weight_one,
        bias_one,
        gain_two,
        weight_two,
        bias_two,
    ):
        count, depth = tokens.shape
        chan = weight_one.shape[-1]
        wide = 2 * head_weight.shape[1]
        in_rows = in_weight.shape[0] * in_weight.shape[1] * in_weight.shape[2] * in_weight.shape[3]
        bf16 = jnp.bfloat16
        hbm = pl.BlockSpec(memory_space=pl.ANY)
        vmem = pl.BlockSpec(memory_space=pltpu.VMEM)
        dma = pltpu.SemaphoreType.DMA
        result = pl.pallas_call(
            functools.partial(body_kernel, tiles, blocks),
            out_shape=jax.ShapeDtypeStruct((TF, 1, 2 * KC, TH, chan), bf16),
            in_specs=[
                hbm, vmem, vmem, vmem, vmem, hbm, vmem, vmem, hbm, vmem, vmem, hbm, vmem,
            ],
            out_specs=vmem,
            scratch_shapes=[
                pltpu.VMEM((count, depth), bf16),
                pltpu.VMEM((count, depth), bf16),
                pltpu.VMEM((count // KC, KC // 2, wide), bf16),
                pltpu.VMEM((2 * TF, 4, KC // 2, wide), bf16),
                pltpu.VMEM((2, 2 * TF, 4, KC, wide), bf16),
                pltpu.VMEM((in_rows, chan), bf16),
                pltpu.VMEM((3, 2 * wide, 4 * chan), bf16),
                pltpu.VMEM((27, chan, chan), bf16),
                pltpu.VMEM((27, chan, chan), bf16),
                pltpu.VMEM((4, EXT_F, EXT_R, KC, chan), bf16),
                pltpu.VMEM((4, EXT_F, EXT_R, KC, chan), bf16),
                pltpu.VMEM((2, EXT_F, EXT_R, KC, chan), bf16),
                pltpu.VMEM((TF, TH, KC, 2 * chan), jnp.float32),
                dma((4,)),
                dma((2, 3)),
                dma,
                dma((12,)),
                dma((2 * TF,)),
                dma((2 * TF,)),
                dma((2,)),
                dma((2,)),
                dma((1,)),
                dma((1,)),
                dma((2,)),
                dma((2,)),
            ],
            compiler_params=pltpu.CompilerParams(
                collective_id=0, has_side_effects=True, vmem_limit_bytes=60 * 1024 * 1024
            ),
            name="decode",
        )(
            tokens,
            head_shift[None],
            head_scale[None],
            head_weight.T,
            head_bias,
            in_weight.reshape(in_rows, chan),
            in_bias,
            gain_one,
            weight_one.reshape(27, chan, chan),
            bias_one,
            gain_two,
            weight_two.reshape(27, chan, chan),
            bias_two,
        )
        return pl.pallas_call(
            place_kernel,
            out_shape=jax.ShapeDtypeStruct(result.shape, bf16),
            in_specs=[hbm],
            out_specs=hbm,
            scratch_shapes=[pltpu.VMEM(result.shape, bf16), dma((2, TF))],
            compiler_params=pltpu.CompilerParams(vmem_limit_bytes=60 * 1024 * 1024),
            name="place",
        )(result)

    in_specs = (P(("tm", "tile"), None), P(), P(), P(), P(), P(), P(), P(), P(), P(), P(), P(), P())
    out_specs = P("tm", "tile", None, None, None)
    return jax.shard_map(body, mesh=mesh, in_specs=in_specs, out_specs=out_specs, check_vma=False)
```

```python
import functools

import jax
import jax.numpy as jnp
from jax import lax
from jax.experimental import pallas as pl
from jax.experimental.pallas import tpu as pltpu
from jax.sharding import PartitionSpec as P

MESH = pl.DeviceIdType.MESH
TF = 4
TH = 4
KC = 32
EXT_F = TF + 2
EXT_R = TH + 2
ODD_BACK, EVEN, ODD, EVEN_ON = range(4)
ALL_ROWS = (0, 1, 2, 3)
ALL_TAPS = (0, 1, 2)

PIECES = {-1: (0, 1, 3), 0: (0, 3, 1), 1: (1, 4, 0), 2: (3, 4, 0), 3: (5, 3, 0), 4: (7, 1, 0)}


def body_kernel(
    tiles,
    blocks,
    tokens,
    shift_ref,
    scale_ref,
    head_w_ref,
    head_b_ref,
    in_w,
    in_b_ref,
    gain_one_ref,
    w_one,
    bias_one_ref,
    gain_two_ref,
    w_two,
    bias_two_ref,
    out_ref,
    tok,
    modulated,
    own,
    got,
    corner,
    w_in,
    w_corner,
    w1,
    w2,
    act_one,
    act_two,
    stream,
    acc,
    tok_sem,
    w_sem,
    in_sem,
    own_send,
    main_recv,
    side_recv,
    row_send,
    row_recv,
    tm_send,
    tm_recv,
    edge_send,
    edge_recv,
):
    me_m = lax.axis_index("tm")
    me_g = lax.axis_index("tile")
    chan = w1.shape[-1]
    depth = tok.shape[1]
    i32 = jnp.int32

    def at(m, g):
        return {"tm": m, "tile": g}

    def row_of(ref):
        return ref[...].reshape(1, ref.shape[0])

    tok_rows = tok.shape[0] // 4
    tok_copies = [
        pltpu.make_async_copy(
            tokens.at[pl.ds(i * tok_rows, tok_rows)],
            tok.at[pl.ds(i * tok_rows, tok_rows)],
            tok_sem.at[i],
        )
        for i in range(4)
    ]
    in_copy = pltpu.make_async_copy(in_w, w_in, in_sem)
    w_copies = [
        [
            pltpu.make_async_copy(src.at[pl.ds(9 * a, 9)], dst.at[pl.ds(9 * a, 9)], w_sem.at[n, a])
            for a in range(3)
        ]
        for n, (src, dst) in enumerate(((w_one, w1), (w_two, w2)))
    ]
    for copy in tok_copies:
        copy.start()
    in_copy.start()

    frame = lax.div(me_g, tiles // TF)
    part = lax.rem(me_g, tiles // TF)
    home = lax.div(me_g, 4)
    place = lax.rem(me_g, 4)

    def target(dm, d):
        g = 4 * part + d
        m = me_m + dm
        inside = (g >= 0) & (g < tiles) & (m < blocks)
        remote = inside if dm else inside & (g != me_g)
        return m, g, remote

    def source(slot, side):
        m = me_m if slot >= TF else me_m - 1
        other = home + jnp.where(place == 0, -1, 1) if side else home
        g = (slot % TF) * (tiles // TF) + other
        inside = m >= 0
        if side:
            inside = (
                inside
                & ((place == 0) | (place == 3))
                & (other >= 0)
                & (other < tiles // TF)
            )
        remote = inside & (g != me_g) if slot >= TF else inside
        return m, g, remote

    has_up = me_g > 0
    has_down = me_g < tiles - 1
    has_prev = me_m > 0
    has_next = me_m < blocks - 1
    sends_edges = has_next & (lax.rem(me_m, 2) == 1)
    passes_edges = has_next & (lax.rem(me_m, 2) == 0)
    gets_edges = has_prev & (lax.rem(me_m, 2) == 0)

    barrier = pltpu.get_barrier_semaphore()

    def greet(m, g, here):
        @pl.when(here)
        def _():
            pl.semaphore_signal(barrier, inc=1, device_id=at(m, g), device_id_type=MESH)

    for slot in range(2 * TF):
        for side in range(2):
            greet(*source(slot, side))
    greet(me_m, me_g - 1, has_up)
    greet(me_m, me_g + 1, has_down)
    greet(me_m - 1, me_g, has_prev)
    greet(me_m - 1, me_g - 1, gets_edges & has_up)
    greet(me_m - 1, me_g + 1, gets_edges & has_down)

    zero_patch = jnp.zeros(got.shape[2:], jnp.bfloat16)

    @pl.when(jnp.logical_not(has_prev))
    def _():
        for slot in range(TF):
            for pair in range(4):
                got[slot, pair] = zero_patch
        for version in range(4):
            for row in range(EXT_R):
                for f in range(2):
                    act_two[version, f, row] = jnp.zeros((KC, chan), jnp.bfloat16)

    @pl.when(jnp.logical_not(has_up))
    def _():
        for slot in range(2 * TF):
            got[slot, 0] = zero_patch
        for version in range(4):
            for f in range(EXT_F):
                act_two[version, f, 0] = jnp.zeros((KC, chan), jnp.bfloat16)

    @pl.when(jnp.logical_not(has_down))
    def _():
        for slot in range(2 * TF):
            got[slot, 3] = zero_patch
        for version in range(4):
            for f in range(EXT_F):
                act_two[version, f, EXT_R - 1] = jnp.zeros((KC, chan), jnp.bfloat16)

    lanes = 128

    def head_rows(i, carry):
        rows = pl.ds(pl.multiple_of(i * 16, 16), 16)

        def piece(j):
            return tok[rows, j * lanes : (j + 1) * lanes].astype(jnp.float32)

        def over_lanes(term):
            parts = [jnp.zeros((16, lanes), jnp.float32)] * 2
            for j in range(depth // lanes):
                parts[j % 2] = parts[j % 2] + term(j)
            return jnp.sum(parts[0] + parts[1], axis=-1, keepdims=True) * (1.0 / depth)

        average = over_lanes(piece)

        def squared(j):
            centred = piece(j) - average
            return centred * centred

        factor = lax.rsqrt(over_lanes(squared) + 1e-06)
        for j in range(depth // lanes):
            part = pl.ds(j * lanes, lanes)
            normed = (piece(j) - average) * factor * (1.0 + scale_ref[:, part]) + shift_ref[:, part]
            modulated[rows, part] = normed.astype(jnp.bfloat16)
        return carry

    for i in range(4):
        tok_copies[i].wait()
        if i == 3:
            for copy in w_copies[0]:
                copy.start()
        blocks_of = tok_rows // 16
        lax.fori_loop(i * blocks_of, (i + 1) * blocks_of, head_rows, 0, unroll=min(4, blocks_of))
    head_w = head_w_ref[...]
    patches = lax.dot_general(
        modulated[...],
        jnp.concatenate([head_w, head_w], axis=0),
        (((1,), (1,)), ((), ())),
        preferred_element_type=jnp.float32,
    )
    head_b = jnp.concatenate([row_of(head_b_ref)] * 2, axis=1)
    spread = (patches + head_b).reshape(own.shape[0], KC, own.shape[2])
    wide_left = lax.broadcasted_iota(i32, own.shape, 2) < own.shape[2] // 2
    own[...] = jnp.where(wide_left, spread[:, : KC // 2], spread[:, KC // 2 :]).astype(jnp.bfloat16)

    def patch_copy(n, dm, d):
        m, g, remote = target(dm, d)
        first, count, slot = PIECES[d]
        return remote, pltpu.make_async_remote_copy(
            src_ref=own.at[pl.ds(first, count)],
            dst_ref=got.at[(0 if dm else TF) + frame, pl.ds(slot, count)],
            send_sem=own_send.at[n],
            recv_sem=(side_recv if d in (-1, 4) else main_recv).at[(0 if dm else TF) + frame],
            device_id=at(m, g),
            device_id_type=MESH,
        )

    sends = [(dm, d) for dm in (1, 0) for d in PIECES]
    count = i32(0)
    for dm, d in sends:
        count = count + target(dm, d)[2].astype(i32)
    for here in (has_up, has_down, has_next, sends_edges & has_up, sends_edges & has_down):
        count = count + here.astype(i32)
    pl.semaphore_wait(barrier, count)

    for n, (dm, d) in enumerate(sends):
        remote, copy = patch_copy(n, dm, d)

        @pl.when(remote)
        def _(copy=copy):
            copy.start()

    for d, (first, size, slot) in PIECES.items():

        @pl.when(4 * part + d == me_g)
        def _(first=first, size=size, slot=slot):
            got[TF + frame, pl.ds(slot, size)] = own[pl.ds(first, size)]

    in_copy.wait()
    w_corner[...] = jnp.zeros(w_corner.shape, jnp.bfloat16)
    for a in range(3):
        for parity, middle in ((0, 2), (1, 1)):
            for cell in range(2):
                for s in range(3):
                    for u in range(3):
                        row = s + cell
                        col = u + middle - 1
                        at_k = (row // 2) * 128 + (col // 2) * 64 + (row % 2) * 32 + (col % 2) * 16
                        at_n = (2 * parity + cell) * chan
                        w_corner[a, pl.ds(at_k, 16), pl.ds(at_n, chan)] = w_in[
                            pl.ds(((a * 3 + u) * 3 + s) * 16, 16), :
                        ]

    for slot in range(2 * TF):
        for side in range(2):
            m, g, remote = source(slot, side)
            for d, (first, size, first_slot) in PIECES.items():
                if (d in (-1, 4)) != bool(side):
                    continue
                which = place == d % 4

                @pl.when(remote & which)
                def _(slot=slot, m=m, g=g, first=first, size=size, first_slot=first_slot, side=side):
                    pltpu.make_async_remote_copy(
                        src_ref=own.at[pl.ds(first, size)],
                        dst_ref=got.at[slot, pl.ds(first_slot, size)],
                        send_sem=own_send.at[0],
                        recv_sem=(side_recv if side else main_recv).at[slot],
                        device_id=at(m, g),
                        device_id_type=MESH,
                    ).wait_recv()

    width = got.shape[-1]
    packed = got[...].astype(jnp.float32).reshape(2 * TF * 4, KC // 2, width)
    turned = pltpu.roll(packed.reshape(-1, width), width // 2, 1).reshape(packed.shape)
    low = lax.broadcasted_iota(i32, packed.shape, 2) < width // 2
    flat = jnp.concatenate(
        [jnp.where(low, packed, turned), jnp.where(low, turned, packed)], axis=1
    ).reshape(2 * TF * 4 * KC, width)
    lane = lax.broadcasted_iota(i32, flat.shape, 1)
    pair_col = lax.rem(lax.broadcasted_iota(i32, flat.shape, 0), KC)
    back = jnp.where(pair_col == 0, 0.0, pltpu.roll(flat, 1, 0))
    on = jnp.where(pair_col == KC - 1, 0.0, pltpu.roll(flat, flat.shape[0] - 1, 0))
    left = lane < width // 2
    corner[0] = jnp.where(left, back, flat).astype(jnp.bfloat16).reshape(corner.shape[1:])
    corner[1] = jnp.where(left, flat, on).astype(jnp.bfloat16).reshape(corner.shape[1:])


    def normed_silu(values, gain, keep=None):
        factor = lax.rsqrt(jnp.sum(values * values, axis=-1, keepdims=True) * (1.0 / chan) + 1e-06)
        if keep is not None:
            factor = factor * keep
        half = values * factor * gain
        return half + half * jnp.tanh(half)

    first_eight = lax.broadcasted_iota(i32, (8, chan), 0)

    def moved_on(act):
        moved = pltpu.roll(act, KC - 1, 0)
        last = jnp.where(first_eight == 7, 0.0, moved[KC - 8 :])
        return jnp.concatenate([moved[: KC - 8], last], axis=0)

    def moved_back(act):
        moved = pltpu.roll(act, 1, 0)
        return jnp.concatenate([jnp.where(first_eight == 0, 0.0, moved[:8]), moved[8:]], axis=0)

    def store_act(ref, f, row, parity, act):
        if parity == 0:
            ref[EVEN, f, row] = act.astype(jnp.bfloat16)
            ref[EVEN_ON, f, row] = moved_on(act).astype(jnp.bfloat16)
        else:
            ref[ODD, f, row] = act.astype(jnp.bfloat16)
            ref[ODD_BACK, f, row] = moved_back(act).astype(jnp.bfloat16)

    gain_one = row_of(gain_one_ref) * 0.5
    in_bias = jnp.concatenate([row_of(in_b_ref)] * 2, axis=1)
    top_keep = has_up.astype(jnp.float32)
    bottom_keep = has_down.astype(jnp.float32)
    prev_keep = has_prev.astype(jnp.float32)

    def input_rows(ci):
        for parity in range(2):
            taps = [
                corner[parity, a : a + EXT_F, ci + di].reshape(EXT_F * KC, width)
                for a in range(3)
                for di in range(2)
            ]
            raw = jnp.dot(
                jnp.concatenate(taps, axis=1),
                w_corner[:, :, 2 * chan * parity : 2 * chan * (parity + 1)].reshape(
                    6 * width, 2 * chan
                ),
                preferred_element_type=jnp.float32,
            )
            raw = (raw + in_bias).reshape(EXT_F, KC, 2 * chan)
            for f in range(EXT_F):
                for cell in range(2):
                    row = 2 * ci + cell
                    values = raw[f, :, cell * chan : (cell + 1) * chan]
                    if f >= 2 and 1 <= row <= TH:
                        stream[parity, f - 2, row - 1] = values.astype(jnp.bfloat16)
                    keep = prev_keep if f < 2 else None
                    for edge, edge_keep in ((0, top_keep), (EXT_R - 1, bottom_keep)):
                        if row == edge:
                            keep = edge_keep if keep is None else keep * edge_keep
                    act = normed_silu(values, gain_one, keep)
                    store_act(act_one, f, row, parity, act)

    input_rows(0)
    input_rows(1)

    def tap(weight, a, u, s):
        return weight[a * 9 + u * 3 + s]

    def cells(field, version, frames, rows, s):
        if rows is ALL_ROWS:
            view = [field[version, f, s : s + TH] for f in frames]
        else:
            view = [field[version, f, v + s][None] for f in frames for v in rows]
        return jnp.concatenate(view, axis=0).reshape(len(frames) * len(rows) * KC, chan)

    def product(field, weight, groups, rows, taps):
        return jnp.dot(
            jnp.concatenate(
                [cells(field, version, frames, rows, s) for version, frames, _ in groups for s in taps],
                axis=1,
            ),
            jnp.concatenate(
                [
                    jnp.concatenate([tap(weight, a, u, s) for a, u in outs], axis=1)
                    for _, _, outs in groups
                    for s in taps
                ],
                axis=0,
            ),
            preferred_element_type=jnp.float32,
        )

    def conv(field, weight, frames, rows, taps, paired):
        shape = (len(frames), len(rows), KC, chan)
        sides = []
        for version, u in ((ODD_BACK, 0), (EVEN_ON, 2)):
            if paired:
                firsts = frames[0::2]
                half = (len(firsts), len(rows), KC, chan)
                two = product(
                    field,
                    weight,
                    [(version, [f + n for f in firsts], ((n, u), (n - 1, u))) for n in (1, 2)],
                    rows,
                    taps,
                )
                one = product(field, weight, [(version, firsts, ((0, u),))], rows, taps)
                other = product(
                    field, weight, [(version, [f + 3 for f in firsts], ((2, u),))], rows, taps
                )
                one = (one + two[:, :chan]).reshape(half)
                other = (other + two[:, chan:]).reshape(half)
                side = jnp.stack([one, other], axis=1)
            else:
                side = product(
                    field,
                    weight,
                    [(version, [f + a for f in frames], ((a, u),)) for a in range(3)],
                    rows,
                    taps,
                )
            sides.append(side.reshape(shape))
        both = product(
            field,
            weight,
            [
                (version, [f + a for f in frames], ((a, u + 1), (a, u)))
                for a in range(3)
                for version, u in ((EVEN, 0), (ODD, 1))
            ],
            rows,
            taps,
        )
        return [
            both[:, p * chan : (p + 1) * chan].reshape(shape) + sides[p] for p in range(2)
        ]

    gain_two = row_of(gain_two_ref) * 0.5
    bias_one = row_of(bias_one_ref)
    bias_two = row_of(bias_two_ref)
    own_frames = list(range(TF))

    def act_two_rows(totals, rows):
        for parity, total in enumerate(totals):
            for f in range(TF):
                for i, v in enumerate(rows):
                    act = normed_silu(total[f, i] + bias_one, gain_two)
                    store_act(act_two, f + 2, v + 1, parity, act)

    def row_copy(way):
        frames = pl.ds(2, TF)
        return pltpu.make_async_remote_copy(
            src_ref=act_two.at[pl.ds(EVEN, 2), frames, 1 if way else TH],
            dst_ref=act_two.at[pl.ds(EVEN, 2), frames, EXT_R - 1 if way else 0],
            send_sem=row_send.at[way],
            recv_sem=row_recv.at[way],
            device_id=at(me_m, me_g - 1 if way else me_g + 1),
            device_id_type=MESH,
        )

    def edge_copy(way):
        return pltpu.make_async_remote_copy(
            src_ref=act_two.at[pl.ds(EVEN, 2), pl.ds(TF, 2), 1 if way else TH],
            dst_ref=act_two.at[pl.ds(EVEN, 2), pl.ds(0, 2), EXT_R - 1 if way else 0],
            send_sem=edge_send.at[way],
            recv_sem=edge_recv.at[way],
            device_id=at(me_m + 1, me_g - 1 if way else me_g + 1),
            device_id_type=MESH,
        )

    def pass_copy(way):
        row = EXT_R - 1 if way else 0
        return pltpu.make_async_remote_copy(
            src_ref=act_two.at[pl.ds(EVEN, 2), pl.ds(TF, 2), row],
            dst_ref=act_two.at[pl.ds(EVEN, 2), pl.ds(0, 2), row],
            send_sem=edge_send.at[way],
            recv_sem=edge_recv.at[way],
            device_id=at(me_m + 1, me_g),
            device_id_type=MESH,
        )

    tm_copy = pltpu.make_async_remote_copy(
        src_ref=act_two.at[pl.ds(EVEN, 2), pl.ds(TF, 2), pl.ds(1, TH)],
        dst_ref=act_two.at[pl.ds(EVEN, 2), pl.ds(0, 2), pl.ds(1, TH)],
        send_sem=tm_send.at[0],
        recv_sem=tm_recv.at[0],
        device_id=at(me_m + 1, me_g),
        device_id_type=MESH,
    )
    way_out = (has_down, has_up)
    way_in = (has_up, has_down)

    def widen(f, row):
        even = act_two[EVEN, f, row].astype(jnp.float32)
        act_two[EVEN_ON, f, row] = moved_on(even).astype(jnp.bfloat16)
        odd = act_two[ODD, f, row].astype(jnp.float32)
        act_two[ODD_BACK, f, row] = moved_back(odd).astype(jnp.bfloat16)

    for copy in w_copies[0]:
        copy.wait()
    for copy in w_copies[1]:
        copy.start()

    for row, way in ((0, 1), (TH - 1, 0)):
        totals = conv(act_one, w1, own_frames, (row,), ALL_TAPS, False)
        if row == 0:
            input_rows(2)
        act_two_rows(totals, (row,))

        @pl.when(way_out[way])
        def _(way=way):
            row_copy(way).start()

        @pl.when(way_out[way] & sends_edges)
        def _(way=way):
            edge_copy(way).start()

    act_two_rows(conv(act_one, w1, own_frames, (1, 2), ALL_TAPS, True), (1, 2))

    @pl.when(has_next)
    def _():
        tm_copy.start()

    for copy in w_copies[1]:
        copy.wait()

    totals = conv(act_two, w2, [2, 3], ALL_ROWS, (1,), True)
    for parity in range(2):
        acc[parity] = totals[parity] + bias_two

    for way in range(2):

        @pl.when(way_in[way])
        def _(way=way):
            row_copy(way).wait_recv()

        @pl.when(way_in[way] & passes_edges)
        def _(way=way):
            pass_copy(way).start()

        @pl.when(way_in[way])
        def _(way=way):
            for f in range(TF):
                widen(2 + f, EXT_R - 1 if way else 0)

    totals = conv(act_two, w2, [2, 3], ALL_ROWS, (0, 2), True)
    for parity in range(2):
        acc[parity] += totals[parity]

    @pl.when(has_prev)
    def _():
        tm_copy.wait_recv()

    for way in range(2):

        @pl.when(way_in[way] & has_prev)
        def _(way=way):
            edge_copy(way).wait_recv()

    @pl.when(has_prev)
    def _():
        for f in range(2):

            def widen_row(row, carry, f=f):
                widen(f, row)
                return carry

            lax.fori_loop(0, EXT_R, widen_row, 0, unroll=True)

    area = 2 * TH * KC
    to = lax.broadcasted_iota(i32, (area, area), 0)
    of = lax.broadcasted_iota(i32, (area, area), 1)
    order = jnp.where(
        (lax.div(to, 8) == lax.rem(of, KC)) & (lax.rem(to, 8) == lax.div(of, KC)), 1.0, 0.0
    ).astype(jnp.bfloat16)

    def finish(f, totals):
        halves = [
            (totals[p] + stream[p, f].astype(jnp.float32))
            .astype(jnp.bfloat16)
            .reshape(TH * KC, chan)
            for p in range(2)
        ]
        placed = jnp.dot(
            order, jnp.concatenate(halves, axis=0), preferred_element_type=jnp.float32
        )
        out_ref[f, 0] = placed.reshape(2 * KC, TH, chan).astype(jnp.bfloat16)

    totals = conv(act_two, w2, [0, 1], ALL_ROWS, ALL_TAPS, True)
    for f in range(2):
        finish(2 + f, [acc[p, f] for p in range(2)])
    for f in range(2):
        finish(f, [totals[p][f] + bias_two for p in range(2)])

    for n, (dm, d) in enumerate(sends):
        remote, copy = patch_copy(n, dm, d)

        @pl.when(remote)
        def _(copy=copy):
            copy.wait_send()

    @pl.when(has_next)
    def _():
        tm_copy.wait_send()

    for way in range(2):

        @pl.when(way_out[way])
        def _(way=way):
            row_copy(way).wait_send()

        @pl.when(way_out[way] & sends_edges)
        def _(way=way):
            edge_copy(way).wait_send()

        @pl.when(way_in[way] & passes_edges)
        def _(way=way):
            pass_copy(way).wait_send()


def place_kernel(held, out, sem):
    copies = [pltpu.make_async_copy(held.at[f], out.at[f], sem.at[f]) for f in range(TF)]
    for copy in copies:
        copy.start()
    for copy in copies:
        copy.wait()


def solution(mesh):
    tiles = mesh.shape["tile"]
    blocks = mesh.shape["tm"]

    def body(
        tokens,
        head_shift,
        head_scale,
        head_weight,
        head_bias,
        in_weight,
        in_bias,
        gain_one,
        weight_one,
        bias_one,
        gain_two,
        weight_two,
        bias_two,
    ):
        count, depth = tokens.shape
        chan = weight_one.shape[-1]
        wide = 2 * head_weight.shape[1]
        in_rows = in_weight.shape[0] * in_weight.shape[1] * in_weight.shape[2] * in_weight.shape[3]
        bf16 = jnp.bfloat16
        hbm = pl.BlockSpec(memory_space=pl.ANY)
        vmem = pl.BlockSpec(memory_space=pltpu.VMEM)
        dma = pltpu.SemaphoreType.DMA
        result = pl.pallas_call(
            functools.partial(body_kernel, tiles, blocks),
            out_shape=pltpu.VMEM((TF, 1, 2 * KC, TH, chan), bf16),
            in_specs=[
                hbm, vmem, vmem, vmem, vmem, hbm, vmem, vmem, hbm, vmem, vmem, hbm, vmem,
            ],
            out_specs=vmem,
            scratch_shapes=[
                pltpu.VMEM((count, depth), bf16),
                pltpu.VMEM((count, depth), bf16),
                pltpu.VMEM((count // KC, KC // 2, wide), bf16),
                pltpu.VMEM((2 * TF, 4, KC // 2, wide), bf16),
                pltpu.VMEM((2, 2 * TF, 4, KC, wide), bf16),
                pltpu.VMEM((in_rows, chan), bf16),
                pltpu.VMEM((3, 2 * wide, 4 * chan), bf16),
                pltpu.VMEM((27, chan, chan), bf16),
                pltpu.VMEM((27, chan, chan), bf16),
                pltpu.VMEM((4, EXT_F, EXT_R, KC, chan), bf16),
                pltpu.VMEM((4, EXT_F, EXT_R, KC, chan), bf16),
                pltpu.VMEM((2, TF, TH, KC, chan), bf16),
                pltpu.VMEM((2, 2, TH, KC, chan), jnp.float32),
                dma((4,)),
                dma((2, 3)),
                dma,
                dma((12,)),
                dma((2 * TF,)),
                dma((2 * TF,)),
                dma((2,)),
                dma((2,)),
                dma((1,)),
                dma((1,)),
                dma((2,)),
                dma((2,)),
            ],
            compiler_params=pltpu.CompilerParams(
                collective_id=0, has_side_effects=True, vmem_limit_bytes=56 * 1024 * 1024
            ),
            name="decode",
        )(
            tokens,
            head_shift[None],
            head_scale[None],
            head_weight.T,
            head_bias,
            in_weight.reshape(in_rows, chan),
            in_bias,
            gain_one,
            weight_one.reshape(27, chan, chan),
            bias_one,
            gain_two,
            weight_two.reshape(27, chan, chan),
            bias_two,
        )
        return pl.pallas_call(
            place_kernel,
            out_shape=jax.ShapeDtypeStruct(result.shape, bf16),
            in_specs=[vmem],
            out_specs=hbm,
            scratch_shapes=[dma((TF,))],
            name="place",
        )(result)

    in_specs = (P(("tm", "tile"), None), P(), P(), P(), P(), P(), P(), P(), P(), P(), P(), P(), P())
    out_specs = P("tm", "tile", None, None, None)
    return jax.shard_map(body, mesh=mesh, in_specs=in_specs, out_specs=out_specs, check_vma=False)
```

```python
import functools

import jax
import jax.numpy as jnp
from jax import lax
from jax.experimental import pallas as pl
from jax.experimental.pallas import tpu as pltpu
from jax.sharding import PartitionSpec as P

MESH = pl.DeviceIdType.MESH
TF = 4
TH = 4
KC = 32
EXT_F = TF + 2
EXT_R = TH + 2
ODD_BACK, EVEN, ODD, EVEN_ON = range(4)
ALL_ROWS = (0, 1, 2, 3)
ALL_TAPS = (0, 1, 2)

PIECES = {-1: (0, 1, 3), 0: (0, 3, 1), 1: (1, 4, 0), 2: (3, 4, 0), 3: (5, 3, 0), 4: (7, 1, 0)}


def body_kernel(
    tiles,
    blocks,
    tokens,
    shift_ref,
    scale_ref,
    head_w_ref,
    head_b_ref,
    in_w,
    in_b_ref,
    gain_one_ref,
    w_one,
    bias_one_ref,
    gain_two_ref,
    w_two,
    bias_two_ref,
    out_ref,
    tok,
    modulated,
    affine,
    own,
    got,
    corner,
    w_in,
    w_corner,
    w1,
    w2,
    act_one,
    act_two,
    stream,
    third,
    acc,
    tok_sem,
    w_sem,
    in_sem,
    own_send,
    main_recv,
    side_recv,
    row_send,
    row_recv,
    tm_send,
    tm_recv,
    edge_send,
    edge_recv,
):
    me_m = lax.axis_index("tm")
    me_g = lax.axis_index("tile")
    chan = w1.shape[-1]
    depth = tok.shape[1]
    i32 = jnp.int32

    def at(m, g):
        return {"tm": m, "tile": g}

    def row_of(ref):
        return ref[...].reshape(1, ref.shape[0])

    tok_rows = tok.shape[0] // 4
    tok_copies = [
        pltpu.make_async_copy(
            tokens.at[pl.ds(i * tok_rows, tok_rows)],
            tok.at[pl.ds(i * tok_rows, tok_rows)],
            tok_sem.at[i],
        )
        for i in range(4)
    ]
    in_copy = pltpu.make_async_copy(in_w, w_in, in_sem)
    w_copies = [
        [
            pltpu.make_async_copy(src.at[pl.ds(9 * a, 9)], dst.at[pl.ds(9 * a, 9)], w_sem.at[n, a])
            for a in range(3)
        ]
        for n, (src, dst) in enumerate(((w_one, w1), (w_two, w2)))
    ]
    for copy in tok_copies:
        copy.start()
    in_copy.start()

    frame = lax.div(me_g, tiles // TF)
    part = lax.rem(me_g, tiles // TF)
    home = lax.div(me_g, 4)
    place = lax.rem(me_g, 4)

    def target(dm, d):
        g = 4 * part + d
        m = me_m + dm
        inside = (g >= 0) & (g < tiles) & (m < blocks)
        remote = inside if dm else inside & (g != me_g)
        return m, g, remote

    def source(slot, side):
        m = me_m if slot >= TF else me_m - 1
        other = home + jnp.where(place == 0, -1, 1) if side else home
        g = (slot % TF) * (tiles // TF) + other
        inside = m >= 0
        if side:
            inside = (
                inside
                & ((place == 0) | (place == 3))
                & (other >= 0)
                & (other < tiles // TF)
            )
        remote = inside & (g != me_g) if slot >= TF else inside
        return m, g, remote

    has_up = me_g > 0
    has_down = me_g < tiles - 1
    has_prev = me_m > 0
    has_next = me_m < blocks - 1
    sends_edges = has_next & (lax.rem(me_m, 2) == 1)
    passes_edges = has_next & (lax.rem(me_m, 2) == 0)
    gets_edges = has_prev & (lax.rem(me_m, 2) == 0)

    barrier = pltpu.get_barrier_semaphore()

    def greet(m, g, here):
        @pl.when(here)
        def _():
            pl.semaphore_signal(barrier, inc=1, device_id=at(m, g), device_id_type=MESH)

    for slot in range(2 * TF):
        for side in range(2):
            greet(*source(slot, side))
    greet(me_m, me_g - 1, has_up)
    greet(me_m, me_g + 1, has_down)
    greet(me_m - 1, me_g, has_prev)
    greet(me_m - 1, me_g - 1, gets_edges & has_up)
    greet(me_m - 1, me_g + 1, gets_edges & has_down)

    zero_patch = jnp.zeros(got.shape[2:], jnp.bfloat16)

    @pl.when(jnp.logical_not(has_prev))
    def _():
        for slot in range(TF):
            for pair in range(4):
                got[slot, pair] = zero_patch
        for version in range(4):
            for row in range(EXT_R):
                for f in range(2):
                    act_two[version, f, row] = jnp.zeros((KC, chan), jnp.bfloat16)

    @pl.when(jnp.logical_not(has_up))
    def _():
        for slot in range(2 * TF):
            got[slot, 0] = zero_patch
        for version in range(4):
            for f in range(EXT_F):
                act_two[version, f, 0] = jnp.zeros((KC, chan), jnp.bfloat16)

    @pl.when(jnp.logical_not(has_down))
    def _():
        for slot in range(2 * TF):
            got[slot, 3] = zero_patch
        for version in range(4):
            for f in range(EXT_F):
                act_two[version, f, EXT_R - 1] = jnp.zeros((KC, chan), jnp.bfloat16)

    lanes = 128

    affine[0] = jnp.broadcast_to(1.0 + scale_ref[...], affine.shape[1:])
    affine[1] = jnp.broadcast_to(shift_ref[...], affine.shape[1:])

    def head_rows(i, carry):
        rows = pl.ds(pl.multiple_of(i * 16, 16), 16)

        def piece(j):
            return tok[rows, j * lanes : (j + 1) * lanes].astype(jnp.float32)

        base = piece(0)[:, :1]
        sums = [jnp.zeros((16, lanes), jnp.float32)] * 2
        squares = [jnp.zeros((16, lanes), jnp.float32)] * 2
        for j in range(depth // lanes):
            away = piece(j) - base
            sums[j % 2] = sums[j % 2] + away
            squares[j % 2] = squares[j % 2] + away * away
        offset = jnp.sum(sums[0] + sums[1], axis=-1, keepdims=True) * (1.0 / depth)
        second = jnp.sum(squares[0] + squares[1], axis=-1, keepdims=True) * (1.0 / depth)
        average = base + offset
        factor = lax.rsqrt(jnp.maximum(second - offset * offset, 0.0) + 1e-06)
        for j in range(depth // lanes):
            part = pl.ds(j * lanes, lanes)
            normed = (piece(j) - average) * factor * affine[0, :, part] + affine[1, :, part]
            modulated[rows, part] = normed.astype(jnp.bfloat16)
        return carry

    for i in range(4):
        tok_copies[i].wait()
        if i == 3:
            for copy in w_copies[0]:
                copy.start()
        blocks_of = tok_rows // 16
        lax.fori_loop(i * blocks_of, (i + 1) * blocks_of, head_rows, 0, unroll=min(4, blocks_of))
    head_w = head_w_ref[...]
    patches = lax.dot_general(
        modulated[...],
        jnp.concatenate([head_w, head_w], axis=0),
        (((1,), (1,)), ((), ())),
        preferred_element_type=jnp.float32,
    )
    head_b = jnp.concatenate([row_of(head_b_ref)] * 2, axis=1)
    spread = (patches + head_b).reshape(own.shape[0], KC, own.shape[2])
    wide_left = lax.broadcasted_iota(i32, own.shape, 2) < own.shape[2] // 2
    own[...] = jnp.where(wide_left, spread[:, : KC // 2], spread[:, KC // 2 :]).astype(jnp.bfloat16)

    def patch_copy(n, dm, d):
        m, g, remote = target(dm, d)
        first, count, slot = PIECES[d]
        return remote, pltpu.make_async_remote_copy(
            src_ref=own.at[pl.ds(first, count)],
            dst_ref=got.at[(0 if dm else TF) + frame, pl.ds(slot, count)],
            send_sem=own_send.at[n],
            recv_sem=(side_recv if d in (-1, 4) else main_recv).at[(0 if dm else TF) + frame],
            device_id=at(m, g),
            device_id_type=MESH,
        )

    sends = [(dm, d) for dm in (1, 0) for d in PIECES]
    count = i32(0)
    for dm, d in sends:
        count = count + target(dm, d)[2].astype(i32)
    for here in (has_up, has_down, has_next, sends_edges & has_up, sends_edges & has_down):
        count = count + here.astype(i32)
    pl.semaphore_wait(barrier, count)

    for n, (dm, d) in enumerate(sends):
        remote, copy = patch_copy(n, dm, d)

        @pl.when(remote)
        def _(copy=copy):
            copy.start()

    for d, (first, size, slot) in PIECES.items():

        @pl.when(4 * part + d == me_g)
        def _(first=first, size=size, slot=slot):
            got[TF + frame, pl.ds(slot, size)] = own[pl.ds(first, size)]

    in_copy.wait()
    w_corner[...] = jnp.zeros(w_corner.shape, jnp.bfloat16)
    for a in range(3):
        for parity, middle in ((0, 2), (1, 1)):
            for cell in range(2):
                for s in range(3):
                    for u in range(3):
                        row = s + cell
                        col = u + middle - 1
                        at_k = (row // 2) * 128 + (col // 2) * 64 + (row % 2) * 32 + (col % 2) * 16
                        at_n = (2 * parity + cell) * chan
                        w_corner[a, pl.ds(at_k, 16), pl.ds(at_n, chan)] = w_in[
                            pl.ds(((a * 3 + u) * 3 + s) * 16, 16), :
                        ]

    for slot in range(2 * TF):
        for side in range(2):
            m, g, remote = source(slot, side)
            for d, (first, size, first_slot) in PIECES.items():
                if (d in (-1, 4)) != bool(side):
                    continue
                which = place == d % 4

                @pl.when(remote & which)
                def _(slot=slot, m=m, g=g, first=first, size=size, first_slot=first_slot, side=side):
                    pltpu.make_async_remote_copy(
                        src_ref=own.at[pl.ds(first, size)],
                        dst_ref=got.at[slot, pl.ds(first_slot, size)],
                        send_sem=own_send.at[0],
                        recv_sem=(side_recv if side else main_recv).at[slot],
                        device_id=at(m, g),
                        device_id_type=MESH,
                    ).wait_recv()

    width = got.shape[-1]
    packed = got[...].astype(jnp.float32).reshape(2 * TF * 4, KC // 2, width)
    turned = pltpu.roll(packed.reshape(-1, width), width // 2, 1).reshape(packed.shape)
    low = lax.broadcasted_iota(i32, packed.shape, 2) < width // 2
    flat = jnp.concatenate(
        [jnp.where(low, packed, turned), jnp.where(low, turned, packed)], axis=1
    ).reshape(2 * TF * 4 * KC, width)
    lane = lax.broadcasted_iota(i32, flat.shape, 1)
    pair_col = lax.rem(lax.broadcasted_iota(i32, flat.shape, 0), KC)
    back = jnp.where(pair_col == 0, 0.0, pltpu.roll(flat, 1, 0))
    on = jnp.where(pair_col == KC - 1, 0.0, pltpu.roll(flat, flat.shape[0] - 1, 0))
    left = lane < width // 2
    corner[0] = jnp.where(left, back, flat).astype(jnp.bfloat16).reshape(corner.shape[1:])
    corner[1] = jnp.where(left, flat, on).astype(jnp.bfloat16).reshape(corner.shape[1:])


    def normed_silu(values, gain, keep=None):
        factor = lax.rsqrt(jnp.sum(values * values, axis=-1, keepdims=True) * (1.0 / chan) + 1e-06)
        if keep is not None:
            factor = factor * keep
        half = values * factor * gain
        return half + half * jnp.tanh(half)

    first_eight = lax.broadcasted_iota(i32, (8, chan), 0)

    def moved_on(act):
        moved = pltpu.roll(act, KC - 1, 0)
        last = jnp.where(first_eight == 7, 0.0, moved[KC - 8 :])
        return jnp.concatenate([moved[: KC - 8], last], axis=0)

    def moved_back(act):
        moved = pltpu.roll(act, 1, 0)
        return jnp.concatenate([jnp.where(first_eight == 0, 0.0, moved[:8]), moved[8:]], axis=0)

    def store_act(ref, f, row, parity, act):
        if parity == 0:
            ref[EVEN, f, row] = act.astype(jnp.bfloat16)
            ref[EVEN_ON, f, row] = moved_on(act).astype(jnp.bfloat16)
        else:
            ref[ODD, f, row] = act.astype(jnp.bfloat16)
            ref[ODD_BACK, f, row] = moved_back(act).astype(jnp.bfloat16)

    gain_one = row_of(gain_one_ref) * 0.5
    in_bias = jnp.concatenate([row_of(in_b_ref)] * 2, axis=1)
    top_keep = has_up.astype(jnp.float32)
    bottom_keep = has_down.astype(jnp.float32)
    prev_keep = has_prev.astype(jnp.float32)

    def input_product(ci, parity):
        taps = [
            corner[parity, a : a + EXT_F, ci + di].reshape(EXT_F * KC, width)
            for a in range(3)
            for di in range(2)
        ]
        raw = jnp.dot(
            jnp.concatenate(taps, axis=1),
            w_corner[:, :, 2 * chan * parity : 2 * chan * (parity + 1)].reshape(
                6 * width, 2 * chan
            ),
            preferred_element_type=jnp.float32,
        )
        return (raw + in_bias).reshape(EXT_F, KC, 2 * chan)

    def input_act(row, parity, values):
        for f in range(EXT_F):
            if f >= 2 and 1 <= row <= TH:
                stream[parity, f - 2, row - 1] = values[f].astype(jnp.bfloat16)
            keep = prev_keep if f < 2 else None
            for edge, edge_keep in ((0, top_keep), (EXT_R - 1, bottom_keep)):
                if row == edge:
                    keep = edge_keep if keep is None else keep * edge_keep
            store_act(act_one, f, row, parity, normed_silu(values[f], gain_one, keep))

    for ci in range(2):
        for parity in range(2):
            raw = input_product(ci, parity)
            input_act(2 * ci, parity, raw[:, :, :chan])
            if ci == 0:
                input_act(1, parity, raw[:, :, chan:])
            else:
                third[parity] = raw[:, :, chan:]

    def rest_of_input():
        for parity in range(2):
            input_act(3, parity, third[parity])
        for parity in range(2):
            raw = input_product(2, parity)
            for cell in range(2):
                input_act(4 + cell, parity, raw[:, :, cell * chan : (cell + 1) * chan])

    def tap(weight, a, u, s):
        return weight[a * 9 + u * 3 + s]

    def cells(field, version, frames, rows, s):
        if rows is ALL_ROWS:
            view = [field[version, f, s : s + TH] for f in frames]
        else:
            view = [field[version, f, v + s][None] for f in frames for v in rows]
        return jnp.concatenate(view, axis=0).reshape(len(frames) * len(rows) * KC, chan)

    def product(field, weight, groups, rows, taps):
        return jnp.dot(
            jnp.concatenate(
                [cells(field, version, frames, rows, s) for version, frames, _ in groups for s in taps],
                axis=1,
            ),
            jnp.concatenate(
                [
                    jnp.concatenate([tap(weight, a, u, s) for a, u in outs], axis=1)
                    for _, _, outs in groups
                    for s in taps
                ],
                axis=0,
            ),
            preferred_element_type=jnp.float32,
        )

    def conv(field, weight, frames, rows, taps, paired):
        shape = (len(frames), len(rows), KC, chan)
        sides = []
        for version, u in ((ODD_BACK, 0), (EVEN_ON, 2)):
            if paired:
                firsts = frames[0::2]
                half = (len(firsts), len(rows), KC, chan)
                two = product(
                    field,
                    weight,
                    [(version, [f + n for f in firsts], ((n, u), (n - 1, u))) for n in (1, 2)],
                    rows,
                    taps,
                )
                one = product(field, weight, [(version, firsts, ((0, u),))], rows, taps)
                other = product(
                    field, weight, [(version, [f + 3 for f in firsts], ((2, u),))], rows, taps
                )
                one = (one + two[:, :chan]).reshape(half)
                other = (other + two[:, chan:]).reshape(half)
                side = jnp.stack([one, other], axis=1)
            else:
                side = product(
                    field,
                    weight,
                    [(version, [f + a for f in frames], ((a, u),)) for a in range(3)],
                    rows,
                    taps,
                )
            sides.append(side.reshape(shape))
        both = product(
            field,
            weight,
            [
                (version, [f + a for f in frames], ((a, u + 1), (a, u)))
                for a in range(3)
                for version, u in ((EVEN, 0), (ODD, 1))
            ],
            rows,
            taps,
        )
        return [
            both[:, p * chan : (p + 1) * chan].reshape(shape) + sides[p] for p in range(2)
        ]

    gain_two = row_of(gain_two_ref) * 0.5
    bias_one = row_of(bias_one_ref)
    bias_two = row_of(bias_two_ref)
    own_frames = list(range(TF))

    def act_two_rows(totals, rows):
        for parity, total in enumerate(totals):
            for f in range(TF):
                for i, v in enumerate(rows):
                    act = normed_silu(total[f, i] + bias_one, gain_two)
                    store_act(act_two, f + 2, v + 1, parity, act)

    def row_copy(way):
        frames = pl.ds(2, TF)
        return pltpu.make_async_remote_copy(
            src_ref=act_two.at[pl.ds(EVEN, 2), frames, 1 if way else TH],
            dst_ref=act_two.at[pl.ds(EVEN, 2), frames, EXT_R - 1 if way else 0],
            send_sem=row_send.at[way],
            recv_sem=row_recv.at[way],
            device_id=at(me_m, me_g - 1 if way else me_g + 1),
            device_id_type=MESH,
        )

    def edge_copy(way):
        return pltpu.make_async_remote_copy(
            src_ref=act_two.at[pl.ds(EVEN, 2), pl.ds(TF, 2), 1 if way else TH],
            dst_ref=act_two.at[pl.ds(EVEN, 2), pl.ds(0, 2), EXT_R - 1 if way else 0],
            send_sem=edge_send.at[way],
            recv_sem=edge_recv.at[way],
            device_id=at(me_m + 1, me_g - 1 if way else me_g + 1),
            device_id_type=MESH,
        )

    def pass_copy(way):
        row = EXT_R - 1 if way else 0
        return pltpu.make_async_remote_copy(
            src_ref=act_two.at[pl.ds(EVEN, 2), pl.ds(TF, 2), row],
            dst_ref=act_two.at[pl.ds(EVEN, 2), pl.ds(0, 2), row],
            send_sem=edge_send.at[way],
            recv_sem=edge_recv.at[way],
            device_id=at(me_m + 1, me_g),
            device_id_type=MESH,
        )

    def tm_copy(n):
        rows = pl.ds((1, TH, 2)[n], (1, 1, 2)[n])
        return pltpu.make_async_remote_copy(
            src_ref=act_two.at[pl.ds(EVEN, 2), pl.ds(TF, 2), rows],
            dst_ref=act_two.at[pl.ds(EVEN, 2), pl.ds(0, 2), rows],
            send_sem=tm_send.at[n],
            recv_sem=tm_recv.at[n],
            device_id=at(me_m + 1, me_g),
            device_id_type=MESH,
        )

    way_out = (has_down, has_up)
    way_in = (has_up, has_down)

    def widen(f, row):
        even = act_two[EVEN, f, row].astype(jnp.float32)
        act_two[EVEN_ON, f, row] = moved_on(even).astype(jnp.bfloat16)
        odd = act_two[ODD, f, row].astype(jnp.float32)
        act_two[ODD_BACK, f, row] = moved_back(odd).astype(jnp.bfloat16)

    for copy in w_copies[0]:
        copy.wait()
    for copy in w_copies[1]:
        copy.start()

    for row, way in ((0, 1), (TH - 1, 0)):
        totals = conv(act_one, w1, own_frames, (row,), ALL_TAPS, False)
        if row == 0:
            rest_of_input()
        act_two_rows(totals, (row,))

        @pl.when(way_out[way])
        def _(way=way):
            row_copy(way).start()

        @pl.when(way_out[way] & sends_edges)
        def _(way=way):
            edge_copy(way).start()

        @pl.when(has_next)
        def _(way=way):
            tm_copy(1 - way).start()

    act_two_rows(conv(act_one, w1, own_frames, (1, 2), ALL_TAPS, True), (1, 2))

    @pl.when(has_next)
    def _():
        tm_copy(2).start()

    for copy in w_copies[1]:
        copy.wait()

    totals = conv(act_two, w2, [2, 3], ALL_ROWS, (1,), True)
    for parity in range(2):
        acc[parity] = totals[parity] + bias_two

    for way in range(2):

        @pl.when(way_in[way])
        def _(way=way):
            row_copy(way).wait_recv()

        @pl.when(way_in[way] & passes_edges)
        def _(way=way):
            pass_copy(way).start()

        @pl.when(way_in[way])
        def _(way=way):
            for f in range(TF):
                widen(2 + f, EXT_R - 1 if way else 0)

    totals = conv(act_two, w2, [2, 3], ALL_ROWS, (0, 2), True)
    for parity in range(2):
        acc[parity] += totals[parity]

    @pl.when(has_prev)
    def _():
        for n in range(3):
            tm_copy(n).wait_recv()

    for way in range(2):

        @pl.when(way_in[way] & has_prev)
        def _(way=way):
            edge_copy(way).wait_recv()

    @pl.when(has_prev)
    def _():
        for f in range(2):

            def widen_row(row, carry, f=f):
                widen(f, row)
                return carry

            lax.fori_loop(0, EXT_R, widen_row, 0, unroll=True)

    area = 2 * TH * KC
    to = lax.broadcasted_iota(i32, (area, area), 0)
    of = lax.broadcasted_iota(i32, (area, area), 1)
    order = jnp.where(
        (lax.div(to, 8) == lax.rem(of, KC)) & (lax.rem(to, 8) == lax.div(of, KC)), 1.0, 0.0
    ).astype(jnp.bfloat16)

    def finish(f, totals):
        halves = [
            (totals[p] + stream[p, f].astype(jnp.float32))
            .astype(jnp.bfloat16)
            .reshape(TH * KC, chan)
            for p in range(2)
        ]
        placed = jnp.dot(
            order, jnp.concatenate(halves, axis=0), preferred_element_type=jnp.float32
        )
        out_ref[f, 0] = placed.reshape(2 * KC, TH, chan).astype(jnp.bfloat16)

    totals = conv(act_two, w2, [0, 1], ALL_ROWS, ALL_TAPS, True)
    for f in range(2):
        finish(2 + f, [acc[p, f] for p in range(2)])
    for f in range(2):
        finish(f, [totals[p][f] + bias_two for p in range(2)])

    for n, (dm, d) in enumerate(sends):
        remote, copy = patch_copy(n, dm, d)

        @pl.when(remote)
        def _(copy=copy):
            copy.wait_send()

    @pl.when(has_next)
    def _():
        for n in range(3):
            tm_copy(n).wait_send()

    for way in range(2):

        @pl.when(way_out[way])
        def _(way=way):
            row_copy(way).wait_send()

        @pl.when(way_out[way] & sends_edges)
        def _(way=way):
            edge_copy(way).wait_send()

        @pl.when(way_in[way] & passes_edges)
        def _(way=way):
            pass_copy(way).wait_send()


def solution(mesh):
    tiles = mesh.shape["tile"]
    blocks = mesh.shape["tm"]

    def body(
        tokens,
        head_shift,
        head_scale,
        head_weight,
        head_bias,
        in_weight,
        in_bias,
        gain_one,
        weight_one,
        bias_one,
        gain_two,
        weight_two,
        bias_two,
    ):
        count, depth = tokens.shape
        chan = weight_one.shape[-1]
        wide = 2 * head_weight.shape[1]
        in_rows = in_weight.shape[0] * in_weight.shape[1] * in_weight.shape[2] * in_weight.shape[3]
        bf16 = jnp.bfloat16
        hbm = pl.BlockSpec(memory_space=pl.ANY)
        vmem = pl.BlockSpec(memory_space=pltpu.VMEM)
        dma = pltpu.SemaphoreType.DMA
        result = pl.pallas_call(
            functools.partial(body_kernel, tiles, blocks),
            out_shape=pltpu.VMEM((TF, 1, 2 * KC, TH, chan), bf16),
            in_specs=[
                hbm, vmem, vmem, vmem, vmem, hbm, vmem, vmem, hbm, vmem, vmem, hbm, vmem,
            ],
            out_specs=vmem,
            scratch_shapes=[
                pltpu.VMEM((count, depth), bf16),
                pltpu.VMEM((count, depth), bf16),
                pltpu.VMEM((2, 16, depth), jnp.float32),
                pltpu.VMEM((count // KC, KC // 2, wide), bf16),
                pltpu.VMEM((2 * TF, 4, KC // 2, wide), bf16),
                pltpu.VMEM((2, 2 * TF, 4, KC, wide), bf16),
                pltpu.VMEM((in_rows, chan), bf16),
                pltpu.VMEM((3, 2 * wide, 4 * chan), bf16),
                pltpu.VMEM((27, chan, chan), bf16),
                pltpu.VMEM((27, chan, chan), bf16),
                pltpu.VMEM((4, EXT_F, EXT_R, KC, chan), bf16),
                pltpu.VMEM((4, EXT_F, EXT_R, KC, chan), bf16),
                pltpu.VMEM((2, TF, TH, KC, chan), bf16),
                pltpu.VMEM((2, EXT_F, KC, chan), jnp.float32),
                pltpu.VMEM((2, 2, TH, KC, chan), jnp.float32),
                dma((4,)),
                dma((2, 3)),
                dma,
                dma((12,)),
                dma((2 * TF,)),
                dma((2 * TF,)),
                dma((2,)),
                dma((2,)),
                dma((3,)),
                dma((3,)),
                dma((2,)),
                dma((2,)),
            ],
            compiler_params=pltpu.CompilerParams(
                collective_id=0, has_side_effects=True, vmem_limit_bytes=56 * 1024 * 1024
            ),
            name="decode",
        )(
            tokens,
            head_shift[None],
            head_scale[None],
            head_weight.T,
            head_bias,
            in_weight.reshape(in_rows, chan),
            in_bias,
            gain_one,
            weight_one.reshape(27, chan, chan),
            bias_one,
            gain_two,
            weight_two.reshape(27, chan, chan),
            bias_two,
        )
        return result

    in_specs = (P(("tm", "tile"), None), P(), P(), P(), P(), P(), P(), P(), P(), P(), P(), P(), P())
    out_specs = P("tm", "tile", None, None, None)
    return jax.shard_map(body, mesh=mesh, in_specs=in_specs, out_specs=out_specs, check_vma=False)
```

```python
import functools

import jax
import jax.numpy as jnp
from jax import lax
from jax.experimental import pallas as pl
from jax.experimental.pallas import tpu as pltpu
from jax.sharding import PartitionSpec as P

MESH = pl.DeviceIdType.MESH
TF = 4
TH = 4
KC = 32
EXT_F = TF + 2
EXT_R = TH + 2
ODD_BACK, EVEN, ODD, EVEN_ON = range(4)
ALL_ROWS = (0, 1, 2, 3)
ALL_TAPS = (0, 1, 2)

PIECES = {-1: (0, 1, 3), 0: (0, 3, 1), 1: (1, 4, 0), 2: (3, 4, 0), 3: (5, 3, 0), 4: (7, 1, 0)}


def body_kernel(
    tiles,
    blocks,
    tokens,
    shift_ref,
    scale_ref,
    head_w_ref,
    head_b_ref,
    in_w,
    in_b_ref,
    gain_one_ref,
    w_one,
    bias_one_ref,
    gain_two_ref,
    w_two,
    bias_two_ref,
    out_ref,
    tok,
    modulated,
    turned_w,
    affine,
    own,
    got,
    corner,
    w_in,
    w_corner,
    w1,
    w2,
    act_one,
    act_two,
    stream,
    third,
    acc,
    tok_sem,
    w_sem,
    in_sem,
    own_send,
    main_recv,
    side_recv,
    row_send,
    row_recv,
    tm_send,
    tm_recv,
    edge_send,
    edge_recv,
):
    me_m = lax.axis_index("tm")
    me_g = lax.axis_index("tile")
    chan = w1.shape[-1]
    depth = tok.shape[1]
    i32 = jnp.int32

    def at(m, g):
        return {"tm": m, "tile": g}

    def row_of(ref):
        return ref[...].reshape(1, ref.shape[0])

    tok_rows = tok.shape[0] // 4
    tok_copies = [
        pltpu.make_async_copy(
            tokens.at[pl.ds(i * tok_rows, tok_rows)],
            tok.at[pl.ds(i * tok_rows, tok_rows)],
            tok_sem.at[i],
        )
        for i in range(4)
    ]
    in_copy = pltpu.make_async_copy(in_w, w_in, in_sem)
    w_copies = [
        [
            pltpu.make_async_copy(src.at[pl.ds(9 * a, 9)], dst.at[pl.ds(9 * a, 9)], w_sem.at[n, a])
            for a in range(3)
        ]
        for n, (src, dst) in enumerate(((w_one, w1), (w_two, w2)))
    ]
    for copy in tok_copies:
        copy.start()
    in_copy.start()

    frame = lax.div(me_g, tiles // TF)
    part = lax.rem(me_g, tiles // TF)
    home = lax.div(me_g, 4)
    place = lax.rem(me_g, 4)

    def target(dm, d):
        g = 4 * part + d
        m = me_m + dm
        inside = (g >= 0) & (g < tiles) & (m < blocks)
        remote = inside if dm else inside & (g != me_g)
        return m, g, remote

    def source(slot, side):
        m = me_m if slot >= TF else me_m - 1
        other = home + jnp.where(place == 0, -1, 1) if side else home
        g = (slot % TF) * (tiles // TF) + other
        inside = m >= 0
        if side:
            inside = (
                inside
                & ((place == 0) | (place == 3))
                & (other >= 0)
                & (other < tiles // TF)
            )
        remote = inside & (g != me_g) if slot >= TF else inside
        return m, g, remote

    has_up = me_g > 0
    has_down = me_g < tiles - 1
    has_prev = me_m > 0
    has_next = me_m < blocks - 1
    sends_edges = has_next & (lax.rem(me_m, 2) == 1)
    passes_edges = has_next & (lax.rem(me_m, 2) == 0)
    gets_edges = has_prev & (lax.rem(me_m, 2) == 0)

    barrier = pltpu.get_barrier_semaphore()

    def greet(m, g, here):
        @pl.when(here)
        def _():
            pl.semaphore_signal(barrier, inc=1, device_id=at(m, g), device_id_type=MESH)

    for slot in range(2 * TF):
        for side in range(2):
            greet(*source(slot, side))
    greet(me_m, me_g - 1, has_up)
    greet(me_m, me_g + 1, has_down)
    greet(me_m - 1, me_g, has_prev)
    greet(me_m - 1, me_g - 1, gets_edges & has_up)
    greet(me_m - 1, me_g + 1, gets_edges & has_down)

    zero_patch = jnp.zeros(got.shape[2:], jnp.bfloat16)

    @pl.when(jnp.logical_not(has_prev))
    def _():
        for slot in range(TF):
            for pair in range(4):
                got[slot, pair] = zero_patch
        for version in range(4):
            for row in range(EXT_R):
                for f in range(2):
                    act_two[version, f, row] = jnp.zeros((KC, chan), jnp.bfloat16)

    @pl.when(jnp.logical_not(has_up))
    def _():
        for slot in range(2 * TF):
            got[slot, 0] = zero_patch
        for version in range(4):
            for f in range(EXT_F):
                act_two[version, f, 0] = jnp.zeros((KC, chan), jnp.bfloat16)

    @pl.when(jnp.logical_not(has_down))
    def _():
        for slot in range(2 * TF):
            got[slot, 3] = zero_patch
        for version in range(4):
            for f in range(EXT_F):
                act_two[version, f, EXT_R - 1] = jnp.zeros((KC, chan), jnp.bfloat16)

    lanes = 128

    head_w = head_w_ref[...]
    turned_w[...] = jnp.concatenate([head_w, head_w], axis=0).T
    affine[0] = jnp.broadcast_to(1.0 + scale_ref[...], affine.shape[1:])
    affine[1] = jnp.broadcast_to(shift_ref[...], affine.shape[1:])

    def head_rows(i, carry):
        rows = pl.ds(pl.multiple_of(i * 16, 16), 16)

        def piece(j):
            return tok[rows, j * lanes : (j + 1) * lanes].astype(jnp.float32)

        base = piece(0)[:, :1]
        sums = [jnp.zeros((16, lanes), jnp.float32)] * 2
        squares = [jnp.zeros((16, lanes), jnp.float32)] * 2
        for j in range(depth // lanes):
            away = piece(j) - base
            sums[j % 2] = sums[j % 2] + away
            squares[j % 2] = squares[j % 2] + away * away
        offset = jnp.sum(sums[0] + sums[1], axis=-1, keepdims=True) * (1.0 / depth)
        second = jnp.sum(squares[0] + squares[1], axis=-1, keepdims=True) * (1.0 / depth)
        average = base + offset
        factor = lax.rsqrt(jnp.maximum(second - offset * offset, 0.0) + 1e-06)
        for j in range(depth // lanes):
            part = pl.ds(j * lanes, lanes)
            normed = (piece(j) - average) * factor * affine[0, :, part] + affine[1, :, part]
            modulated[rows, part] = normed.astype(jnp.bfloat16)
        return carry

    for i in range(4):
        tok_copies[i].wait()
        if i == 3:
            for copy in w_copies[0]:
                copy.start()
        blocks_of = tok_rows // 16
        lax.fori_loop(i * blocks_of, (i + 1) * blocks_of, head_rows, 0, unroll=min(4, blocks_of))
    patches = jnp.dot(modulated[...], turned_w[...], preferred_element_type=jnp.float32)
    head_b = jnp.concatenate([row_of(head_b_ref)] * 2, axis=1)
    spread = (patches + head_b).reshape(own.shape[0], KC, own.shape[2])
    wide_left = lax.broadcasted_iota(i32, own.shape, 2) < own.shape[2] // 2
    own[...] = jnp.where(wide_left, spread[:, : KC // 2], spread[:, KC // 2 :]).astype(jnp.bfloat16)

    def patch_copy(n, dm, d):
        m, g, remote = target(dm, d)
        first, count, slot = PIECES[d]
        return remote, pltpu.make_async_remote_copy(
            src_ref=own.at[pl.ds(first, count)],
            dst_ref=got.at[(0 if dm else TF) + frame, pl.ds(slot, count)],
            send_sem=own_send.at[n],
            recv_sem=(side_recv if d in (-1, 4) else main_recv).at[(0 if dm else TF) + frame],
            device_id=at(m, g),
            device_id_type=MESH,
        )

    sends = [(dm, d) for dm in (1, 0) for d in PIECES]
    count = i32(0)
    for dm, d in sends:
        count = count + target(dm, d)[2].astype(i32)
    for here in (has_up, has_down, has_next, sends_edges & has_up, sends_edges & has_down):
        count = count + here.astype(i32)
    pl.semaphore_wait(barrier, count)

    for n, (dm, d) in enumerate(sends):
        remote, copy = patch_copy(n, dm, d)

        @pl.when(remote)
        def _(copy=copy):
            copy.start()

    for d, (first, size, slot) in PIECES.items():

        @pl.when(4 * part + d == me_g)
        def _(first=first, size=size, slot=slot):
            got[TF + frame, pl.ds(slot, size)] = own[pl.ds(first, size)]

    in_copy.wait()
    w_corner[...] = jnp.zeros(w_corner.shape, jnp.bfloat16)
    for a in range(3):
        for parity, middle in ((0, 2), (1, 1)):
            for cell in range(2):
                for s in range(3):
                    for u in range(3):
                        row = s + cell
                        col = u + middle - 1
                        at_k = (row // 2) * 128 + (col // 2) * 64 + (row % 2) * 32 + (col % 2) * 16
                        at_n = (2 * parity + cell) * chan
                        w_corner[a, pl.ds(at_k, 16), pl.ds(at_n, chan)] = w_in[
                            pl.ds(((a * 3 + u) * 3 + s) * 16, 16), :
                        ]

    for slot in range(2 * TF):
        for side in range(2):
            m, g, remote = source(slot, side)
            for d, (first, size, first_slot) in PIECES.items():
                if (d in (-1, 4)) != bool(side):
                    continue
                which = place == d % 4

                @pl.when(remote & which)
                def _(slot=slot, m=m, g=g, first=first, size=size, first_slot=first_slot, side=side):
                    pltpu.make_async_remote_copy(
                        src_ref=own.at[pl.ds(first, size)],
                        dst_ref=got.at[slot, pl.ds(first_slot, size)],
                        send_sem=own_send.at[0],
                        recv_sem=(side_recv if side else main_recv).at[slot],
                        device_id=at(m, g),
                        device_id_type=MESH,
                    ).wait_recv()

    width = got.shape[-1]
    packed = got[...].astype(jnp.float32).reshape(2 * TF * 4, KC // 2, width)
    turned = pltpu.roll(packed.reshape(-1, width), width // 2, 1).reshape(packed.shape)
    low = lax.broadcasted_iota(i32, packed.shape, 2) < width // 2
    flat = jnp.concatenate(
        [jnp.where(low, packed, turned), jnp.where(low, turned, packed)], axis=1
    ).reshape(2 * TF * 4 * KC, width)
    lane = lax.broadcasted_iota(i32, flat.shape, 1)
    pair_col = lax.rem(lax.broadcasted_iota(i32, flat.shape, 0), KC)
    back = jnp.where(pair_col == 0, 0.0, pltpu.roll(flat, 1, 0))
    on = jnp.where(pair_col == KC - 1, 0.0, pltpu.roll(flat, flat.shape[0] - 1, 0))
    left = lane < width // 2
    corner[0] = jnp.where(left, back, flat).astype(jnp.bfloat16).reshape(corner.shape[1:])
    corner[1] = jnp.where(left, flat, on).astype(jnp.bfloat16).reshape(corner.shape[1:])


    def normed_silu(values, gain, keep=None):
        factor = lax.rsqrt(jnp.sum(values * values, axis=-1, keepdims=True) * (1.0 / chan) + 1e-06)
        if keep is not None:
            factor = factor * keep
        half = values * factor * gain
        return half + half * jnp.tanh(half)

    first_eight = lax.broadcasted_iota(i32, (8, chan), 0)

    def moved_on(act):
        moved = pltpu.roll(act, KC - 1, 0)
        last = jnp.where(first_eight == 7, 0.0, moved[KC - 8 :])
        return jnp.concatenate([moved[: KC - 8], last], axis=0)

    def moved_back(act):
        moved = pltpu.roll(act, 1, 0)
        return jnp.concatenate([jnp.where(first_eight == 0, 0.0, moved[:8]), moved[8:]], axis=0)

    def store_act(ref, f, row, parity, act):
        if parity == 0:
            ref[EVEN, f, row] = act.astype(jnp.bfloat16)
            ref[EVEN_ON, f, row] = moved_on(act).astype(jnp.bfloat16)
        else:
            ref[ODD, f, row] = act.astype(jnp.bfloat16)
            ref[ODD_BACK, f, row] = moved_back(act).astype(jnp.bfloat16)

    gain_one = row_of(gain_one_ref) * 0.5
    in_bias = jnp.concatenate([row_of(in_b_ref)] * 2, axis=1)
    top_keep = has_up.astype(jnp.float32)
    bottom_keep = has_down.astype(jnp.float32)
    prev_keep = has_prev.astype(jnp.float32)

    def input_product(ci, parity):
        taps = [
            corner[parity, a : a + EXT_F, ci + di].reshape(EXT_F * KC, width)
            for a in range(3)
            for di in range(2)
        ]
        raw = jnp.dot(
            jnp.concatenate(taps, axis=1),
            w_corner[:, :, 2 * chan * parity : 2 * chan * (parity + 1)].reshape(
                6 * width, 2 * chan
            ),
            preferred_element_type=jnp.float32,
        )
        return (raw + in_bias).reshape(EXT_F, KC, 2 * chan)

    def input_act(row, parity, values):
        for f in range(EXT_F):
            if f >= 2 and 1 <= row <= TH:
                stream[parity, f - 2, row - 1] = values[f].astype(jnp.bfloat16)
            keep = prev_keep if f < 2 else None
            for edge, edge_keep in ((0, top_keep), (EXT_R - 1, bottom_keep)):
                if row == edge:
                    keep = edge_keep if keep is None else keep * edge_keep
            store_act(act_one, f, row, parity, normed_silu(values[f], gain_one, keep))

    raws = [input_product(0, parity) for parity in range(2)]
    for parity in range(2):
        for cell in range(2):
            input_act(cell, parity, raws[parity][:, :, cell * chan : (cell + 1) * chan])
        raw = input_product(1, parity)
        third[parity] = raw[:, :, chan:]
        raws.append(raw)
    for parity in range(2):
        input_act(2, parity, raws[2 + parity][:, :, :chan])

    def last_rows(parity):
        raw = input_product(2, parity)
        for cell in range(2):
            input_act(4 + cell, parity, raw[:, :, cell * chan : (cell + 1) * chan])

    rest_of_input = (
        lambda: input_act(3, 0, third[0]),
        lambda: input_act(3, 1, third[1]),
        lambda: last_rows(0),
        lambda: last_rows(1),
    )

    def tap(weight, a, u, s):
        return weight[a * 9 + u * 3 + s]

    def cells(field, version, frames, rows, s):
        if rows is ALL_ROWS:
            view = [field[version, f, s : s + TH] for f in frames]
        else:
            view = [field[version, f, v + s][None] for f in frames for v in rows]
        return jnp.concatenate(view, axis=0).reshape(len(frames) * len(rows) * KC, chan)

    def product(field, weight, groups, rows, taps, part=slice(None)):
        return jnp.dot(
            jnp.concatenate(
                [cells(field, version, frames, rows, s) for version, frames, _ in groups for s in taps],
                axis=1,
            ),
            jnp.concatenate(
                [
                    jnp.concatenate([tap(weight, a, u, s) for a, u in outs], axis=1)[:, part]
                    for _, _, outs in groups
                    for s in taps
                ],
                axis=0,
            ),
            preferred_element_type=jnp.float32,
        )

    def conv(field, weight, frames, rows, taps, paired, sides_first, beside=()):
        shape = (len(frames), len(rows), KC, chan)
        calls = iter(beside)

        def between():
            call = next(calls, None)
            if call is not None:
                call()

        def side(version, u):
            if paired:
                firsts = frames[0::2]
                half = (len(firsts), len(rows), KC, chan)
                two = product(
                    field,
                    weight,
                    [(version, [f + n for f in firsts], ((n, u), (n - 1, u))) for n in (1, 2)],
                    rows,
                    taps,
                )
                one = product(field, weight, [(version, firsts, ((0, u),))], rows, taps)
                other = product(
                    field, weight, [(version, [f + 3 for f in firsts], ((2, u),))], rows, taps
                )
                one = (one + two[:, :chan]).reshape(half)
                other = (other + two[:, chan:]).reshape(half)
                total = jnp.stack([one, other], axis=1)
            else:
                total = product(
                    field,
                    weight,
                    [(version, [f + a for f in frames], ((a, u),)) for a in range(3)],
                    rows,
                    taps,
                )
            between()
            return total.reshape(shape)

        def both(lanes):
            total = product(
                field,
                weight,
                [
                    (version, [f + a for f in frames], ((a, u + 1), (a, u)))
                    for a in range(3)
                    for version, u in ((EVEN, 0), (ODD, 1))
                ],
                rows,
                taps,
                lanes,
            )
            between()
            return total

        cut = 4 * chan // 3
        if sides_first:
            even = side(ODD_BACK, 0)
            odd = side(EVEN_ON, 2)
        low = both(slice(0, cut))
        if sides_first:
            yield low[:, :chan].reshape(shape) + even
        high = both(slice(cut, 2 * chan))
        if not sides_first:
            even = side(ODD_BACK, 0)
            yield low[:, :chan].reshape(shape) + even
            odd = side(EVEN_ON, 2)
        yield jnp.concatenate([low[:, chan:], high], axis=1).reshape(shape) + odd

    gain_two = row_of(gain_two_ref) * 0.5
    bias_one = row_of(bias_one_ref)
    bias_two = row_of(bias_two_ref)
    own_frames = list(range(TF))

    def act_two_rows(totals, rows):
        for parity, total in enumerate(totals):
            for f in range(TF):
                for i, v in enumerate(rows):
                    act = normed_silu(total[f, i] + bias_one, gain_two)
                    store_act(act_two, f + 2, v + 1, parity, act)

    def row_copy(way):
        frames = pl.ds(2, TF)
        return pltpu.make_async_remote_copy(
            src_ref=act_two.at[pl.ds(EVEN, 2), frames, 1 if way else TH],
            dst_ref=act_two.at[pl.ds(EVEN, 2), frames, EXT_R - 1 if way else 0],
            send_sem=row_send.at[way],
            recv_sem=row_recv.at[way],
            device_id=at(me_m, me_g - 1 if way else me_g + 1),
            device_id_type=MESH,
        )

    def edge_copy(way):
        return pltpu.make_async_remote_copy(
            src_ref=act_two.at[pl.ds(EVEN, 2), pl.ds(TF, 2), 1 if way else TH],
            dst_ref=act_two.at[pl.ds(EVEN, 2), pl.ds(0, 2), EXT_R - 1 if way else 0],
            send_sem=edge_send.at[way],
            recv_sem=edge_recv.at[way],
            device_id=at(me_m + 1, me_g - 1 if way else me_g + 1),
            device_id_type=MESH,
        )

    def pass_copy(way):
        row = EXT_R - 1 if way else 0
        return pltpu.make_async_remote_copy(
            src_ref=act_two.at[pl.ds(EVEN, 2), pl.ds(TF, 2), row],
            dst_ref=act_two.at[pl.ds(EVEN, 2), pl.ds(0, 2), row],
            send_sem=edge_send.at[way],
            recv_sem=edge_recv.at[way],
            device_id=at(me_m + 1, me_g),
            device_id_type=MESH,
        )

    tm_copy = pltpu.make_async_remote_copy(
        src_ref=act_two.at[pl.ds(EVEN, 2), pl.ds(TF, 2), pl.ds(1, TH)],
        dst_ref=act_two.at[pl.ds(EVEN, 2), pl.ds(0, 2), pl.ds(1, TH)],
        send_sem=tm_send.at[0],
        recv_sem=tm_recv.at[0],
        device_id=at(me_m + 1, me_g),
        device_id_type=MESH,
    )
    way_out = (has_down, has_up)
    way_in = (has_up, has_down)

    def widen(f, row):
        even = act_two[EVEN, f, row].astype(jnp.float32)
        act_two[EVEN_ON, f, row] = moved_on(even).astype(jnp.bfloat16)
        odd = act_two[ODD, f, row].astype(jnp.float32)
        act_two[ODD_BACK, f, row] = moved_back(odd).astype(jnp.bfloat16)

    for copy in w_copies[0]:
        copy.wait()
    for copy in w_copies[1]:
        copy.start()

    for row, way in ((0, 1), (TH - 1, 0)):
        beside = rest_of_input if row == 0 else ()
        act_two_rows(
            conv(act_one, w1, own_frames, (row,), ALL_TAPS, False, True, beside), (row,)
        )

        @pl.when(way_out[way])
        def _(way=way):
            row_copy(way).start()

        @pl.when(way_out[way] & sends_edges)
        def _(way=way):
            edge_copy(way).start()

    act_two_rows(conv(act_one, w1, own_frames, (1, 2), ALL_TAPS, True, True), (1, 2))

    @pl.when(has_next)
    def _():
        tm_copy.start()

    for copy in w_copies[1]:
        copy.wait()

    for parity, total in enumerate(conv(act_two, w2, [2, 3], ALL_ROWS, (1,), True, True)):
        acc[parity] = total + bias_two

    for way in range(2):

        @pl.when(way_in[way])
        def _(way=way):
            row_copy(way).wait_recv()

        @pl.when(way_in[way] & passes_edges)
        def _(way=way):
            pass_copy(way).start()

    for row in (0, EXT_R - 1):
        for f in range(2, EXT_F):
            widen(f, row)

    for parity, total in enumerate(conv(act_two, w2, [2, 3], ALL_ROWS, (0, 2), True, False)):
        acc[parity] += total

    @pl.when(has_prev)
    def _():
        tm_copy.wait_recv()

    for way in range(2):

        @pl.when(way_in[way] & has_prev)
        def _(way=way):
            edge_copy(way).wait_recv()

    for f in range(2):
        for row in range(EXT_R):
            widen(f, row)

    area = 2 * TH * KC
    to = lax.broadcasted_iota(i32, (area, area), 0)
    of = lax.broadcasted_iota(i32, (area, area), 1)
    order = jnp.where(
        (lax.div(to, 8) == lax.rem(of, KC)) & (lax.rem(to, 8) == lax.div(of, KC)), 1.0, 0.0
    ).astype(jnp.bfloat16)

    def finish(f, totals):
        halves = [
            (totals[p] + stream[p, f].astype(jnp.float32))
            .astype(jnp.bfloat16)
            .reshape(TH * KC, chan)
            for p in range(2)
        ]
        placed = jnp.dot(
            order, jnp.concatenate(halves, axis=0), preferred_element_type=jnp.float32
        )
        out_ref[f, 0] = placed.reshape(2 * KC, TH, chan).astype(jnp.bfloat16)

    done = [lambda f=f: finish(2 + f, [acc[p, f] for p in range(2)]) for f in range(2)]
    totals = list(conv(act_two, w2, [0, 1], ALL_ROWS, ALL_TAPS, True, False, done))
    for f in range(2):
        finish(f, [totals[p][f] + bias_two for p in range(2)])

    for n, (dm, d) in enumerate(sends):
        remote, copy = patch_copy(n, dm, d)

        @pl.when(remote)
        def _(copy=copy):
            copy.wait_send()

    @pl.when(has_next)
    def _():
        tm_copy.wait_send()

    for way in range(2):

        @pl.when(way_out[way])
        def _(way=way):
            row_copy(way).wait_send()

        @pl.when(way_out[way] & sends_edges)
        def _(way=way):
            edge_copy(way).wait_send()

        @pl.when(way_in[way] & passes_edges)
        def _(way=way):
            pass_copy(way).wait_send()


def solution(mesh):
    tiles = mesh.shape["tile"]
    blocks = mesh.shape["tm"]

    def body(
        tokens,
        head_shift,
        head_scale,
        head_weight,
        head_bias,
        in_weight,
        in_bias,
        gain_one,
        weight_one,
        bias_one,
        gain_two,
        weight_two,
        bias_two,
    ):
        count, depth = tokens.shape
        chan = weight_one.shape[-1]
        wide = 2 * head_weight.shape[1]
        in_rows = in_weight.shape[0] * in_weight.shape[1] * in_weight.shape[2] * in_weight.shape[3]
        bf16 = jnp.bfloat16
        hbm = pl.BlockSpec(memory_space=pl.ANY)
        vmem = pl.BlockSpec(memory_space=pltpu.VMEM)
        dma = pltpu.SemaphoreType.DMA
        result = pl.pallas_call(
            functools.partial(body_kernel, tiles, blocks),
            out_shape=pltpu.VMEM((TF, 1, 2 * KC, TH, chan), bf16),
            in_specs=[
                hbm, vmem, vmem, vmem, vmem, hbm, vmem, vmem, hbm, vmem, vmem, hbm, vmem,
            ],
            out_specs=vmem,
            scratch_shapes=[
                pltpu.VMEM((count, depth), bf16),
                pltpu.VMEM((count, depth), bf16),
                pltpu.VMEM((depth, wide), bf16),
                pltpu.VMEM((2, 16, depth), jnp.float32),
                pltpu.VMEM((count // KC, KC // 2, wide), bf16),
                pltpu.VMEM((2 * TF, 4, KC // 2, wide), bf16),
                pltpu.VMEM((2, 2 * TF, 4, KC, wide), bf16),
                pltpu.VMEM((in_rows, chan), bf16),
                pltpu.VMEM((3, 2 * wide, 4 * chan), bf16),
                pltpu.VMEM((27, chan, chan), bf16),
                pltpu.VMEM((27, chan, chan), bf16),
                pltpu.VMEM((4, EXT_F, EXT_R, KC, chan), bf16),
                pltpu.VMEM((4, EXT_F, EXT_R, KC, chan), bf16),
                pltpu.VMEM((2, TF, TH, KC, chan), bf16),
                pltpu.VMEM((2, EXT_F, KC, chan), jnp.float32),
                pltpu.VMEM((2, 2, TH, KC, chan), jnp.float32),
                dma((4,)),
                dma((2, 3)),
                dma,
                dma((12,)),
                dma((2 * TF,)),
                dma((2 * TF,)),
                dma((2,)),
                dma((2,)),
                dma((1,)),
                dma((1,)),
                dma((2,)),
                dma((2,)),
            ],
            compiler_params=pltpu.CompilerParams(
                collective_id=0, has_side_effects=True, vmem_limit_bytes=56 * 1024 * 1024
            ),
            name="decode",
        )(
            tokens,
            head_shift[None],
            head_scale[None],
            head_weight.T,
            head_bias,
            in_weight.reshape(in_rows, chan),
            in_bias,
            gain_one,
            weight_one.reshape(27, chan, chan),
            bias_one,
            gain_two,
            weight_two.reshape(27, chan, chan),
            bias_two,
        )
        return result

    in_specs = (P(("tm", "tile"), None), P(), P(), P(), P(), P(), P(), P(), P(), P(), P(), P(), P())
    out_specs = P("tm", "tile", None, None, None)
    return jax.shard_map(body, mesh=mesh, in_specs=in_specs, out_specs=out_specs, check_vma=False)
```

```python
import functools

import jax
import jax.numpy as jnp
from jax import lax
from jax.experimental import pallas as pl
from jax.experimental.pallas import tpu as pltpu
from jax.sharding import PartitionSpec as P

MESH = pl.DeviceIdType.MESH
TF = 4
TH = 4
KC = 32
EXT_F = TF + 2
EXT_R = TH + 2
ODD_BACK, EVEN, ODD, EVEN_ON = range(4)
ALL_ROWS = (0, 1, 2, 3)
ALL_TAPS = (0, 1, 2)

PIECES = {-1: (0, 1, 3), 0: (0, 3, 1), 1: (1, 4, 0), 2: (3, 4, 0), 3: (5, 3, 0), 4: (7, 1, 0)}


def body_kernel(
    tiles,
    blocks,
    tokens,
    shift_ref,
    scale_ref,
    head_w_ref,
    head_b_ref,
    in_w,
    in_b_ref,
    gain_one_ref,
    w_one,
    bias_one_ref,
    gain_two_ref,
    w_two,
    bias_two_ref,
    out_ref,
    tok,
    modulated,
    turned_w,
    affine,
    own,
    got,
    corner,
    w_in,
    w_corner,
    w1,
    w2,
    act_one,
    act_two,
    stream,
    third,
    acc,
    tok_sem,
    w_sem,
    in_sem,
    own_send,
    main_recv,
    side_recv,
    row_send,
    row_recv,
    tm_send,
    tm_recv,
    edge_send,
    edge_recv,
):
    me_m = lax.axis_index("tm")
    me_g = lax.axis_index("tile")
    chan = w1.shape[-1]
    depth = tok.shape[1]
    i32 = jnp.int32

    def at(m, g):
        return {"tm": m, "tile": g}

    def row_of(ref):
        return ref[...].reshape(1, ref.shape[0])

    tok_rows = tok.shape[0] // 4
    tok_copies = [
        pltpu.make_async_copy(
            tokens.at[pl.ds(i * tok_rows, tok_rows)],
            tok.at[pl.ds(i * tok_rows, tok_rows)],
            tok_sem.at[i],
        )
        for i in range(4)
    ]
    in_copy = pltpu.make_async_copy(in_w, w_in, in_sem)
    w_copies = [
        [
            pltpu.make_async_copy(src.at[pl.ds(9 * a, 9)], dst.at[pl.ds(9 * a, 9)], w_sem.at[n, a])
            for a in range(3)
        ]
        for n, (src, dst) in enumerate(((w_one, w1), (w_two, w2)))
    ]
    for copy in tok_copies:
        copy.start()
    in_copy.start()

    frame = lax.div(me_g, tiles // TF)
    part = lax.rem(me_g, tiles // TF)
    home = lax.div(me_g, 4)
    place = lax.rem(me_g, 4)

    def target(dm, d):
        g = 4 * part + d
        m = me_m + dm
        inside = (g >= 0) & (g < tiles) & (m < blocks)
        remote = inside if dm else inside & (g != me_g)
        return m, g, remote

    def source(slot, side):
        m = me_m if slot >= TF else me_m - 1
        other = home + jnp.where(place == 0, -1, 1) if side else home
        g = (slot % TF) * (tiles // TF) + other
        inside = m >= 0
        if side:
            inside = (
                inside
                & ((place == 0) | (place == 3))
                & (other >= 0)
                & (other < tiles // TF)
            )
        remote = inside & (g != me_g) if slot >= TF else inside
        return m, g, remote

    has_up = me_g > 0
    has_down = me_g < tiles - 1
    has_prev = me_m > 0
    has_next = me_m < blocks - 1
    sends_edges = has_next & (lax.rem(me_m, 2) == 1)
    passes_edges = has_next & (lax.rem(me_m, 2) == 0)
    gets_edges = has_prev & (lax.rem(me_m, 2) == 0)

    barrier = pltpu.get_barrier_semaphore()

    def greet(m, g, here):
        @pl.when(here)
        def _():
            pl.semaphore_signal(barrier, inc=1, device_id=at(m, g), device_id_type=MESH)

    for slot in range(2 * TF):
        for side in range(2):
            greet(*source(slot, side))
    greet(me_m, me_g - 1, has_up)
    greet(me_m, me_g + 1, has_down)
    greet(me_m - 1, me_g, has_prev)
    greet(me_m - 1, me_g - 1, gets_edges & has_up)
    greet(me_m - 1, me_g + 1, gets_edges & has_down)

    zero_patch = jnp.zeros(got.shape[2:], jnp.bfloat16)

    @pl.when(jnp.logical_not(has_prev))
    def _():
        for slot in range(TF):
            for pair in range(4):
                got[slot, pair] = zero_patch
        for version in range(4):
            for row in range(EXT_R):
                for f in range(2):
                    act_two[version, f, row] = jnp.zeros((KC, chan), jnp.bfloat16)

    @pl.when(jnp.logical_not(has_up))
    def _():
        for slot in range(2 * TF):
            got[slot, 0] = zero_patch
        for version in range(4):
            for f in range(EXT_F):
                act_two[version, f, 0] = jnp.zeros((KC, chan), jnp.bfloat16)

    @pl.when(jnp.logical_not(has_down))
    def _():
        for slot in range(2 * TF):
            got[slot, 3] = zero_patch
        for version in range(4):
            for f in range(EXT_F):
                act_two[version, f, EXT_R - 1] = jnp.zeros((KC, chan), jnp.bfloat16)

    lanes = 128

    head_w = head_w_ref[...]
    turned_w[...] = jnp.concatenate([head_w, head_w], axis=0).T
    affine[0] = jnp.broadcast_to(1.0 + scale_ref[...], affine.shape[1:])
    affine[1] = jnp.broadcast_to(shift_ref[...], affine.shape[1:])

    def head_rows(i, carry):
        rows = pl.ds(pl.multiple_of(i * 16, 16), 16)

        def piece(j):
            return tok[rows, j * lanes : (j + 1) * lanes].astype(jnp.float32)

        base = piece(0)[:, :1]
        sums = [jnp.zeros((16, lanes), jnp.float32)] * 2
        squares = [jnp.zeros((16, lanes), jnp.float32)] * 2
        for j in range(depth // lanes):
            away = piece(j) - base
            sums[j % 2] = sums[j % 2] + away
            squares[j % 2] = squares[j % 2] + away * away
        offset = jnp.sum(sums[0] + sums[1], axis=-1, keepdims=True) * (1.0 / depth)
        second = jnp.sum(squares[0] + squares[1], axis=-1, keepdims=True) * (1.0 / depth)
        average = base + offset
        factor = lax.rsqrt(jnp.maximum(second - offset * offset, 0.0) + 1e-06)
        for j in range(depth // lanes):
            part = pl.ds(j * lanes, lanes)
            normed = (piece(j) - average) * factor * affine[0, :, part] + affine[1, :, part]
            modulated[rows, part] = normed.astype(jnp.bfloat16)
        return carry

    for i in range(4):
        tok_copies[i].wait()
        if i == 3:
            for copy in w_copies[0]:
                copy.start()
        blocks_of = tok_rows // 16
        lax.fori_loop(i * blocks_of, (i + 1) * blocks_of, head_rows, 0, unroll=min(4, blocks_of))
    patches = jnp.dot(modulated[...], turned_w[...], preferred_element_type=jnp.float32)
    head_b = jnp.concatenate([row_of(head_b_ref)] * 2, axis=1)
    spread = (patches + head_b).reshape(own.shape[0], KC, own.shape[2])
    wide_left = lax.broadcasted_iota(i32, own.shape, 2) < own.shape[2] // 2
    own[...] = jnp.where(wide_left, spread[:, : KC // 2], spread[:, KC // 2 :]).astype(jnp.bfloat16)

    def patch_copy(n, dm, d):
        m, g, remote = target(dm, d)
        first, count, slot = PIECES[d]
        return remote, pltpu.make_async_remote_copy(
            src_ref=own.at[pl.ds(first, count)],
            dst_ref=got.at[(0 if dm else TF) + frame, pl.ds(slot, count)],
            send_sem=own_send.at[n],
            recv_sem=(side_recv if d in (-1, 4) else main_recv).at[(0 if dm else TF) + frame],
            device_id=at(m, g),
            device_id_type=MESH,
        )

    sends = [(dm, d) for dm in (1, 0) for d in PIECES]
    count = i32(0)
    for dm, d in sends:
        count = count + target(dm, d)[2].astype(i32)
    for here in (has_up, has_down, has_next, sends_edges & has_up, sends_edges & has_down):
        count = count + here.astype(i32)
    pl.semaphore_wait(barrier, count)

    for n, (dm, d) in enumerate(sends):
        remote, copy = patch_copy(n, dm, d)

        @pl.when(remote)
        def _(copy=copy):
            copy.start()

    for d, (first, size, slot) in PIECES.items():

        @pl.when(4 * part + d == me_g)
        def _(first=first, size=size, slot=slot):
            got[TF + frame, pl.ds(slot, size)] = own[pl.ds(first, size)]

    in_copy.wait()
    w_corner[...] = jnp.zeros(w_corner.shape, jnp.bfloat16)
    for a in range(3):
        for parity, middle in ((0, 2), (1, 1)):
            for cell in range(2):
                for s in range(3):
                    for u in range(3):
                        row = s + cell
                        col = u + middle - 1
                        at_k = (row // 2) * 128 + (col // 2) * 64 + (row % 2) * 32 + (col % 2) * 16
                        at_n = (2 * parity + cell) * chan
                        w_corner[a, pl.ds(at_k, 16), pl.ds(at_n, chan)] = w_in[
                            pl.ds(((a * 3 + u) * 3 + s) * 16, 16), :
                        ]

    for slot in range(2 * TF):
        for side in range(2):
            m, g, remote = source(slot, side)
            for d, (first, size, first_slot) in PIECES.items():
                if (d in (-1, 4)) != bool(side):
                    continue
                which = place == d % 4

                @pl.when(remote & which)
                def _(slot=slot, m=m, g=g, first=first, size=size, first_slot=first_slot, side=side):
                    pltpu.make_async_remote_copy(
                        src_ref=own.at[pl.ds(first, size)],
                        dst_ref=got.at[slot, pl.ds(first_slot, size)],
                        send_sem=own_send.at[0],
                        recv_sem=(side_recv if side else main_recv).at[slot],
                        device_id=at(m, g),
                        device_id_type=MESH,
                    ).wait_recv()

    width = got.shape[-1]
    packed = got[...].astype(jnp.float32).reshape(2 * TF * 4, KC // 2, width)
    turned = pltpu.roll(packed.reshape(-1, width), width // 2, 1).reshape(packed.shape)
    low = lax.broadcasted_iota(i32, packed.shape, 2) < width // 2
    flat = jnp.concatenate(
        [jnp.where(low, packed, turned), jnp.where(low, turned, packed)], axis=1
    ).reshape(2 * TF * 4 * KC, width)
    lane = lax.broadcasted_iota(i32, flat.shape, 1)
    pair_col = lax.rem(lax.broadcasted_iota(i32, flat.shape, 0), KC)
    back = jnp.where(pair_col == 0, 0.0, pltpu.roll(flat, 1, 0))
    on = jnp.where(pair_col == KC - 1, 0.0, pltpu.roll(flat, flat.shape[0] - 1, 0))
    left = lane < width // 2
    corner[0] = jnp.where(left, back, flat).astype(jnp.bfloat16).reshape(corner.shape[1:])
    corner[1] = jnp.where(left, flat, on).astype(jnp.bfloat16).reshape(corner.shape[1:])


    def normed_silu(values, gain, keep=None):
        factor = lax.rsqrt(jnp.sum(values * values, axis=-1, keepdims=True) * (1.0 / chan) + 1e-06)
        if keep is not None:
            factor = factor * keep
        half = values * factor * gain
        return half + half * jnp.tanh(half)

    first_eight = lax.broadcasted_iota(i32, (8, chan), 0)

    def moved_on(act):
        moved = pltpu.roll(act, KC - 1, 0)
        last = jnp.where(first_eight == 7, 0.0, moved[KC - 8 :])
        return jnp.concatenate([moved[: KC - 8], last], axis=0)

    def moved_back(act):
        moved = pltpu.roll(act, 1, 0)
        return jnp.concatenate([jnp.where(first_eight == 0, 0.0, moved[:8]), moved[8:]], axis=0)

    def store_act(ref, f, row, parity, act):
        if parity == 0:
            ref[EVEN, f, row] = act.astype(jnp.bfloat16)
            ref[EVEN_ON, f, row] = moved_on(act).astype(jnp.bfloat16)
        else:
            ref[ODD, f, row] = act.astype(jnp.bfloat16)
            ref[ODD_BACK, f, row] = moved_back(act).astype(jnp.bfloat16)

    gain_one = row_of(gain_one_ref) * 0.5
    in_bias = jnp.concatenate([row_of(in_b_ref)] * 2, axis=1)
    top_keep = has_up.astype(jnp.float32)
    bottom_keep = has_down.astype(jnp.float32)
    prev_keep = has_prev.astype(jnp.float32)

    def input_product(ci, parity):
        taps = [
            corner[parity, a : a + EXT_F, ci + di].reshape(EXT_F * KC, width)
            for a in range(3)
            for di in range(2)
        ]
        raw = jnp.dot(
            jnp.concatenate(taps, axis=1),
            w_corner[:, :, 2 * chan * parity : 2 * chan * (parity + 1)].reshape(
                6 * width, 2 * chan
            ),
            preferred_element_type=jnp.float32,
        )
        return (raw + in_bias).reshape(EXT_F, KC, 2 * chan)

    def input_act(row, parity, values):
        for f in range(EXT_F):
            if f >= 2 and 1 <= row <= TH:
                stream[parity, f - 2, row - 1] = values[f].astype(jnp.bfloat16)
            keep = prev_keep if f < 2 else None
            for edge, edge_keep in ((0, top_keep), (EXT_R - 1, bottom_keep)):
                if row == edge:
                    keep = edge_keep if keep is None else keep * edge_keep
            store_act(act_one, f, row, parity, normed_silu(values[f], gain_one, keep))

    raws = [input_product(0, parity) for parity in range(2)]
    for parity in range(2):
        for cell in range(2):
            input_act(cell, parity, raws[parity][:, :, cell * chan : (cell + 1) * chan])
        raw = input_product(1, parity)
        third[parity] = raw[:, :, chan:]
        raws.append(raw)
    for parity in range(2):
        input_act(2, parity, raws[2 + parity][:, :, :chan])

    def last_rows(parity):
        raw = input_product(2, parity)
        for cell in range(2):
            input_act(4 + cell, parity, raw[:, :, cell * chan : (cell + 1) * chan])

    rest_of_input = (
        lambda: input_act(3, 0, third[0]),
        lambda: input_act(3, 1, third[1]),
        lambda: last_rows(0),
        lambda: last_rows(1),
    )

    def tap(weight, a, u, s):
        return weight[a * 9 + u * 3 + s]

    def cells(field, version, frames, rows, s):
        if rows is ALL_ROWS:
            view = [field[version, f, s : s + TH] for f in frames]
        else:
            view = [field[version, f, v + s][None] for f in frames for v in rows]
        return jnp.concatenate(view, axis=0).reshape(len(frames) * len(rows) * KC, chan)

    def product(field, weight, groups, rows, taps, part=slice(None)):
        return jnp.dot(
            jnp.concatenate(
                [cells(field, version, frames, rows, s) for version, frames, _ in groups for s in taps],
                axis=1,
            ),
            jnp.concatenate(
                [
                    jnp.concatenate([tap(weight, a, u, s) for a, u in outs], axis=1)[:, part]
                    for _, _, outs in groups
                    for s in taps
                ],
                axis=0,
            ),
            preferred_element_type=jnp.float32,
        )

    def conv(field, weight, frames, rows, taps, paired, sides_first, beside=()):
        shape = (len(frames), len(rows), KC, chan)
        calls = iter(beside)

        def between():
            call = next(calls, None)
            if call is not None:
                call()

        def side(version, u):
            if paired:
                firsts = frames[0::2]
                half = (len(firsts), len(rows), KC, chan)
                two = product(
                    field,
                    weight,
                    [(version, [f + n for f in firsts], ((n, u), (n - 1, u))) for n in (1, 2)],
                    rows,
                    taps,
                )
                one = product(field, weight, [(version, firsts, ((0, u),))], rows, taps)
                other = product(
                    field, weight, [(version, [f + 3 for f in firsts], ((2, u),))], rows, taps
                )
                one = (one + two[:, :chan]).reshape(half)
                other = (other + two[:, chan:]).reshape(half)
                total = jnp.stack([one, other], axis=1)
            else:
                total = product(
                    field,
                    weight,
                    [(version, [f + a for f in frames], ((a, u),)) for a in range(3)],
                    rows,
                    taps,
                )
            between()
            return total.reshape(shape)

        def both(lanes):
            total = product(
                field,
                weight,
                [
                    (version, [f + a for f in frames], ((a, u + 1), (a, u)))
                    for a in range(3)
                    for version, u in ((EVEN, 0), (ODD, 1))
                ],
                rows,
                taps,
                lanes,
            )
            between()
            return total

        cut = 4 * chan // 3
        if sides_first:
            even = side(ODD_BACK, 0)
            odd = side(EVEN_ON, 2)
        low = both(slice(0, cut))
        if sides_first:
            yield low[:, :chan].reshape(shape) + even
        high = both(slice(cut, 2 * chan))
        if not sides_first:
            even = side(ODD_BACK, 0)
            yield low[:, :chan].reshape(shape) + even
            odd = side(EVEN_ON, 2)
        yield jnp.concatenate([low[:, chan:], high], axis=1).reshape(shape) + odd

    gain_two = row_of(gain_two_ref) * 0.5
    bias_one = row_of(bias_one_ref)
    bias_two = row_of(bias_two_ref)
    own_frames = list(range(TF))

    def act_two_rows(totals, rows):
        for parity, total in enumerate(totals):
            for f in range(TF):
                for i, v in enumerate(rows):
                    act = normed_silu(total[f, i] + bias_one, gain_two)
                    store_act(act_two, f + 2, v + 1, parity, act)

    def row_copy(way):
        frames = pl.ds(2, TF)
        return pltpu.make_async_remote_copy(
            src_ref=act_two.at[pl.ds(EVEN, 2), frames, 1 if way else TH],
            dst_ref=act_two.at[pl.ds(EVEN, 2), frames, EXT_R - 1 if way else 0],
            send_sem=row_send.at[way],
            recv_sem=row_recv.at[way],
            device_id=at(me_m, me_g - 1 if way else me_g + 1),
            device_id_type=MESH,
        )

    def edge_copy(way):
        return pltpu.make_async_remote_copy(
            src_ref=act_two.at[pl.ds(EVEN, 2), pl.ds(TF, 2), 1 if way else TH],
            dst_ref=act_two.at[pl.ds(EVEN, 2), pl.ds(0, 2), EXT_R - 1 if way else 0],
            send_sem=edge_send.at[way],
            recv_sem=edge_recv.at[way],
            device_id=at(me_m + 1, me_g - 1 if way else me_g + 1),
            device_id_type=MESH,
        )

    def pass_copy(way):
        row = EXT_R - 1 if way else 0
        return pltpu.make_async_remote_copy(
            src_ref=act_two.at[pl.ds(EVEN, 2), pl.ds(TF, 2), row],
            dst_ref=act_two.at[pl.ds(EVEN, 2), pl.ds(0, 2), row],
            send_sem=edge_send.at[way],
            recv_sem=edge_recv.at[way],
            device_id=at(me_m + 1, me_g),
            device_id_type=MESH,
        )

    tm_copy = pltpu.make_async_remote_copy(
        src_ref=act_two.at[pl.ds(EVEN, 2), pl.ds(TF, 2), pl.ds(1, TH)],
        dst_ref=act_two.at[pl.ds(EVEN, 2), pl.ds(0, 2), pl.ds(1, TH)],
        send_sem=tm_send.at[0],
        recv_sem=tm_recv.at[0],
        device_id=at(me_m + 1, me_g),
        device_id_type=MESH,
    )
    way_out = (has_down, has_up)
    way_in = (has_up, has_down)

    def widen(f, row):
        even = act_two[EVEN, f, row].astype(jnp.float32)
        act_two[EVEN_ON, f, row] = moved_on(even).astype(jnp.bfloat16)
        odd = act_two[ODD, f, row].astype(jnp.float32)
        act_two[ODD_BACK, f, row] = moved_back(odd).astype(jnp.bfloat16)

    for copy in w_copies[0]:
        copy.wait()
    for copy in w_copies[1]:
        copy.start()

    for row, way in ((0, 1), (TH - 1, 0)):
        beside = rest_of_input if row == 0 else ()
        act_two_rows(
            conv(act_one, w1, own_frames, (row,), ALL_TAPS, False, True, beside), (row,)
        )

        @pl.when(way_out[way])
        def _(way=way):
            row_copy(way).start()

        @pl.when(way_out[way] & sends_edges)
        def _(way=way):
            edge_copy(way).start()

    act_two_rows(conv(act_one, w1, own_frames, (1, 2), ALL_TAPS, True, True), (1, 2))

    @pl.when(has_next)
    def _():
        tm_copy.start()

    for copy in w_copies[1]:
        copy.wait()

    def add(frames, rows, totals, fresh):
        for parity, total in enumerate(totals):
            for n, f in enumerate(frames):
                for i, v in enumerate(rows):
                    base = bias_two if fresh else acc[parity, f, v]
                    acc[parity, f, v] = base + total[n, i]

    def late_frames(rows, taps, sides_first):
        return conv(act_two, w2, [2, 3], rows, taps, False, sides_first)

    edge_rows = (0, TH - 1)
    add([2, 3], (1, 2), late_frames((1, 2), ALL_TAPS, True), True)
    add([2, 3], edge_rows, late_frames(edge_rows, (1,), True), True)

    for way in range(2):

        @pl.when(way_in[way])
        def _(way=way):
            row_copy(way).wait_recv()

        @pl.when(way_in[way] & passes_edges)
        def _(way=way):
            pass_copy(way).start()

    for row in (0, EXT_R - 1):
        for f in range(2, EXT_F):
            widen(f, row)

    add([2, 3], edge_rows, late_frames(edge_rows, (0, 2), False), False)

    def early_frames(own, beside):
        calls = iter(beside)
        full, one, one_out = ((2, [2, 3]), 2, 1) if own else ((0, [0, 1]), 1, 0)
        single, lone = (3, 2) if own else (0, 0)
        pair_taps = ((EVEN, 0), (ODD, 1))

        def pairs(time, frames):
            total = product(
                act_two,
                w2,
                [(version, frames, ((time, u + 1), (time, u))) for version, u in pair_taps],
                ALL_ROWS,
                ALL_TAPS,
            )
            call = next(calls, None)
            if call is not None:
                call()
            return total.reshape(len(frames), TH, KC, 2 * chan)

        whole = pairs(*full)
        part = pairs(1, [one])[0]
        shape = (TH, KC, chan)
        totals = []
        for p, (version, u) in enumerate(((ODD_BACK, 0), (EVEN_ON, 2))):
            times = ((2, u), (1, u)) if own else ((1, u), (0, u))
            two = product(act_two, w2, [(version, [one], times)], ALL_ROWS, ALL_TAPS)
            other = product(act_two, w2, [(version, [single], ((lone, u),))], ALL_ROWS, ALL_TAPS)
            lanes = slice(p * chan, (p + 1) * chan)
            sums = []
            for f in range(2):
                total = whole[f, :, :, lanes] + two[:, f * chan : (f + 1) * chan].reshape(shape)
                if f == one_out:
                    total = total + part[:, :, lanes] + other.reshape(shape)
                sums.append(total)
            totals.append(sums)
        return totals

    area = 2 * TH * KC
    to = lax.broadcasted_iota(i32, (area, area), 0)
    of = lax.broadcasted_iota(i32, (area, area), 1)
    order = jnp.where(
        (lax.div(to, 8) == lax.rem(of, KC)) & (lax.rem(to, 8) == lax.div(of, KC)), 1.0, 0.0
    ).astype(jnp.bfloat16)

    def finish(f, totals):
        halves = [
            (totals[p] + stream[p, f].astype(jnp.float32))
            .astype(jnp.bfloat16)
            .reshape(TH * KC, chan)
            for p in range(2)
        ]
        placed = jnp.dot(
            order, jnp.concatenate(halves, axis=0), preferred_element_type=jnp.float32
        )
        out_ref[f, 0] = placed.reshape(2 * KC, TH, chan).astype(jnp.bfloat16)

    done = [lambda f=f: finish(2 + f, [acc[p, 2 + f] for p in range(2)]) for f in range(2)]
    for parity, sums in enumerate(early_frames(True, done)):
        for f in range(2):
            acc[parity, f] = sums[f] + bias_two

    @pl.when(has_prev)
    def _():
        tm_copy.wait_recv()

    for way in range(2):

        @pl.when(way_in[way] & has_prev)
        def _(way=way):
            edge_copy(way).wait_recv()

    for f in range(2):
        for row in range(EXT_R):
            widen(f, row)

    totals = early_frames(False, ())
    for f in range(2):
        finish(f, [acc[p, f] + totals[p][f] for p in range(2)])

    for n, (dm, d) in enumerate(sends):
        remote, copy = patch_copy(n, dm, d)

        @pl.when(remote)
        def _(copy=copy):
            copy.wait_send()

    @pl.when(has_next)
    def _():
        tm_copy.wait_send()

    for way in range(2):

        @pl.when(way_out[way])
        def _(way=way):
            row_copy(way).wait_send()

        @pl.when(way_out[way] & sends_edges)
        def _(way=way):
            edge_copy(way).wait_send()

        @pl.when(way_in[way] & passes_edges)
        def _(way=way):
            pass_copy(way).wait_send()


def solution(mesh):
    tiles = mesh.shape["tile"]
    blocks = mesh.shape["tm"]

    def body(
        tokens,
        head_shift,
        head_scale,
        head_weight,
        head_bias,
        in_weight,
        in_bias,
        gain_one,
        weight_one,
        bias_one,
        gain_two,
        weight_two,
        bias_two,
    ):
        count, depth = tokens.shape
        chan = weight_one.shape[-1]
        wide = 2 * head_weight.shape[1]
        in_rows = in_weight.shape[0] * in_weight.shape[1] * in_weight.shape[2] * in_weight.shape[3]
        bf16 = jnp.bfloat16
        hbm = pl.BlockSpec(memory_space=pl.ANY)
        vmem = pl.BlockSpec(memory_space=pltpu.VMEM)
        dma = pltpu.SemaphoreType.DMA
        result = pl.pallas_call(
            functools.partial(body_kernel, tiles, blocks),
            out_shape=pltpu.VMEM((TF, 1, 2 * KC, TH, chan), bf16),
            in_specs=[
                hbm, vmem, vmem, vmem, vmem, hbm, vmem, vmem, hbm, vmem, vmem, hbm, vmem,
            ],
            out_specs=vmem,
            scratch_shapes=[
                pltpu.VMEM((count, depth), bf16),
                pltpu.VMEM((count, depth), bf16),
                pltpu.VMEM((depth, wide), bf16),
                pltpu.VMEM((2, 16, depth), jnp.float32),
                pltpu.VMEM((count // KC, KC // 2, wide), bf16),
                pltpu.VMEM((2 * TF, 4, KC // 2, wide), bf16),
                pltpu.VMEM((2, 2 * TF, 4, KC, wide), bf16),
                pltpu.VMEM((in_rows, chan), bf16),
                pltpu.VMEM((3, 2 * wide, 4 * chan), bf16),
                pltpu.VMEM((27, chan, chan), bf16),
                pltpu.VMEM((27, chan, chan), bf16),
                pltpu.VMEM((4, EXT_F, EXT_R, KC, chan), bf16),
                pltpu.VMEM((4, EXT_F, EXT_R, KC, chan), bf16),
                pltpu.VMEM((2, TF, TH, KC, chan), bf16),
                pltpu.VMEM((2, EXT_F, KC, chan), jnp.float32),
                pltpu.VMEM((2, TF, TH, KC, chan), jnp.float32),
                dma((4,)),
                dma((2, 3)),
                dma,
                dma((12,)),
                dma((2 * TF,)),
                dma((2 * TF,)),
                dma((2,)),
                dma((2,)),
                dma((1,)),
                dma((1,)),
                dma((2,)),
                dma((2,)),
            ],
            compiler_params=pltpu.CompilerParams(
                collective_id=0, has_side_effects=True, vmem_limit_bytes=56 * 1024 * 1024
            ),
            name="decode",
        )(
            tokens,
            head_shift[None],
            head_scale[None],
            head_weight.T,
            head_bias,
            in_weight.reshape(in_rows, chan),
            in_bias,
            gain_one,
            weight_one.reshape(27, chan, chan),
            bias_one,
            gain_two,
            weight_two.reshape(27, chan, chan),
            bias_two,
        )
        return result

    in_specs = (P(("tm", "tile"), None), P(), P(), P(), P(), P(), P(), P(), P(), P(), P(), P(), P())
    out_specs = P("tm", "tile", None, None, None)
    return jax.shard_map(body, mesh=mesh, in_specs=in_specs, out_specs=out_specs, check_vma=False)
```

```python
import functools

import jax
import jax.numpy as jnp
from jax import lax
from jax.experimental import pallas as pl
from jax.experimental.pallas import tpu as pltpu
from jax.sharding import PartitionSpec as P

MESH = pl.DeviceIdType.MESH
TF = 4
TH = 4
KC = 32
EXT_F = TF + 2
EXT_R = TH + 2
ODD_BACK, EVEN, ODD, EVEN_ON = range(4)
ALL_ROWS = (0, 1, 2, 3)
ALL_TAPS = (0, 1, 2)

PIECES = {-1: (0, 1, 3), 0: (0, 3, 1), 1: (1, 4, 0), 2: (3, 4, 0), 3: (5, 3, 0), 4: (7, 1, 0)}


def body_kernel(
    tiles,
    blocks,
    tokens,
    shift_ref,
    scale_ref,
    head_w_ref,
    head_b_ref,
    in_w,
    in_b_ref,
    gain_one_ref,
    w_one,
    bias_one_ref,
    gain_two_ref,
    w_two,
    bias_two_ref,
    out_ref,
    tok,
    modulated,
    turned_w,
    affine,
    own,
    got,
    corner,
    w_in,
    w_corner,
    w1,
    w2,
    act_one,
    act_two,
    stream,
    third,
    acc,
    tok_sem,
    w_sem,
    in_sem,
    own_send,
    main_recv,
    side_recv,
    row_send,
    row_recv,
    tm_send,
    tm_recv,
    edge_send,
    edge_recv,
):
    me_m = lax.axis_index("tm")
    me_g = lax.axis_index("tile")
    chan = w1.shape[-1]
    depth = tok.shape[1]
    i32 = jnp.int32

    def at(m, g):
        return {"tm": m, "tile": g}

    def row_of(ref):
        return ref[...].reshape(1, ref.shape[0])

    tok_parts = ((0, 2), (2, 5), (5, 8))
    tok_copies = [
        pltpu.make_async_copy(
            tokens.at[pl.ds(first * KC, (last - first) * KC)],
            tok.at[pl.ds(first * KC, (last - first) * KC)],
            tok_sem.at[i],
        )
        for i, (first, last) in enumerate(tok_parts)
    ]
    in_copy = pltpu.make_async_copy(in_w, w_in, in_sem)
    w_copies = [
        [
            pltpu.make_async_copy(src.at[pl.ds(9 * a, 9)], dst.at[pl.ds(9 * a, 9)], w_sem.at[n, a])
            for a in range(3)
        ]
        for n, (src, dst) in enumerate(((w_one, w1), (w_two, w2)))
    ]
    for copy in tok_copies:
        copy.start()
    in_copy.start()

    frame = lax.div(me_g, tiles // TF)
    part = lax.rem(me_g, tiles // TF)
    home = lax.div(me_g, 4)
    place = lax.rem(me_g, 4)

    def target(dm, d):
        g = 4 * part + d
        m = me_m + dm
        inside = (g >= 0) & (g < tiles) & (m < blocks)
        remote = inside if dm else inside & (g != me_g)
        return m, g, remote

    def source(slot, side):
        m = me_m if slot >= TF else me_m - 1
        other = home + jnp.where(place == 0, -1, 1) if side else home
        g = (slot % TF) * (tiles // TF) + other
        inside = m >= 0
        if side:
            inside = (
                inside
                & ((place == 0) | (place == 3))
                & (other >= 0)
                & (other < tiles // TF)
            )
        remote = inside & (g != me_g) if slot >= TF else inside
        return m, g, remote

    has_up = me_g > 0
    has_down = me_g < tiles - 1
    has_prev = me_m > 0
    has_next = me_m < blocks - 1
    sends_edges = has_next & (lax.rem(me_m, 2) == 1)
    passes_edges = has_next & (lax.rem(me_m, 2) == 0)
    gets_edges = has_prev & (lax.rem(me_m, 2) == 0)

    barrier = pltpu.get_barrier_semaphore()

    def greet(m, g, here):
        @pl.when(here)
        def _():
            pl.semaphore_signal(barrier, inc=1, device_id=at(m, g), device_id_type=MESH)

    for slot in range(2 * TF):
        for side in range(2):
            greet(*source(slot, side))
    greet(me_m, me_g - 1, has_up)
    greet(me_m, me_g + 1, has_down)
    greet(me_m - 1, me_g, has_prev)
    greet(me_m - 1, me_g - 1, gets_edges & has_up)
    greet(me_m - 1, me_g + 1, gets_edges & has_down)

    zero_patch = jnp.zeros(got.shape[2:], jnp.bfloat16)

    @pl.when(jnp.logical_not(has_prev))
    def _():
        for slot in range(TF):
            for pair in range(4):
                got[slot, pair] = zero_patch
        for version in range(4):
            for row in range(EXT_R):
                for f in range(2):
                    act_two[version, f, row] = jnp.zeros((KC, chan), jnp.bfloat16)

    @pl.when(jnp.logical_not(has_up))
    def _():
        for slot in range(2 * TF):
            got[slot, 0] = zero_patch
        for version in range(4):
            for f in range(EXT_F):
                act_two[version, f, 0] = jnp.zeros((KC, chan), jnp.bfloat16)

    @pl.when(jnp.logical_not(has_down))
    def _():
        for slot in range(2 * TF):
            got[slot, 3] = zero_patch
        for version in range(4):
            for f in range(EXT_F):
                act_two[version, f, EXT_R - 1] = jnp.zeros((KC, chan), jnp.bfloat16)

    lanes = 128

    head_w = head_w_ref[...]
    turned_w[...] = jnp.concatenate([head_w, head_w], axis=0).T
    affine[0] = jnp.broadcast_to(1.0 + scale_ref[...], affine.shape[1:])
    affine[1] = jnp.broadcast_to(shift_ref[...], affine.shape[1:])

    def head_rows(i, carry):
        rows = pl.ds(pl.multiple_of(i * 16, 16), 16)

        def piece(j):
            return tok[rows, j * lanes : (j + 1) * lanes].astype(jnp.float32)

        base = piece(0)[:, :1]
        sums = [jnp.zeros((16, lanes), jnp.float32)] * 2
        squares = [jnp.zeros((16, lanes), jnp.float32)] * 2
        for j in range(depth // lanes):
            away = piece(j) - base
            sums[j % 2] = sums[j % 2] + away
            squares[j % 2] = squares[j % 2] + away * away
        offset = jnp.sum(sums[0] + sums[1], axis=-1, keepdims=True) * (1.0 / depth)
        second = jnp.sum(squares[0] + squares[1], axis=-1, keepdims=True) * (1.0 / depth)
        average = base + offset
        factor = lax.rsqrt(jnp.maximum(second - offset * offset, 0.0) + 1e-06)
        for j in range(depth // lanes):
            part = pl.ds(j * lanes, lanes)
            normed = (piece(j) - average) * factor * affine[0, :, part] + affine[1, :, part]
            modulated[rows, part] = normed.astype(jnp.bfloat16)
        return carry

    head_b = jnp.concatenate([row_of(head_b_ref)] * 2, axis=1)

    def head_part(first, last):
        patches = jnp.dot(
            modulated[first * KC : last * KC, :],
            turned_w[...],
            preferred_element_type=jnp.float32,
        )
        spread = (patches + head_b).reshape(last - first, KC, own.shape[2])
        packed_shape = (last - first,) + own.shape[1:]
        wide_left = lax.broadcasted_iota(i32, packed_shape, 2) < own.shape[2] // 2
        own[first:last] = jnp.where(
            wide_left, spread[:, : KC // 2], spread[:, KC // 2 :]
        ).astype(jnp.bfloat16)

    def head_tokens(i):
        tok_copies[i].wait()
        if i == 2:
            for copy in w_copies[0]:
                copy.start()
        first, last = (n * KC // 16 for n in tok_parts[i])
        lax.fori_loop(first, last, head_rows, 0, unroll=(last - first) // 2)

    head_tokens(0)
    head_tokens(1)
    head_part(0, 5)

    def patch_copy(n, dm, d):
        m, g, remote = target(dm, d)
        first, count, slot = PIECES[d]
        return remote, pltpu.make_async_remote_copy(
            src_ref=own.at[pl.ds(first, count)],
            dst_ref=got.at[(0 if dm else TF) + frame, pl.ds(slot, count)],
            send_sem=own_send.at[n],
            recv_sem=(side_recv if d in (-1, 4) else main_recv).at[(0 if dm else TF) + frame],
            device_id=at(m, g),
            device_id_type=MESH,
        )

    sends = [(dm, d) for dm in (1, 0) for d in PIECES]
    count = i32(0)
    for dm, d in sends:
        count = count + target(dm, d)[2].astype(i32)
    for here in (has_up, has_down, has_next, sends_edges & has_up, sends_edges & has_down):
        count = count + here.astype(i32)
    pl.semaphore_wait(barrier, count)

    def send_patches(pieces):
        for n, (dm, d) in enumerate(sends):
            if d not in pieces:
                continue
            remote, copy = patch_copy(n, dm, d)

            @pl.when(remote)
            def _(copy=copy):
                copy.start()

    send_patches((-1, 0, 1))
    head_tokens(2)
    head_part(5, 8)
    send_patches((2, 3, 4))

    for d, (first, size, slot) in PIECES.items():

        @pl.when(4 * part + d == me_g)
        def _(first=first, size=size, slot=slot):
            got[TF + frame, pl.ds(slot, size)] = own[pl.ds(first, size)]

    in_copy.wait()
    w_corner[...] = jnp.zeros(w_corner.shape, jnp.bfloat16)
    for a in range(3):
        for parity, middle in ((0, 2), (1, 1)):
            for cell in range(2):
                for s in range(3):
                    for u in range(3):
                        row = s + cell
                        col = u + middle - 1
                        at_k = (row // 2) * 128 + (col // 2) * 64 + (row % 2) * 32 + (col % 2) * 16
                        at_n = (2 * parity + cell) * chan
                        w_corner[a, pl.ds(at_k, 16), pl.ds(at_n, chan)] = w_in[
                            pl.ds(((a * 3 + u) * 3 + s) * 16, 16), :
                        ]

    for slot in range(2 * TF):
        for side in range(2):
            m, g, remote = source(slot, side)
            for d, (first, size, first_slot) in PIECES.items():
                if (d in (-1, 4)) != bool(side):
                    continue
                which = place == d % 4

                @pl.when(remote & which)
                def _(slot=slot, m=m, g=g, first=first, size=size, first_slot=first_slot, side=side):
                    pltpu.make_async_remote_copy(
                        src_ref=own.at[pl.ds(first, size)],
                        dst_ref=got.at[slot, pl.ds(first_slot, size)],
                        send_sem=own_send.at[0],
                        recv_sem=(side_recv if side else main_recv).at[slot],
                        device_id=at(m, g),
                        device_id_type=MESH,
                    ).wait_recv()

    width = got.shape[-1]
    packed = got[...].astype(jnp.float32).reshape(2 * TF * 4, KC // 2, width)
    turned = pltpu.roll(packed.reshape(-1, width), width // 2, 1).reshape(packed.shape)
    low = lax.broadcasted_iota(i32, packed.shape, 2) < width // 2
    flat = jnp.concatenate(
        [jnp.where(low, packed, turned), jnp.where(low, turned, packed)], axis=1
    ).reshape(2 * TF * 4 * KC, width)
    lane = lax.broadcasted_iota(i32, flat.shape, 1)
    pair_col = lax.rem(lax.broadcasted_iota(i32, flat.shape, 0), KC)
    back = jnp.where(pair_col == 0, 0.0, pltpu.roll(flat, 1, 0))
    on = jnp.where(pair_col == KC - 1, 0.0, pltpu.roll(flat, flat.shape[0] - 1, 0))
    left = lane < width // 2
    corner[0] = jnp.where(left, back, flat).astype(jnp.bfloat16).reshape(corner.shape[1:])
    corner[1] = jnp.where(left, flat, on).astype(jnp.bfloat16).reshape(corner.shape[1:])


    def normed_silu(values, gain, keep=None):
        factor = lax.rsqrt(jnp.sum(values * values, axis=-1, keepdims=True) * (1.0 / chan) + 1e-06)
        if keep is not None:
            factor = factor * keep
        half = values * factor * gain
        return half + half * jnp.tanh(half)

    first_eight = lax.broadcasted_iota(i32, (8, chan), 0)

    def moved_on(act):
        moved = pltpu.roll(act, KC - 1, 0)
        last = jnp.where(first_eight == 7, 0.0, moved[KC - 8 :])
        return jnp.concatenate([moved[: KC - 8], last], axis=0)

    def moved_back(act):
        moved = pltpu.roll(act, 1, 0)
        return jnp.concatenate([jnp.where(first_eight == 0, 0.0, moved[:8]), moved[8:]], axis=0)

    def store_act(ref, f, row, parity, act):
        if parity == 0:
            ref[EVEN, f, row] = act.astype(jnp.bfloat16)
            ref[EVEN_ON, f, row] = moved_on(act).astype(jnp.bfloat16)
        else:
            ref[ODD, f, row] = act.astype(jnp.bfloat16)
            ref[ODD_BACK, f, row] = moved_back(act).astype(jnp.bfloat16)

    gain_one = row_of(gain_one_ref) * 0.5
    in_bias = jnp.concatenate([row_of(in_b_ref)] * 2, axis=1)
    top_keep = has_up.astype(jnp.float32)
    bottom_keep = has_down.astype(jnp.float32)
    prev_keep = has_prev.astype(jnp.float32)

    def input_product(ci, parity):
        taps = [
            corner[parity, a : a + EXT_F, ci + di].reshape(EXT_F * KC, width)
            for a in range(3)
            for di in range(2)
        ]
        raw = jnp.dot(
            jnp.concatenate(taps, axis=1),
            w_corner[:, :, 2 * chan * parity : 2 * chan * (parity + 1)].reshape(
                6 * width, 2 * chan
            ),
            preferred_element_type=jnp.float32,
        )
        return (raw + in_bias).reshape(EXT_F, KC, 2 * chan)

    def input_act(row, parity, values):
        for f in range(EXT_F):
            if f >= 2 and 1 <= row <= TH:
                stream[parity, f - 2, row - 1] = values[f].astype(jnp.bfloat16)
            keep = prev_keep if f < 2 else None
            for edge, edge_keep in ((0, top_keep), (EXT_R - 1, bottom_keep)):
                if row == edge:
                    keep = edge_keep if keep is None else keep * edge_keep
            store_act(act_one, f, row, parity, normed_silu(values[f], gain_one, keep))

    raws = [input_product(0, parity) for parity in range(2)]
    for parity in range(2):
        for cell in range(2):
            input_act(cell, parity, raws[parity][:, :, cell * chan : (cell + 1) * chan])
        raw = input_product(1, parity)
        third[parity] = raw[:, :, chan:]
        raws.append(raw)
    for parity in range(2):
        input_act(2, parity, raws[2 + parity][:, :, :chan])

    def last_rows(parity):
        raw = input_product(2, parity)
        for cell in range(2):
            input_act(4 + cell, parity, raw[:, :, cell * chan : (cell + 1) * chan])

    rest_of_input = (
        lambda: input_act(3, 0, third[0]),
        lambda: input_act(3, 1, third[1]),
        lambda: last_rows(0),
        lambda: last_rows(1),
    )

    def tap(weight, a, u, s):
        return weight[a * 9 + u * 3 + s]

    def cells(field, version, frames, rows, s):
        if rows is ALL_ROWS:
            view = [field[version, f, s : s + TH] for f in frames]
        else:
            view = [field[version, f, v + s][None] for f in frames for v in rows]
        return jnp.concatenate(view, axis=0).reshape(len(frames) * len(rows) * KC, chan)

    def product(field, weight, groups, rows, taps, part=slice(None)):
        return jnp.dot(
            jnp.concatenate(
                [cells(field, version, frames, rows, s) for version, frames, _ in groups for s in taps],
                axis=1,
            ),
            jnp.concatenate(
                [
                    jnp.concatenate([tap(weight, a, u, s) for a, u in outs], axis=1)[:, part]
                    for _, _, outs in groups
                    for s in taps
                ],
                axis=0,
            ),
            preferred_element_type=jnp.float32,
        )

    def conv(field, weight, frames, rows, taps, paired, sides_first, beside=()):
        shape = (len(frames), len(rows), KC, chan)
        calls = iter(beside)

        def between():
            call = next(calls, None)
            if call is not None:
                call()

        def side(version, u):
            if paired:
                firsts = frames[0::2]
                half = (len(firsts), len(rows), KC, chan)
                two = product(
                    field,
                    weight,
                    [(version, [f + n for f in firsts], ((n, u), (n - 1, u))) for n in (1, 2)],
                    rows,
                    taps,
                )
                one = product(field, weight, [(version, firsts, ((0, u),))], rows, taps)
                other = product(
                    field, weight, [(version, [f + 3 for f in firsts], ((2, u),))], rows, taps
                )
                one = (one + two[:, :chan]).reshape(half)
                other = (other + two[:, chan:]).reshape(half)
                total = jnp.stack([one, other], axis=1)
            else:
                total = product(
                    field,
                    weight,
                    [(version, [f + a for f in frames], ((a, u),)) for a in range(3)],
                    rows,
                    taps,
                )
            between()
            return total.reshape(shape)

        def both(lanes):
            total = product(
                field,
                weight,
                [
                    (version, [f + a for f in frames], ((a, u + 1), (a, u)))
                    for a in range(3)
                    for version, u in ((EVEN, 0), (ODD, 1))
                ],
                rows,
                taps,
                lanes,
            )
            between()
            return total

        cut = 4 * chan // 3
        if sides_first:
            even = side(ODD_BACK, 0)
            odd = side(EVEN_ON, 2)
        low = both(slice(0, cut))
        if sides_first:
            yield low[:, :chan].reshape(shape) + even
        high = both(slice(cut, 2 * chan))
        if not sides_first:
            even = side(ODD_BACK, 0)
            yield low[:, :chan].reshape(shape) + even
            odd = side(EVEN_ON, 2)
        yield jnp.concatenate([low[:, chan:], high], axis=1).reshape(shape) + odd

    gain_two = row_of(gain_two_ref) * 0.5
    bias_one = row_of(bias_one_ref)
    bias_two = row_of(bias_two_ref)
    own_frames = list(range(TF))

    def act_two_rows(totals, rows):
        for parity, total in enumerate(totals):
            for f in range(TF):
                for i, v in enumerate(rows):
                    act = normed_silu(total[f, i] + bias_one, gain_two)
                    store_act(act_two, f + 2, v + 1, parity, act)

    def row_copy(way):
        frames = pl.ds(2, TF)
        return pltpu.make_async_remote_copy(
            src_ref=act_two.at[pl.ds(EVEN, 2), frames, 1 if way else TH],
            dst_ref=act_two.at[pl.ds(EVEN, 2), frames, EXT_R - 1 if way else 0],
            send_sem=row_send.at[way],
            recv_sem=row_recv.at[way],
            device_id=at(me_m, me_g - 1 if way else me_g + 1),
            device_id_type=MESH,
        )

    def edge_copy(way):
        return pltpu.make_async_remote_copy(
            src_ref=act_two.at[pl.ds(EVEN, 2), pl.ds(TF, 2), 1 if way else TH],
            dst_ref=act_two.at[pl.ds(EVEN, 2), pl.ds(0, 2), EXT_R - 1 if way else 0],
            send_sem=edge_send.at[way],
            recv_sem=edge_recv.at[way],
            device_id=at(me_m + 1, me_g - 1 if way else me_g + 1),
            device_id_type=MESH,
        )

    def pass_copy(way):
        row = EXT_R - 1 if way else 0
        return pltpu.make_async_remote_copy(
            src_ref=act_two.at[pl.ds(EVEN, 2), pl.ds(TF, 2), row],
            dst_ref=act_two.at[pl.ds(EVEN, 2), pl.ds(0, 2), row],
            send_sem=edge_send.at[way],
            recv_sem=edge_recv.at[way],
            device_id=at(me_m + 1, me_g),
            device_id_type=MESH,
        )

    tm_copy = pltpu.make_async_remote_copy(
        src_ref=act_two.at[pl.ds(EVEN, 2), pl.ds(TF, 2), pl.ds(1, TH)],
        dst_ref=act_two.at[pl.ds(EVEN, 2), pl.ds(0, 2), pl.ds(1, TH)],
        send_sem=tm_send.at[0],
        recv_sem=tm_recv.at[0],
        device_id=at(me_m + 1, me_g),
        device_id_type=MESH,
    )
    way_out = (has_down, has_up)
    way_in = (has_up, has_down)

    def widen(f, row):
        even = act_two[EVEN, f, row].astype(jnp.float32)
        act_two[EVEN_ON, f, row] = moved_on(even).astype(jnp.bfloat16)
        odd = act_two[ODD, f, row].astype(jnp.float32)
        act_two[ODD_BACK, f, row] = moved_back(odd).astype(jnp.bfloat16)

    for copy in w_copies[0]:
        copy.wait()
    for copy in w_copies[1]:
        copy.start()

    for row, way in ((0, 1), (TH - 1, 0)):
        beside = rest_of_input if row == 0 else ()
        act_two_rows(
            conv(act_one, w1, own_frames, (row,), ALL_TAPS, False, True, beside), (row,)
        )

        @pl.when(way_out[way])
        def _(way=way):
            row_copy(way).start()

        @pl.when(way_out[way] & sends_edges)
        def _(way=way):
            edge_copy(way).start()

    act_two_rows(conv(act_one, w1, own_frames, (1, 2), ALL_TAPS, True, True), (1, 2))

    @pl.when(has_next)
    def _():
        tm_copy.start()

    for copy in w_copies[1]:
        copy.wait()

    for parity, total in enumerate(conv(act_two, w2, [2, 3], ALL_ROWS, (1,), True, True)):
        acc[parity] = total + bias_two

    for way in range(2):

        @pl.when(way_in[way])
        def _(way=way):
            row_copy(way).wait_recv()

        @pl.when(way_in[way] & passes_edges)
        def _(way=way):
            pass_copy(way).start()

    for row in (0, EXT_R - 1):
        for f in range(2, EXT_F):
            widen(f, row)

    for parity, total in enumerate(conv(act_two, w2, [2, 3], ALL_ROWS, (0, 2), True, False)):
        acc[parity] += total

    @pl.when(has_prev)
    def _():
        tm_copy.wait_recv()

    for way in range(2):

        @pl.when(way_in[way] & has_prev)
        def _(way=way):
            edge_copy(way).wait_recv()

    for f in range(2):
        for row in range(EXT_R):
            widen(f, row)

    area = 2 * TH * KC
    to = lax.broadcasted_iota(i32, (area, area), 0)
    of = lax.broadcasted_iota(i32, (area, area), 1)
    order = jnp.where(
        (lax.div(to, 8) == lax.rem(of, KC)) & (lax.rem(to, 8) == lax.div(of, KC)), 1.0, 0.0
    ).astype(jnp.bfloat16)

    def finish(f, totals):
        halves = [
            (totals[p] + stream[p, f].astype(jnp.float32))
            .astype(jnp.bfloat16)
            .reshape(TH * KC, chan)
            for p in range(2)
        ]
        placed = jnp.dot(
            order, jnp.concatenate(halves, axis=0), preferred_element_type=jnp.float32
        )
        out_ref[f, 0] = placed.reshape(2 * KC, TH, chan).astype(jnp.bfloat16)

    done = [lambda f=f: finish(2 + f, [acc[p, f] for p in range(2)]) for f in range(2)]
    totals = list(conv(act_two, w2, [0, 1], ALL_ROWS, ALL_TAPS, True, False, done))
    for f in range(2):
        finish(f, [totals[p][f] + bias_two for p in range(2)])

    for n, (dm, d) in enumerate(sends):
        remote, copy = patch_copy(n, dm, d)

        @pl.when(remote)
        def _(copy=copy):
            copy.wait_send()

    @pl.when(has_next)
    def _():
        tm_copy.wait_send()

    for way in range(2):

        @pl.when(way_out[way])
        def _(way=way):
            row_copy(way).wait_send()

        @pl.when(way_out[way] & sends_edges)
        def _(way=way):
            edge_copy(way).wait_send()

        @pl.when(way_in[way] & passes_edges)
        def _(way=way):
            pass_copy(way).wait_send()


def solution(mesh):
    tiles = mesh.shape["tile"]
    blocks = mesh.shape["tm"]

    def body(
        tokens,
        head_shift,
        head_scale,
        head_weight,
        head_bias,
        in_weight,
        in_bias,
        gain_one,
        weight_one,
        bias_one,
        gain_two,
        weight_two,
        bias_two,
    ):
        count, depth = tokens.shape
        chan = weight_one.shape[-1]
        wide = 2 * head_weight.shape[1]
        in_rows = in_weight.shape[0] * in_weight.shape[1] * in_weight.shape[2] * in_weight.shape[3]
        bf16 = jnp.bfloat16
        hbm = pl.BlockSpec(memory_space=pl.ANY)
        vmem = pl.BlockSpec(memory_space=pltpu.VMEM)
        dma = pltpu.SemaphoreType.DMA
        result = pl.pallas_call(
            functools.partial(body_kernel, tiles, blocks),
            out_shape=pltpu.VMEM((TF, 1, 2 * KC, TH, chan), bf16),
            in_specs=[
                hbm, vmem, vmem, vmem, vmem, hbm, vmem, vmem, hbm, vmem, vmem, hbm, vmem,
            ],
            out_specs=vmem,
            scratch_shapes=[
                pltpu.VMEM((count, depth), bf16),
                pltpu.VMEM((count, depth), bf16),
                pltpu.VMEM((depth, wide), bf16),
                pltpu.VMEM((2, 16, depth), jnp.float32),
                pltpu.VMEM((count // KC, KC // 2, wide), bf16),
                pltpu.VMEM((2 * TF, 4, KC // 2, wide), bf16),
                pltpu.VMEM((2, 2 * TF, 4, KC, wide), bf16),
                pltpu.VMEM((in_rows, chan), bf16),
                pltpu.VMEM((3, 2 * wide, 4 * chan), bf16),
                pltpu.VMEM((27, chan, chan), bf16),
                pltpu.VMEM((27, chan, chan), bf16),
                pltpu.VMEM((4, EXT_F, EXT_R, KC, chan), bf16),
                pltpu.VMEM((4, EXT_F, EXT_R, KC, chan), bf16),
                pltpu.VMEM((2, TF, TH, KC, chan), bf16),
                pltpu.VMEM((2, EXT_F, KC, chan), jnp.float32),
                pltpu.VMEM((2, 2, TH, KC, chan), jnp.float32),
                dma((3,)),
                dma((2, 3)),
                dma,
                dma((12,)),
                dma((2 * TF,)),
                dma((2 * TF,)),
                dma((2,)),
                dma((2,)),
                dma((1,)),
                dma((1,)),
                dma((2,)),
                dma((2,)),
            ],
            compiler_params=pltpu.CompilerParams(
                collective_id=0, has_side_effects=True, vmem_limit_bytes=56 * 1024 * 1024
            ),
            name="decode",
        )(
            tokens,
            head_shift[None],
            head_scale[None],
            head_weight.T,
            head_bias,
            in_weight.reshape(in_rows, chan),
            in_bias,
            gain_one,
            weight_one.reshape(27, chan, chan),
            bias_one,
            gain_two,
            weight_two.reshape(27, chan, chan),
            bias_two,
        )
        return result

    in_specs = (P(("tm", "tile"), None), P(), P(), P(), P(), P(), P(), P(), P(), P(), P(), P(), P())
    out_specs = P("tm", "tile", None, None, None)
    return jax.shard_map(body, mesh=mesh, in_specs=in_specs, out_specs=out_specs, check_vma=False)
```

```python
import functools

import jax
import jax.numpy as jnp
from jax import lax
from jax.experimental import pallas as pl
from jax.experimental.pallas import tpu as pltpu
from jax.sharding import PartitionSpec as P

MESH = pl.DeviceIdType.MESH
TF = 4
TH = 4
KC = 32
EXT_F = TF + 2
EXT_R = TH + 2
ODD_BACK, EVEN, ODD, EVEN_ON = range(4)
ALL_ROWS = (0, 1, 2, 3)
ALL_TAPS = (0, 1, 2)

PIECES = {-1: (0, 1, 3), 0: (0, 3, 1), 1: (1, 4, 0), 2: (3, 4, 0), 3: (5, 3, 0), 4: (7, 1, 0)}


def body_kernel(
    tiles,
    blocks,
    tokens,
    shift_ref,
    scale_ref,
    head_w_ref,
    head_b_ref,
    in_w,
    in_b_ref,
    gain_one_ref,
    w_one,
    bias_one_ref,
    gain_two_ref,
    w_two,
    bias_two_ref,
    out_ref,
    tok,
    modulated,
    turned_w,
    affine,
    own,
    got,
    corner,
    w_in,
    w_corner,
    w1,
    w2,
    act_one,
    act_two,
    stream,
    third,
    acc,
    tok_sem,
    w_sem,
    in_sem,
    own_send,
    main_recv,
    side_recv,
    row_send,
    row_recv,
    tm_send,
    tm_recv,
    edge_send,
    edge_recv,
):
    me_m = lax.axis_index("tm")
    me_g = lax.axis_index("tile")
    chan = w1.shape[-1]
    depth = tok.shape[1]
    i32 = jnp.int32

    def at(m, g):
        return {"tm": m, "tile": g}

    def row_of(ref):
        return ref[...].reshape(1, ref.shape[0])

    tok_rows = tok.shape[0] // 4
    tok_copies = [
        pltpu.make_async_copy(
            tokens.at[pl.ds(i * tok_rows, tok_rows)],
            tok.at[pl.ds(i * tok_rows, tok_rows)],
            tok_sem.at[i],
        )
        for i in range(4)
    ]
    in_copy = pltpu.make_async_copy(in_w, w_in, in_sem)
    w_copies = [
        [
            pltpu.make_async_copy(src.at[pl.ds(9 * a, 9)], dst.at[pl.ds(9 * a, 9)], w_sem.at[n, a])
            for a in range(3)
        ]
        for n, (src, dst) in enumerate(((w_one, w1), (w_two, w2)))
    ]
    for copy in tok_copies:
        copy.start()
    in_copy.start()

    frame = lax.div(me_g, tiles // TF)
    part = lax.rem(me_g, tiles // TF)
    home = lax.div(me_g, 4)
    place = lax.rem(me_g, 4)

    def target(dm, d):
        g = 4 * part + d
        m = me_m + dm
        inside = (g >= 0) & (g < tiles) & (m < blocks)
        remote = inside if dm else inside & (g != me_g)
        return m, g, remote

    def source(slot, side):
        m = me_m if slot >= TF else me_m - 1
        other = home + jnp.where(place == 0, -1, 1) if side else home
        g = (slot % TF) * (tiles // TF) + other
        inside = m >= 0
        if side:
            inside = (
                inside
                & ((place == 0) | (place == 3))
                & (other >= 0)
                & (other < tiles // TF)
            )
        remote = inside & (g != me_g) if slot >= TF else inside
        return m, g, remote

    has_up = me_g > 0
    has_down = me_g < tiles - 1
    has_prev = me_m > 0
    has_next = me_m < blocks - 1
    sends_edges = has_next & (lax.rem(me_m, 2) == 1)
    passes_edges = has_next & (lax.rem(me_m, 2) == 0)
    gets_edges = has_prev & (lax.rem(me_m, 2) == 0)

    barrier = pltpu.get_barrier_semaphore()

    def greet(m, g, here):
        @pl.when(here)
        def _():
            pl.semaphore_signal(barrier, inc=1, device_id=at(m, g), device_id_type=MESH)

    for slot in range(2 * TF):
        for side in range(2):
            greet(*source(slot, side))
    greet(me_m, me_g - 1, has_up)
    greet(me_m, me_g + 1, has_down)
    greet(me_m - 1, me_g, has_prev)
    greet(me_m - 1, me_g - 1, gets_edges & has_up)
    greet(me_m - 1, me_g + 1, gets_edges & has_down)

    zero_patch = jnp.zeros(got.shape[2:], jnp.bfloat16)

    @pl.when(jnp.logical_not(has_prev))
    def _():
        for slot in range(TF):
            for pair in range(4):
                got[slot, pair] = zero_patch
        for version in range(4):
            for row in range(EXT_R):
                for f in range(2):
                    act_two[version, f, row] = jnp.zeros((KC, chan), jnp.bfloat16)

    @pl.when(jnp.logical_not(has_up))
    def _():
        for slot in range(2 * TF):
            got[slot, 0] = zero_patch
        for version in range(4):
            for f in range(EXT_F):
                act_two[version, f, 0] = jnp.zeros((KC, chan), jnp.bfloat16)

    @pl.when(jnp.logical_not(has_down))
    def _():
        for slot in range(2 * TF):
            got[slot, 3] = zero_patch
        for version in range(4):
            for f in range(EXT_F):
                act_two[version, f, EXT_R - 1] = jnp.zeros((KC, chan), jnp.bfloat16)

    lanes = 128

    head_w = head_w_ref[...]
    turned_w[...] = jnp.concatenate([head_w, head_w], axis=0).T
    affine[0] = jnp.broadcast_to(1.0 + scale_ref[...], affine.shape[1:])
    affine[1] = jnp.broadcast_to(shift_ref[...], affine.shape[1:])

    def head_rows(i, carry):
        rows = pl.ds(pl.multiple_of(i * 16, 16), 16)

        def piece(j):
            return tok[rows, j * lanes : (j + 1) * lanes].astype(jnp.float32)

        base = piece(0)[:, :1]
        sums = [jnp.zeros((16, lanes), jnp.float32)] * 2
        squares = [jnp.zeros((16, lanes), jnp.float32)] * 2
        for j in range(depth // lanes):
            away = piece(j) - base
            sums[j % 2] = sums[j % 2] + away
            squares[j % 2] = squares[j % 2] + away * away
        offset = jnp.sum(sums[0] + sums[1], axis=-1, keepdims=True) * (1.0 / depth)
        second = jnp.sum(squares[0] + squares[1], axis=-1, keepdims=True) * (1.0 / depth)
        average = base + offset
        factor = lax.rsqrt(jnp.maximum(second - offset * offset, 0.0) + 1e-06)
        for j in range(depth // lanes):
            part = pl.ds(j * lanes, lanes)
            normed = (piece(j) - average) * factor * affine[0, :, part] + affine[1, :, part]
            modulated[rows, part] = normed.astype(jnp.bfloat16)
        return carry

    for i in range(4):
        tok_copies[i].wait()
        if i == 3:
            for copy in w_copies[0]:
                copy.start()
        blocks_of = tok_rows // 16
        lax.fori_loop(i * blocks_of, (i + 1) * blocks_of, head_rows, 0, unroll=min(4, blocks_of))
    patches = jnp.dot(modulated[...], turned_w[...], preferred_element_type=jnp.float32)
    head_b = jnp.concatenate([row_of(head_b_ref)] * 2, axis=1)
    spread = (patches + head_b).reshape(own.shape[0], KC, own.shape[2])
    wide_left = lax.broadcasted_iota(i32, own.shape, 2) < own.shape[2] // 2
    own[...] = jnp.where(wide_left, spread[:, : KC // 2], spread[:, KC // 2 :]).astype(jnp.bfloat16)

    def patch_copy(n, dm, d):
        m, g, remote = target(dm, d)
        first, count, slot = PIECES[d]
        return remote, pltpu.make_async_remote_copy(
            src_ref=own.at[pl.ds(first, count)],
            dst_ref=got.at[(0 if dm else TF) + frame, pl.ds(slot, count)],
            send_sem=own_send.at[n],
            recv_sem=(side_recv if d in (-1, 4) else main_recv).at[(0 if dm else TF) + frame],
            device_id=at(m, g),
            device_id_type=MESH,
        )

    sends = [(dm, d) for dm in (1, 0) for d in PIECES]
    count = i32(0)
    for dm, d in sends:
        count = count + target(dm, d)[2].astype(i32)
    for here in (has_up, has_down, has_next, sends_edges & has_up, sends_edges & has_down):
        count = count + here.astype(i32)
    pl.semaphore_wait(barrier, count)

    for n, (dm, d) in enumerate(sends):
        remote, copy = patch_copy(n, dm, d)

        @pl.when(remote)
        def _(copy=copy):
            copy.start()

    for d, (first, size, slot) in PIECES.items():

        @pl.when(4 * part + d == me_g)
        def _(first=first, size=size, slot=slot):
            got[TF + frame, pl.ds(slot, size)] = own[pl.ds(first, size)]

    in_copy.wait()
    w_corner[...] = jnp.zeros(w_corner.shape, jnp.bfloat16)
    for a in range(3):
        for parity, middle in ((0, 2), (1, 1)):
            for cell in range(2):
                for s in range(3):
                    for u in range(3):
                        row = s + cell
                        col = u + middle - 1
                        at_k = (row // 2) * 128 + (col // 2) * 64 + (row % 2) * 32 + (col % 2) * 16
                        at_n = (2 * parity + cell) * chan
                        w_corner[a, pl.ds(at_k, 16), pl.ds(at_n, chan)] = w_in[
                            pl.ds(((a * 3 + u) * 3 + s) * 16, 16), :
                        ]

    for slot in range(2 * TF):
        for side in range(2):
            m, g, remote = source(slot, side)
            for d, (first, size, first_slot) in PIECES.items():
                if (d in (-1, 4)) != bool(side):
                    continue
                which = place == d % 4

                @pl.when(remote & which)
                def _(slot=slot, m=m, g=g, first=first, size=size, first_slot=first_slot, side=side):
                    pltpu.make_async_remote_copy(
                        src_ref=own.at[pl.ds(first, size)],
                        dst_ref=got.at[slot, pl.ds(first_slot, size)],
                        send_sem=own_send.at[0],
                        recv_sem=(side_recv if side else main_recv).at[slot],
                        device_id=at(m, g),
                        device_id_type=MESH,
                    ).wait_recv()

    width = got.shape[-1]
    packed = got[...].astype(jnp.float32).reshape(2 * TF * 4, KC // 2, width)
    turned = pltpu.roll(packed.reshape(-1, width), width // 2, 1).reshape(packed.shape)
    low = lax.broadcasted_iota(i32, packed.shape, 2) < width // 2
    flat = jnp.concatenate(
        [jnp.where(low, packed, turned), jnp.where(low, turned, packed)], axis=1
    ).reshape(2 * TF * 4 * KC, width)
    lane = lax.broadcasted_iota(i32, flat.shape, 1)
    pair_col = lax.rem(lax.broadcasted_iota(i32, flat.shape, 0), KC)
    back = jnp.where(pair_col == 0, 0.0, pltpu.roll(flat, 1, 0))
    on = jnp.where(pair_col == KC - 1, 0.0, pltpu.roll(flat, flat.shape[0] - 1, 0))
    left = lane < width // 2
    corner[0] = jnp.where(left, back, flat).astype(jnp.bfloat16).reshape(corner.shape[1:])
    corner[1] = jnp.where(left, flat, on).astype(jnp.bfloat16).reshape(corner.shape[1:])


    def normed_silu(values, gain, keep=None):
        factor = lax.rsqrt(jnp.sum(values * values, axis=-1, keepdims=True) * (1.0 / chan) + 1e-06)
        if keep is not None:
            factor = factor * keep
        half = values * factor * gain
        return half + half * jnp.tanh(half)

    first_eight = lax.broadcasted_iota(i32, (8, chan), 0)

    def moved_on(act):
        moved = pltpu.roll(act, KC - 1, 0)
        last = jnp.where(first_eight == 7, 0.0, moved[KC - 8 :])
        return jnp.concatenate([moved[: KC - 8], last], axis=0)

    def moved_back(act):
        moved = pltpu.roll(act, 1, 0)
        return jnp.concatenate([jnp.where(first_eight == 0, 0.0, moved[:8]), moved[8:]], axis=0)

    def store_act(ref, f, row, parity, act):
        if parity == 0:
            ref[EVEN, f, row] = act.astype(jnp.bfloat16)
            ref[EVEN_ON, f, row] = moved_on(act).astype(jnp.bfloat16)
        else:
            ref[ODD, f, row] = act.astype(jnp.bfloat16)
            ref[ODD_BACK, f, row] = moved_back(act).astype(jnp.bfloat16)

    gain_one = row_of(gain_one_ref) * 0.5
    in_bias = jnp.concatenate([row_of(in_b_ref)] * 2, axis=1)
    top_keep = has_up.astype(jnp.float32)
    bottom_keep = has_down.astype(jnp.float32)
    prev_keep = has_prev.astype(jnp.float32)

    def input_product(ci, parity):
        taps = [
            corner[parity, a : a + EXT_F, ci + di].reshape(EXT_F * KC, width)
            for a in range(3)
            for di in range(2)
        ]
        raw = jnp.dot(
            jnp.concatenate(taps, axis=1),
            w_corner[:, :, 2 * chan * parity : 2 * chan * (parity + 1)].reshape(
                6 * width, 2 * chan
            ),
            preferred_element_type=jnp.float32,
        )
        return (raw + in_bias).reshape(EXT_F, KC, 2 * chan)

    def input_act(row, parity, values):
        for f in range(EXT_F):
            if f >= 2 and 1 <= row <= TH:
                stream[parity, f - 2, row - 1] = values[f].astype(jnp.bfloat16)
            keep = prev_keep if f < 2 else None
            for edge, edge_keep in ((0, top_keep), (EXT_R - 1, bottom_keep)):
                if row == edge:
                    keep = edge_keep if keep is None else keep * edge_keep
            store_act(act_one, f, row, parity, normed_silu(values[f], gain_one, keep))

    raws = [input_product(0, parity) for parity in range(2)]
    for parity in range(2):
        for cell in range(2):
            input_act(cell, parity, raws[parity][:, :, cell * chan : (cell + 1) * chan])
        raw = input_product(1, parity)
        third[parity] = raw[:, :, chan:]
        raws.append(raw)
    for parity in range(2):
        input_act(2, parity, raws[2 + parity][:, :, :chan])

    def last_rows(parity):
        raw = input_product(2, parity)
        for cell in range(2):
            input_act(4 + cell, parity, raw[:, :, cell * chan : (cell + 1) * chan])

    def fourth_row():
        for parity in range(2):
            input_act(3, parity, third[parity])

    rest_of_input = (lambda: last_rows(0), lambda: last_rows(1), fourth_row)

    def tap(weight, a, u, s):
        return weight[a * 9 + u * 3 + s]

    def cells(field, version, frames, rows, s):
        if rows is ALL_ROWS:
            view = [field[version, f, s : s + TH] for f in frames]
        else:
            view = [field[version, f, v + s][None] for f in frames for v in rows]
        return jnp.concatenate(view, axis=0).reshape(len(frames) * len(rows) * KC, chan)

    def product(field, weight, groups, rows, taps, part=slice(None)):
        return jnp.dot(
            jnp.concatenate(
                [cells(field, version, frames, rows, s) for version, frames, _ in groups for s in taps],
                axis=1,
            ),
            jnp.concatenate(
                [
                    jnp.concatenate([tap(weight, a, u, s) for a, u in outs], axis=1)[:, part]
                    for _, _, outs in groups
                    for s in taps
                ],
                axis=0,
            ),
            preferred_element_type=jnp.float32,
        )

    def conv(field, weight, frames, rows, taps, paired, sides_first, beside=()):
        shape = (len(frames), len(rows), KC, chan)
        calls = iter(beside)

        def between():
            call = next(calls, None)
            if call is not None:
                call()

        def side(version, u):
            if paired:
                firsts = frames[0::2]
                half = (len(firsts), len(rows), KC, chan)
                two = product(
                    field,
                    weight,
                    [(version, [f + n for f in firsts], ((n, u), (n - 1, u))) for n in (1, 2)],
                    rows,
                    taps,
                )
                one = product(field, weight, [(version, firsts, ((0, u),))], rows, taps)
                other = product(
                    field, weight, [(version, [f + 3 for f in firsts], ((2, u),))], rows, taps
                )
                one = (one + two[:, :chan]).reshape(half)
                other = (other + two[:, chan:]).reshape(half)
                total = jnp.stack([one, other], axis=1)
            else:
                total = product(
                    field,
                    weight,
                    [(version, [f + a for f in frames], ((a, u),)) for a in range(3)],
                    rows,
                    taps,
                )
            between()
            return total.reshape(shape)

        def both(lanes):
            total = product(
                field,
                weight,
                [
                    (version, [f + a for f in frames], ((a, u + 1), (a, u)))
                    for a in range(3)
                    for version, u in ((EVEN, 0), (ODD, 1))
                ],
                rows,
                taps,
                lanes,
            )
            between()
            return total

        cut = 4 * chan // 3
        if sides_first:
            even = side(ODD_BACK, 0)
            odd = side(EVEN_ON, 2)
        low = both(slice(0, cut))
        if sides_first:
            yield low[:, :chan].reshape(shape) + even
        high = both(slice(cut, 2 * chan))
        if not sides_first:
            even = side(ODD_BACK, 0)
            yield low[:, :chan].reshape(shape) + even
            odd = side(EVEN_ON, 2)
        yield jnp.concatenate([low[:, chan:], high], axis=1).reshape(shape) + odd

    gain_two = row_of(gain_two_ref) * 0.5
    bias_one = row_of(bias_one_ref)
    bias_two = row_of(bias_two_ref)
    own_frames = list(range(TF))

    def act_two_part(total, rows, parity):
        for f in range(TF):
            for i, v in enumerate(rows):
                act = normed_silu(total[f, i] + bias_one, gain_two)
                store_act(act_two, f + 2, v + 1, parity, act)

    def act_two_rows(totals, rows):
        for parity, total in enumerate(totals):
            act_two_part(total, rows, parity)

    def row_copy(way):
        frames = pl.ds(2, TF)
        return pltpu.make_async_remote_copy(
            src_ref=act_two.at[pl.ds(EVEN, 2), frames, 1 if way else TH],
            dst_ref=act_two.at[pl.ds(EVEN, 2), frames, EXT_R - 1 if way else 0],
            send_sem=row_send.at[way],
            recv_sem=row_recv.at[way],
            device_id=at(me_m, me_g - 1 if way else me_g + 1),
            device_id_type=MESH,
        )

    def edge_copy(way):
        return pltpu.make_async_remote_copy(
            src_ref=act_two.at[pl.ds(EVEN, 2), pl.ds(TF, 2), 1 if way else TH],
            dst_ref=act_two.at[pl.ds(EVEN, 2), pl.ds(0, 2), EXT_R - 1 if way else 0],
            send_sem=edge_send.at[way],
            recv_sem=edge_recv.at[way],
            device_id=at(me_m + 1, me_g - 1 if way else me_g + 1),
            device_id_type=MESH,
        )

    def pass_copy(way):
        row = EXT_R - 1 if way else 0
        return pltpu.make_async_remote_copy(
            src_ref=act_two.at[pl.ds(EVEN, 2), pl.ds(TF, 2), row],
            dst_ref=act_two.at[pl.ds(EVEN, 2), pl.ds(0, 2), row],
            send_sem=edge_send.at[way],
            recv_sem=edge_recv.at[way],
            device_id=at(me_m + 1, me_g),
            device_id_type=MESH,
        )

    tm_copy = pltpu.make_async_remote_copy(
        src_ref=act_two.at[pl.ds(EVEN, 2), pl.ds(TF, 2), pl.ds(1, TH)],
        dst_ref=act_two.at[pl.ds(EVEN, 2), pl.ds(0, 2), pl.ds(1, TH)],
        send_sem=tm_send.at[0],
        recv_sem=tm_recv.at[0],
        device_id=at(me_m + 1, me_g),
        device_id_type=MESH,
    )
    way_out = (has_down, has_up)
    way_in = (has_up, has_down)

    def widen(f, row):
        even = act_two[EVEN, f, row].astype(jnp.float32)
        act_two[EVEN_ON, f, row] = moved_on(even).astype(jnp.bfloat16)
        odd = act_two[ODD, f, row].astype(jnp.float32)
        act_two[ODD_BACK, f, row] = moved_back(odd).astype(jnp.bfloat16)

    for copy in w_copies[0]:
        copy.wait()
    for copy in w_copies[1]:
        copy.start()

    for row, way in ((0, 1), (TH - 1, 0)):
        beside = rest_of_input if row == 0 else ()
        act_two_rows(
            conv(act_one, w1, own_frames, (row,), ALL_TAPS, False, True, beside), (row,)
        )

        @pl.when(way_out[way])
        def _(way=way):
            row_copy(way).start()

        @pl.when(way_out[way] & sends_edges)
        def _(way=way):
            edge_copy(way).start()

    for copy in w_copies[1]:
        copy.wait()

    def along_rows(rows, beside=()):
        totals = conv(act_two, w2, [2, 3], rows, (1,), False, True, beside)
        for parity, total in enumerate(totals):
            for i, v in enumerate(rows):
                acc[parity, :, v] = total[:, i] + bias_two

    middle = (1, 2)
    totals = conv(act_one, w1, own_frames, middle, ALL_TAPS, True, True)
    act_two_part(next(totals), middle, 0)
    odd_total = next(totals)
    along_rows((0, TH - 1), [lambda: act_two_part(odd_total, middle, 1)])

    @pl.when(has_next)
    def _():
        tm_copy.start()

    along_rows(middle)

    for way in range(2):

        @pl.when(way_in[way])
        def _(way=way):
            row_copy(way).wait_recv()

        @pl.when(way_in[way] & passes_edges)
        def _(way=way):
            pass_copy(way).start()

    for row in (0, EXT_R - 1):
        for f in range(2, EXT_F):
            widen(f, row)

    for parity, total in enumerate(conv(act_two, w2, [2, 3], ALL_ROWS, (0, 2), True, False)):
        acc[parity] += total

    @pl.when(has_prev)
    def _():
        tm_copy.wait_recv()

    for way in range(2):

        @pl.when(way_in[way] & has_prev)
        def _(way=way):
            edge_copy(way).wait_recv()

    for f in range(2):
        for row in range(EXT_R):
            widen(f, row)

    area = 2 * TH * KC
    to = lax.broadcasted_iota(i32, (area, area), 0)
    of = lax.broadcasted_iota(i32, (area, area), 1)
    order = jnp.where(
        (lax.div(to, 8) == lax.rem(of, KC)) & (lax.rem(to, 8) == lax.div(of, KC)), 1.0, 0.0
    ).astype(jnp.bfloat16)

    def finish(f, totals):
        halves = [
            (totals[p] + stream[p, f].astype(jnp.float32))
            .astype(jnp.bfloat16)
            .reshape(TH * KC, chan)
            for p in range(2)
        ]
        placed = jnp.dot(
            order, jnp.concatenate(halves, axis=0), preferred_element_type=jnp.float32
        )
        out_ref[f, 0] = placed.reshape(2 * KC, TH, chan).astype(jnp.bfloat16)

    done = [lambda f=f: finish(2 + f, [acc[p, f] for p in range(2)]) for f in range(2)]
    totals = list(conv(act_two, w2, [0, 1], ALL_ROWS, ALL_TAPS, True, False, done))
    for f in range(2):
        finish(f, [totals[p][f] + bias_two for p in range(2)])

    for n, (dm, d) in enumerate(sends):
        remote, copy = patch_copy(n, dm, d)

        @pl.when(remote)
        def _(copy=copy):
            copy.wait_send()

    @pl.when(has_next)
    def _():
        tm_copy.wait_send()

    for way in range(2):

        @pl.when(way_out[way])
        def _(way=way):
            row_copy(way).wait_send()

        @pl.when(way_out[way] & sends_edges)
        def _(way=way):
            edge_copy(way).wait_send()

        @pl.when(way_in[way] & passes_edges)
        def _(way=way):
            pass_copy(way).wait_send()


def solution(mesh):
    tiles = mesh.shape["tile"]
    blocks = mesh.shape["tm"]

    def body(
        tokens,
        head_shift,
        head_scale,
        head_weight,
        head_bias,
        in_weight,
        in_bias,
        gain_one,
        weight_one,
        bias_one,
        gain_two,
        weight_two,
        bias_two,
    ):
        count, depth = tokens.shape
        chan = weight_one.shape[-1]
        wide = 2 * head_weight.shape[1]
        in_rows = in_weight.shape[0] * in_weight.shape[1] * in_weight.shape[2] * in_weight.shape[3]
        bf16 = jnp.bfloat16
        hbm = pl.BlockSpec(memory_space=pl.ANY)
        vmem = pl.BlockSpec(memory_space=pltpu.VMEM)
        dma = pltpu.SemaphoreType.DMA
        result = pl.pallas_call(
            functools.partial(body_kernel, tiles, blocks),
            out_shape=pltpu.VMEM((TF, 1, 2 * KC, TH, chan), bf16),
            in_specs=[
                hbm, vmem, vmem, vmem, vmem, hbm, vmem, vmem, hbm, vmem, vmem, hbm, vmem,
            ],
            out_specs=vmem,
            scratch_shapes=[
                pltpu.VMEM((count, depth), bf16),
                pltpu.VMEM((count, depth), bf16),
                pltpu.VMEM((depth, wide), bf16),
                pltpu.VMEM((2, 16, depth), jnp.float32),
                pltpu.VMEM((count // KC, KC // 2, wide), bf16),
                pltpu.VMEM((2 * TF, 4, KC // 2, wide), bf16),
                pltpu.VMEM((2, 2 * TF, 4, KC, wide), bf16),
                pltpu.VMEM((in_rows, chan), bf16),
                pltpu.VMEM((3, 2 * wide, 4 * chan), bf16),
                pltpu.VMEM((27, chan, chan), bf16),
                pltpu.VMEM((27, chan, chan), bf16),
                pltpu.VMEM((4, EXT_F, EXT_R, KC, chan), bf16),
                pltpu.VMEM((4, EXT_F, EXT_R, KC, chan), bf16),
                pltpu.VMEM((2, TF, TH, KC, chan), bf16),
                pltpu.VMEM((2, EXT_F, KC, chan), jnp.float32),
                pltpu.VMEM((2, 2, TH, KC, chan), jnp.float32),
                dma((4,)),
                dma((2, 3)),
                dma,
                dma((12,)),
                dma((2 * TF,)),
                dma((2 * TF,)),
                dma((2,)),
                dma((2,)),
                dma((1,)),
                dma((1,)),
                dma((2,)),
                dma((2,)),
            ],
            compiler_params=pltpu.CompilerParams(
                collective_id=0, has_side_effects=True, vmem_limit_bytes=56 * 1024 * 1024
            ),
            name="decode",
        )(
            tokens,
            head_shift[None],
            head_scale[None],
            head_weight.T,
            head_bias,
            in_weight.reshape(in_rows, chan),
            in_bias,
            gain_one,
            weight_one.reshape(27, chan, chan),
            bias_one,
            gain_two,
            weight_two.reshape(27, chan, chan),
            bias_two,
        )
        return result

    in_specs = (P(("tm", "tile"), None), P(), P(), P(), P(), P(), P(), P(), P(), P(), P(), P(), P())
    out_specs = P("tm", "tile", None, None, None)
    return jax.shard_map(body, mesh=mesh, in_specs=in_specs, out_specs=out_specs, check_vma=False)
```
